256 devices in a mesh: wide: 32 (over y, z_lo, core), narrow: 8 (over x, z_hi).
Axes of the slice: x: 4, y: 4, z: 8 (z_hi: 2, z_lo: 4; z = z_hi * 4 + z_lo), core: 2. Of those that a mesh axis runs over, the one named last changes fastest.
Arguments:
- amplitudes: bfloat16 [524288, 1024], P(('wide', 'narrow')), may hold values from -0.03125 to 0.03125
- integral_slab: bfloat16 [524288, 1024], P(('wide', 'narrow')), may hold values from -0.046875 to 0.046875
- coupling: float32 [256, 1024, 1024], P(('wide', 'narrow')), may hold values from -0.046875 to 0.046875
- pair_of_block: int32 [256], replicated, may hold values from 0 to 255, each once
- pair_shift: float32 [256], replicated, may hold values from -4 to 4
- virt_energy: float32 [1024], replicated, may hold values from 0 to 26
- core_energy: float32 [64], replicated, may hold values from -6 to -4
- core_index: int32 [2], replicated, may hold values from 0 to 63, as said below
- frequency: float32 [16], replicated, may hold values from 6 to 30
- dipole: float32 [64, 1024], P(None, 'narrow'), may hold values from -6 to 6
Outputs:
- response: float32 [2, 32, 1024], P(None, None, 'narrow')
- residual_rms: float32 [2, 32], replicated
The draws below stay inside these ranges and needn't reach their ends.
Inputs may be any that keep to these rules, and one draw needn't show every extreme that they name: `core_index`: the 2 core orbitals are different occupied orbitals, and the last of them is orbital 64 - 1.
All inputs are finite; a program needn't handle non-finite values.
Results may differ from the reference program's by a relative error of at most 0.0003.
Values sent between devices are 32-bit elements; how exact they have to be, the bound alone decides.
A program may use at most 64 MiB of HBM per device.

```python
import jax
import jax.numpy as jnp
from jax import lax

NV = 1024
NOCC = 64
NF = 16
NCORE = 2
ITERS = 2
ROWS_DEV = 2048
ROWS = 524288
PAIRS = 256
CF = 32
DEVICES = 256


def draw_core_index(key, part):
    order = jax.random.permutation(jax.random.fold_in(key, 7), NOCC - 1)
    others = order[:NCORE - 1].astype(jnp.int32)
    return jnp.concatenate([others, jnp.full((1,), NOCC - 1, jnp.int32)], 0)


def draw_frequency(key, part):
    subkey = jax.random.fold_in(key, 11)
    places = jnp.arange(NF, dtype=jnp.float32)
    jitter = jnp.clip(0.5 + 0.12 * jax.random.normal(subkey, (NF,), jnp.float32), 0.2, 0.8)
    return (6.0 + 24.0 * (places + jitter) / NF).astype(jnp.float32)


def strengthened(drawn, own_key, source, target, parts, factor):
    def block_of(position):
        return (jnp.arange(drawn.shape[position]) // (drawn.shape[position] // parts)).reshape((-1,) + (1,) * (drawn.ndim - 1 - position))

    first = jax.random.permutation(own_key, parts)[block_of(target)]
    other_side = (block_of(target) + parts // 2) % parts
    return jnp.where((block_of(source) == first) | (block_of(source) == other_side), factor * drawn, drawn)


def level_of(key, dims, pieces, least, high):
    factor_of, own = 1.0, jax.random.fold_in(key, 6)
    for axis_at, parts in pieces:
        heights = jnp.exp(jax.random.uniform(jax.random.fold_in(own, axis_at), (parts,), jnp.float32, least / len(pieces), high / len(pieces)))
        factor_of = factor_of * jnp.repeat(heights, dims[axis_at] // parts).reshape([-1 if axis == axis_at else 1 for axis in range(len(dims))])
    return factor_of


def noise(rng, shape, width, most, shards=(), kind=jnp.bfloat16):
    drawn = width * jax.random.normal(rng, shape, jnp.float32)
    if shards:
        drawn = drawn * level_of(rng, shape, shards, -0.22, 0.18)
    return jnp.clip(drawn, -most, most).astype(kind)


def bell_draw_with(rng, extent, spread, reach, pieces, heavy, kind=jnp.bfloat16):
    entries = spread * jax.random.normal(rng, extent, jnp.float32)
    if pieces:
        entries = entries * level_of(rng, extent, pieces, -0.22, 0.18)
    return jnp.clip(strengthened(entries, jax.random.fold_in(rng, 3), *heavy), -reach, reach).astype(kind)


def setup_inputs(seed: int = 0) -> dict:
    key_of = jax.random.split(jax.random.key(seed), 11)
    amplitudes = bell_draw_with(key_of[0], (ROWS, NV), ROWS ** -0.5, 0.03125, ((0, 256),), (0, 1, 256, 6.0))
    integral_slab = noise(key_of[1], (ROWS, NV), (16 * NV) ** -0.5, 0.046875, ((0, 256),))
    coupling = noise(key_of[2], (PAIRS, NV, NV), (16 * NV) ** -0.5, 0.046875, ((0, 256),), jnp.float32)
    pair_of_block = jax.random.permutation(key_of[3], PAIRS).astype(jnp.int32)
    pair_shift = jnp.clip(jax.random.uniform(key_of[4], (PAIRS,), jnp.float32, -4.0, 4.0), -4.0, 4.0)
    virt_energy = jnp.clip(jax.random.uniform(key_of[5], (NV,), jnp.float32, 0.0, 26.0), 0.0, 26.0)
    core_energy = jnp.clip(jax.random.uniform(key_of[6], (NOCC,), jnp.float32, -6.0, -4.0), -6.0, -4.0)
    core_index = draw_core_index(jax.random.fold_in(key_of[10], 71), 0)
    frequency = draw_frequency(jax.random.fold_in(key_of[10], 71), 0)
    dipole = noise(key_of[9], (NOCC, NV), 1.0, 6.0, ((1, 8),), jnp.float32)
    return {"amplitudes": amplitudes, "integral_slab": integral_slab, "coupling": coupling, "pair_of_block": pair_of_block, "pair_shift": pair_shift, "virt_energy": virt_energy, "core_energy": core_energy, "core_index": core_index, "frequency": frequency, "dipole": dipole}


damping = 0.5
highest = lax.Precision.HIGHEST

def divide_precond(real_part, imag_part, level, level_mag):
    return ((real_part * level - imag_part * damping) / level_mag, (imag_part * level + real_part * damping) / level_mag)

def divide_denom(real_part, imag_part, denom_real, denom_mag):
    return ((real_part * denom_real + imag_part * damping) / denom_mag, (imag_part * denom_real - real_part * damping) / denom_mag)

def apply_precond(real_part, imag_part, level):
    return (level * real_part + damping * imag_part, level * imag_part - damping * real_part)

def reference(amplitudes, integral_slab, coupling, pair_of_block, pair_shift, virt_energy, core_energy, core_index, frequency, dipole):
    row_blocks = amplitudes.reshape(DEVICES, ROWS_DEV, NV)
    slab_blocks = integral_slab.reshape(DEVICES, ROWS_DEV, NV)

    def accumulate(total, blocks):
        left_block, right_block = blocks
        product = lax.dot_general(left_block, right_block, (((0,), (0,)), ((), ())), preferred_element_type=jnp.float32)
        return (total + product, None)
    singles, _ = lax.scan(accumulate, jnp.zeros((NV, NV), jnp.float32), (row_blocks, slab_blocks))
    picked_energy = core_energy[core_index]
    shift = (frequency[None, :] + picked_energy[:, None]).reshape(-1)
    level = virt_energy[None, :] - shift[:, None]
    level_mag = level * level + damping * damping
    rhs = jnp.repeat(dipole[core_index], NF, axis=0)
    resp_re, resp_im = divide_precond(rhs, jnp.zeros_like(rhs), level, level_mag)
    slot_shift = pair_shift[pair_of_block]

    def fold_pairs(flattened):

        def one_slot(total, slot_data):
            matrix, offset = slot_data
            doubles_in = jnp.dot(flattened, matrix.T, precision=highest)
            denom_real = shift[:, None] - offset - virt_energy[None, :]
            denom_mag = denom_real * denom_real + damping * damping
            out_re, out_im = divide_denom(doubles_in[:CF], doubles_in[CF:], denom_real, denom_mag)
            outgoing = jnp.concatenate([out_re, out_im], 0)
            return (total + jnp.dot(outgoing, matrix, precision=highest), None)
        folded, _ = lax.scan(one_slot, jnp.zeros_like(flattened), (coupling, slot_shift))
        return folded
    rms_rows = []
    for sweep in range(ITERS):
        flattened = jnp.concatenate([resp_re, resp_im], 0)
        folded = fold_pairs(flattened)
        singles_term = jnp.dot(flattened, singles.T, precision=highest)
        applied = singles_term + folded
        app_re, app_im = apply_precond(resp_re, resp_im, level)
        res_re = rhs - (app_re + applied[:CF])
        res_im = -(app_im + applied[CF:])
        squares = lax.optimization_barrier(jnp.sum(res_re * res_re + res_im * res_im, axis=1))
        rms_rows.append(jnp.sqrt(squares / (2 * NV) + 1e-06))
        step_re, step_im = divide_precond(res_re, res_im, level, level_mag)
        resp_re = resp_re + step_re
        resp_im = resp_im + step_im
    return (jnp.stack([resp_re, resp_im], 0), jnp.stack(rms_rows, 0))
```

```python
from functools import partial

import jax
import jax.numpy as jnp
from jax import lax
from jax.experimental import pallas as pl
from jax.experimental.pallas import tpu as pltpu
from jax.sharding import PartitionSpec as P

ITERS = 2
DAMP = 0.5
MESH = pl.DeviceIdType.MESH
F32 = jnp.float32
BF16 = jnp.bfloat16

NX, NY, NZ, NZLO = 4, 4, 8, 4
PLANE = tuple((dx, dy) for dx in range(NX) for dy in range(NY))[1:]
GROUPS, SUB, LANES, BLOCKS = 4, 8, 128, 8
PIECE = 2 * SUB
COLS = GROUPS * PIECE
HALF = BLOCKS // 2


def place(x, y, z, core):
    return {
        "wide": (y * NZLO + lax.rem(z, NZLO)) * 2 + core,
        "narrow": x * 2 + z // NZLO,
    }


def nt(left, right):
    return lax.dot_general(left, right, (((1,), (1,)), ((), ())), preferred_element_type=F32)


def nn(left, right):
    return lax.dot_general(left, right, (((1,), (0,)), ((), ())), preferred_element_type=F32)


def halves(value):
    high = value.astype(BF16)
    low = (value - high.astype(F32)).astype(BF16)
    return high, low


def kernel(
    pair_of_block, pair_shift, core_energy, core_index, frequency,
    virt, dipole, amp_hbm, slab_hbm, coup_hbm,
    out_ref, rms_ref,
    amp, slab, coup, coup_hi, coup_lo,
    picked, dip, rhs, pre_re, pre_im, level, den_re, den_im, resp, pieces, t_pieces, w_pieces,
    part, from_core, own, from_plane, columns, applied, spare,
    hbm_sem, dip_sems, core_sems, plane_sems, column_sems, gather_sems, share_sems,
):
    wide, narrow = lax.axis_index("wide"), lax.axis_index("narrow")
    x, y, core = narrow // 2, wide // (2 * NZLO), lax.rem(wide, 2)
    z_hi, z_lo = lax.rem(narrow, 2), lax.rem(wide // 2, NZLO)
    z = z_hi * NZLO + z_lo
    mirror = (1 - z_hi) * NZLO + lax.rem(z_lo + 2, NZLO)

    loads = [
        pltpu.make_async_copy(slab_hbm, slab, hbm_sem.at[0]),
        pltpu.make_async_copy(coup_hbm.at[0], coup, hbm_sem.at[1]),
        pltpu.make_async_copy(amp_hbm, amp, hbm_sem.at[2]),
    ]
    for load in loads:
        load.start()

    sibling = place(x, y, z, 1 - core)
    plane = [place(lax.rem(x + dx, NX), lax.rem(y + dy, NY), z, core) for dx, dy in PLANE]
    plane_xy = [(lax.rem(x + dx, NX), lax.rem(y + dy, NY)) for dx, dy in PLANE]
    column = [place(x, y, lax.rem(z + d, NZ), core) for d in range(1, NZ)]
    mirrors = [place(lax.rem(x + d, NX), y, mirror, core) for d in range(NX)]
    holders = [place(lax.rem(x + d, NX), y, z, core) for d in range(1, NX)] + mirrors

    barrier = pltpu.get_barrier_semaphore()
    greeted = [sibling] + plane + column + mirrors[1:]
    for device in greeted:
        pl.semaphore_signal(barrier, inc=1, device_id=device, device_id_type=MESH)

    def remote(src, dst, sems, device):
        return pltpu.make_async_remote_copy(
            src_ref=src, dst_ref=dst, send_sem=sems.at[0], recv_sem=sems.at[1],
            device_id=device, device_id_type=MESH,
        )

    sublane = lax.broadcasted_iota(jnp.int32, (SUB, LANES), 0)
    lane = lax.broadcasted_iota(jnp.int32, (SUB, LANES), 1)
    offset = pair_shift[pair_of_block[wide * 8 + narrow]]
    for g in range(GROUPS):
        energy = core_energy[core_index[g // 2]]
        shift = jnp.zeros((SUB, LANES), F32)
        for j in range(SUB):
            value = frequency[(g % 2) * SUB + j] + energy
            shift = jnp.where(sublane == j, value, shift)
        rows = pl.ds(g * SUB, SUB)
        for b in range(BLOCKS):
            energies = jnp.broadcast_to(virt[b : b + 1, :], (SUB, LANES))
            lev = energies - shift
            inverse = 1.0 / (lev * lev + DAMP * DAMP)
            level[b, rows, :] = lev
            pre_re[b, rows, :] = lev * inverse
            pre_im[b, rows, :] = DAMP * inverse
            den = (shift - offset) - energies
            inverse = 1.0 / (den * den + DAMP * DAMP)
            den_re[b, rows, :] = den * inverse
            den_im[b, rows, :] = DAMP * inverse
    for c in range(2):
        picked[c : c + 1, :] = dipole[pl.ds(core_index[c], 1), :]

    pl.semaphore_wait(barrier, len(greeted))
    for device in holders:
        remote(picked, dip.at[narrow], dip_sems, device).start()
    dip[narrow] = picked[...]

    loads[1].wait()
    high, low = halves(coup[...])
    coup_hi[...] = high
    coup_lo[...] = low
    loads[0].wait()

    others = remote(dip.at[pl.ds(0, BLOCKS - 1)], dip.at[pl.ds(0, BLOCKS - 1)], dip_sems, sibling)
    others.wait_recv()
    for g in range(GROUPS):
        for b in range(BLOCKS):
            source = jnp.broadcast_to(dip[b, g // 2 : g // 2 + 1, :], (SUB, LANES))
            rows = pl.ds(g * SUB, SUB)
            rhs[b, rows, :] = source
            resp[0, b, pl.ds(g * PIECE, SUB), :] = source * pre_re[b, rows, :]
            resp[0, b, pl.ds(g * PIECE + SUB, SUB), :] = source * pre_im[b, rows, :]

    for sweep in range(ITERS):
        for b in range(BLOCKS):
            high, low = halves(resp[sweep, b])
            pieces[:COLS, b * LANES : (b + 1) * LANES] = high
            pieces[COLS:, b * LANES : (b + 1) * LANES] = low
        both = nt(pieces[...], coup_hi[...])
        doubles = both[:COLS] + both[COLS:] + nt(pieces[:COLS, :], coup_lo[...])
        for g in range(GROUPS):
            rows = pl.ds(g * SUB, SUB)
            for b in range(BLOCKS):
                cols = slice(b * LANES, (b + 1) * LANES)
                real = doubles[g * PIECE : g * PIECE + SUB, cols]
                imag = doubles[g * PIECE + SUB : (g + 1) * PIECE, cols]
                q_re, q_im = den_re[b, rows, :], den_im[b, rows, :]
                quotient = jnp.concatenate([real * q_re + imag * q_im, imag * q_re - real * q_im], 0)
                high, low = halves(quotient)
                w_pieces[g * PIECE : (g + 1) * PIECE, cols] = high
                w_pieces[COLS + g * PIECE : COLS + (g + 1) * PIECE, cols] = low
        both = nt(pieces[...], slab[...])
        high, low = halves(both[:COLS] + both[COLS:])
        t_pieces[:COLS, :] = high
        t_pieces[COLS:, :] = low
        if sweep == 0:
            loads[2].wait()

        swap = None
        for turn in range(2):
            side = (1 - core) if turn == 0 else core
            cols = pl.ds(pl.multiple_of(side * (HALF * LANES), HALF * LANES), HALF * LANES)
            both = nn(t_pieces[...], amp[:, cols]) + nn(w_pieces[...], coup_hi[:, cols])
            share = both[:COLS] + both[COLS:] + nn(w_pieces[:COLS, :], coup_lo[:, cols])
            for b in range(HALF):
                part[sweep, side * HALF + b] = share[:, b * LANES : (b + 1) * LANES]
            if turn == 0:
                swap = remote(
                    part.at[sweep, pl.ds(side * HALF, HALF)], from_core.at[sweep],
                    core_sems.at[sweep], sibling,
                )
                swap.start()
        swap.wait_recv()
        for b in range(HALF):
            own[sweep, b] = part[sweep, core * HALF + b] + from_core[sweep, b]

        for i, device in enumerate(plane):
            to_x, to_y = plane_xy[i]
            remote(
                own.at[sweep, to_x, pl.ds(to_y * PIECE, PIECE)], from_plane.at[sweep, i],
                plane_sems.at[sweep], device,
            ).start()
        in_plane = remote(from_plane.at[sweep], from_plane.at[sweep], plane_sems.at[sweep], sibling)
        in_plane.wait_recv()
        total = own[sweep, x, pl.ds(y * PIECE, PIECE), :]
        for i in range(len(plane)):
            total = total + from_plane[sweep, i]
        columns[sweep, z] = total

        for device in column:
            remote(columns.at[sweep, z], columns.at[sweep, z], column_sems.at[sweep], device).start()
        seven = columns.at[sweep, pl.ds(0, NZ - 1)]
        in_column = remote(seven, seven, column_sems.at[sweep], sibling)
        in_column.wait_recv()
        total = columns[sweep, 0]
        for i in range(1, NZ):
            total = total + columns[sweep, i]
        applied[sweep, core * HALF + x, pl.ds(y * PIECE, PIECE), :] = total

        block = applied.at[sweep, core * HALF + x, pl.ds(y * PIECE, PIECE)]
        for device in plane:
            remote(block, block, gather_sems.at[sweep], device).start()
        gathered = remote(from_plane.at[sweep], from_plane.at[sweep], gather_sems.at[sweep], sibling)
        gathered.wait_recv()
        mine = applied.at[sweep, pl.ds(core * HALF, HALF)]
        swap_back = remote(mine, mine, share_sems.at[sweep], sibling)
        swap_back.start()
        swap_back.wait_recv()

        line = jnp.zeros((1, LANES), F32)
        for g in range(GROUPS):
            rows = pl.ds(g * SUB, SUB)
            squares = jnp.zeros((SUB, LANES), F32)
            for b in range(BLOCKS):
                re_rows, im_rows = pl.ds(g * PIECE, SUB), pl.ds(g * PIECE + SUB, SUB)
                re, im = resp[sweep, b, re_rows, :], resp[sweep, b, im_rows, :]
                lev = level[b, rows, :]
                res_re = rhs[b, rows, :] - ((lev * re + DAMP * im) + applied[sweep, b, re_rows, :])
                res_im = -((lev * im - DAMP * re) + applied[sweep, b, im_rows, :])
                squares = squares + (res_re * res_re + res_im * res_im)
                p_re, p_im = pre_re[b, rows, :], pre_im[b, rows, :]
                resp[sweep + 1, b, re_rows, :] = re + (res_re * p_re - res_im * p_im)
                resp[sweep + 1, b, im_rows, :] = im + (res_im * p_re + res_re * p_im)
            summed = jnp.sum(squares, axis=1, keepdims=True)
            spread = jnp.where(lane == sublane + g * SUB, jnp.broadcast_to(summed, (SUB, LANES)), 0.0)
            line = line + jnp.sum(spread, axis=0, keepdims=True)
        rms = jnp.sqrt(line / (2 * BLOCKS * LANES) + 1e-06)
        rms_ref[sweep : sweep + 1, :] = rms[:, : GROUPS * SUB]

    for g in range(GROUPS):
        rows = pl.ds(g * SUB, SUB)
        out_ref[0, rows, :] = resp[ITERS, narrow, pl.ds(g * PIECE, SUB), :]
        out_ref[1, rows, :] = resp[ITERS, narrow, pl.ds(g * PIECE + SUB, SUB), :]

    others.wait_send()
    for sweep in range(ITERS):
        remote(from_core.at[sweep], from_core.at[sweep], core_sems.at[sweep], sibling).wait_send()
        remote(from_core.at[sweep], from_core.at[sweep], share_sems.at[sweep], sibling).wait_send()
        plane_bytes = from_plane.at[sweep]
        remote(plane_bytes, plane_bytes, plane_sems.at[sweep], sibling).wait_send()
        remote(plane_bytes, plane_bytes, gather_sems.at[sweep], sibling).wait_send()
        seven = columns.at[sweep, pl.ds(0, NZ - 1)]
        remote(seven, seven, column_sems.at[sweep], sibling).wait_send()


def per_device(
    amplitudes, integral_slab, coupling, pair_of_block, pair_shift, virt_energy,
    core_energy, core_index, frequency, dipole,
):
    rows, virt_total = amplitudes.shape
    k_total = GROUPS * SUB
    whole = (BLOCKS, k_total, LANES)
    vmem = pl.BlockSpec(memory_space=pltpu.VMEM)
    smem = pl.BlockSpec(memory_space=pltpu.SMEM)
    anywhere = pl.BlockSpec(memory_space=pl.ANY)
    dma = pltpu.SemaphoreType.DMA
    return pl.pallas_call(
        kernel,
        name="response",
        out_shape=(
            jax.ShapeDtypeStruct((2, k_total, LANES), F32),
            jax.ShapeDtypeStruct((ITERS, k_total), F32),
        ),
        in_specs=[smem] * 5 + [vmem] * 2 + [anywhere] * 3,
        out_specs=(vmem, vmem),
        scratch_shapes=[
            pltpu.VMEM((rows, virt_total), BF16),
            pltpu.VMEM((rows, virt_total), BF16),
            pltpu.VMEM((virt_total, virt_total), F32),
            pltpu.VMEM((virt_total, virt_total), BF16),
            pltpu.VMEM((virt_total, virt_total), BF16),
            pltpu.VMEM((2, LANES), F32),
            pltpu.VMEM((BLOCKS, 2, LANES), F32),
            pltpu.VMEM(whole, F32),
            pltpu.VMEM(whole, F32),
            pltpu.VMEM(whole, F32),
            pltpu.VMEM(whole, F32),
            pltpu.VMEM(whole, F32),
            pltpu.VMEM(whole, F32),
            pltpu.VMEM((ITERS + 1, BLOCKS, COLS, LANES), F32),
            pltpu.VMEM((2 * COLS, virt_total), BF16),
            pltpu.VMEM((2 * COLS, rows), BF16),
            pltpu.VMEM((2 * COLS, virt_total), BF16),
            pltpu.VMEM((ITERS, BLOCKS, COLS, LANES), F32),
            pltpu.VMEM((ITERS, HALF, COLS, LANES), F32),
            pltpu.VMEM((ITERS, HALF, COLS, LANES), F32),
            pltpu.VMEM((ITERS, len(PLANE), PIECE, LANES), F32),
            pltpu.VMEM((ITERS, NZ, PIECE, LANES), F32),
            pltpu.VMEM((ITERS, BLOCKS, COLS, LANES), F32),
            pltpu.VMEM((SUB, LANES), F32),
            dma((3,)),
            dma((2,)),
            dma((ITERS, 2)),
            dma((ITERS, 2)),
            dma((ITERS, 2)),
            dma((ITERS, 2)),
            dma((ITERS, 2)),
        ],
        compiler_params=pltpu.CompilerParams(
            collective_id=0, has_side_effects=True, vmem_limit_bytes=56 * 2**20
        ),
    )(
        pair_of_block, pair_shift, core_energy, core_index, frequency,
        virt_energy.reshape(BLOCKS, LANES), dipole, amplitudes, integral_slab, coupling,
    )


def solution(mesh):
    rows = P(("wide", "narrow"), None)
    placed = (rows, rows, P(("wide", "narrow"), None, None)) + (P(),) * 6 + (P(None, "narrow"),)
    return jax.shard_map(
        per_device,
        mesh=mesh,
        in_specs=placed,
        out_specs=(P(None, None, "narrow"), P()),
        check_vma=False,
    )
```

```python
from functools import partial

import jax
import jax.numpy as jnp
from jax import lax
from jax.experimental import pallas as pl
from jax.experimental.pallas import tpu as pltpu
from jax.sharding import PartitionSpec as P

DAMP = 0.5
MESH = pl.DeviceIdType.MESH
F32 = jnp.float32
BF16 = jnp.bfloat16

NX, NY, NZ, NZLO = 4, 4, 8, 4
PLANE = tuple((dx, dy) for dx in range(NX) for dy in range(NY))[1:]
GROUPS, SUB, LANES, BLOCKS = 4, 8, 128, 8
PIECE = 2 * SUB
COLS = GROUPS * PIECE
HALF = BLOCKS // 2
HALF_COLS = HALF * LANES
STRIP = 256


def place(x, y, z, core):
    return {
        "wide": (y * NZLO + lax.rem(z, NZLO)) * 2 + core,
        "narrow": x * 2 + z // NZLO,
    }


def nn(left, right):
    return lax.dot_general(left, right, (((1,), (0,)), ((), ())), preferred_element_type=F32)


def halves(value):
    high = value.astype(BF16)
    low = (value - high.astype(F32)).astype(BF16)
    return high, low


def remote(src, dst, sems, device):
    return pltpu.make_async_remote_copy(
        src_ref=src, dst_ref=dst, send_sem=sems.at[0], recv_sem=sems.at[1],
        device_id=device, device_id_type=MESH,
    )


def kernel(
    stop,
    pair_of_block_hbm, pair_shift_hbm, core_energy_hbm, core_index_hbm, frequency_hbm,
    virt_hbm, dipole_hbm, amp_hbm, slab_hbm, coup_hbm,
    out_ref, rms_ref,
    pair_of_block, pair_shift, core_energy, core_index, frequency, virt, dipole,
    amp, slab, coup, slab_t, coup_hi, coup_lo, coup_t_hi, coup_t_lo,
    picked, dip, rhs, pre_re, pre_im, level, den_re, den_im, resp, base, res,
    pieces, t_pieces, w_pieces,
    part, from_core, own, from_plane, columns, applied, final, lines, line_out,
    small_sem, hbm_sem, dip_sems, core_sems, plane_sems, column_sems, gather_sems, share_sem,
    final_sems, line_sems,
):
    wide, narrow = lax.axis_index("wide"), lax.axis_index("narrow")
    x, y, core = narrow // 2, wide // (2 * NZLO), lax.rem(wide, 2)
    z_hi, z_lo = lax.rem(narrow, 2), lax.rem(wide // 2, NZLO)
    z = z_hi * NZLO + z_lo
    mirror = (1 - z_hi) * NZLO + lax.rem(z_lo + 2, NZLO)

    small = [
        pltpu.make_async_copy(src, dst, small_sem.at[i])
        for i, (src, dst) in enumerate((
            (core_index_hbm, core_index), (dipole_hbm, dipole), (virt_hbm, virt),
            (core_energy_hbm, core_energy), (frequency_hbm, frequency),
            (pair_of_block_hbm, pair_of_block), (pair_shift_hbm, pair_shift),
        ))
    ]
    loads = [
        pltpu.make_async_copy(coup_hbm.at[0], coup, hbm_sem.at[0]),
        pltpu.make_async_copy(slab_hbm, slab, hbm_sem.at[1]),
        pltpu.make_async_copy(amp_hbm, amp, hbm_sem.at[2]),
    ]
    for load in small + loads:
        load.start()

    sibling = place(x, y, z, 1 - core)
    plane_xy = [(lax.rem(x + dx, NX), lax.rem(y + dy, NY)) for dx, dy in PLANE]
    plane = [place(to_x, to_y, z, core) for to_x, to_y in plane_xy]
    across = [place(to_x, to_y, z, 1 - core) for to_x, to_y in plane_xy]
    column = [place(x, y, lax.rem(z + d, NZ), core) for d in range(1, NZ)]
    mirrors = [place(lax.rem(x + d, NX), y, mirror, core) for d in range(NX)]
    holders = [place(lax.rem(x + d, NX), y, z, core) for d in range(1, NX)] + mirrors

    barrier = pltpu.get_barrier_semaphore()
    greeted = mirrors[1:] + plane + across + column + [sibling]
    for device in greeted:
        pl.semaphore_signal(barrier, inc=1, device_id=device, device_id_type=MESH)

    for load in small:
        load.wait()
    for c in range(2):
        picked[c : c + 1, :] = dipole[pl.ds(core_index[c], 1), :]
    pl.semaphore_wait(barrier, len(greeted))
    if stop == 0:
        for load in loads:
            load.wait()
        return
    for device in holders:
        remote(picked, dip.at[narrow], dip_sems, device).start()
    dip[narrow] = picked[...]

    sublane = lax.broadcasted_iota(jnp.int32, (SUB, LANES), 0)
    lane = lax.broadcasted_iota(jnp.int32, (SUB, LANES), 1)
    offset = pair_shift[pair_of_block[wide * 8 + narrow]]
    for g in range(GROUPS):
        energy = core_energy[core_index[g // 2]]
        shift = jnp.zeros((SUB, LANES), F32)
        for j in range(SUB):
            value = frequency[(g % 2) * SUB + j] + energy
            shift = jnp.where(sublane == j, value, shift)
        rows = pl.ds(g * SUB, SUB)
        for b in range(BLOCKS):
            energies = jnp.broadcast_to(virt[b : b + 1, :], (SUB, LANES))
            lev = energies - shift
            inverse = 1.0 / (lev * lev + DAMP * DAMP)
            level[b, rows, :] = lev
            pre_re[b, rows, :] = lev * inverse
            pre_im[b, rows, :] = DAMP * inverse
            den = (shift - offset) - energies
            inverse = 1.0 / (den * den + DAMP * DAMP)
            den_re[b, rows, :] = den * inverse
            den_im[b, rows, :] = DAMP * inverse
    if stop == "a":
        for load in loads:
            load.wait()
        dips = dip.at[pl.ds(0, BLOCKS - 1)]
        remote(dips, dips, dip_sems, sibling).wait()
        return

    loads[0].wait()

    def split_rows(i, _):
        rows = pl.ds(pl.multiple_of(i * STRIP, STRIP), STRIP)
        strip = coup[rows, :]
        high, low = halves(strip)
        coup_hi[rows, :] = high
        coup_lo[rows, :] = low
        coup_t_hi[:, rows] = high.T
        coup_t_lo[:, rows] = low.T
        return 0

    lax.fori_loop(0, coup.shape[0] // STRIP, split_rows, 0)
    loads[1].wait()

    def turn_rows(i, _):
        rows = pl.ds(pl.multiple_of(i * STRIP, STRIP), STRIP)
        slab_t[:, rows] = slab[rows, :].T
        return 0

    lax.fori_loop(0, slab.shape[0] // STRIP, turn_rows, 0)
    loads[2].wait()
    if stop == "b":
        dips = dip.at[pl.ds(0, BLOCKS - 1)]
        remote(dips, dips, dip_sems, sibling).wait()
        return

    dips = dip.at[pl.ds(0, BLOCKS - 1)]
    others = remote(dips, dips, dip_sems, sibling)
    others.wait_recv()
    if stop == 1:
        others.wait_send()
        return

    def start_half(half):
        for g in range(GROUPS):
            rows, re_rows, im_rows = pl.ds(g * SUB, SUB), pl.ds(g * PIECE, SUB), pl.ds(g * PIECE + SUB, SUB)
            for j in range(HALF):
                b, cols = half * HALF + j, slice(j * LANES, (j + 1) * LANES)
                source = jnp.broadcast_to(dip[b, g // 2 : g // 2 + 1, :], (SUB, LANES))
                rhs[b, rows, :] = source
                re, im = source * pre_re[b, rows, :], source * pre_im[b, rows, :]
                resp[0, b, re_rows, :] = re
                resp[0, b, im_rows, :] = im
                high, low = halves(jnp.concatenate([re, im], 0))
                pieces[half, g * PIECE : (g + 1) * PIECE, cols] = high
                pieces[half, COLS + g * PIECE : COLS + (g + 1) * PIECE, cols] = low

    def next_half(half):
        for g in range(GROUPS):
            rows, re_rows, im_rows = pl.ds(g * SUB, SUB), pl.ds(g * PIECE, SUB), pl.ds(g * PIECE + SUB, SUB)
            for j in range(HALF):
                b, cols = half * HALF + j, slice(j * LANES, (j + 1) * LANES)
                res_re = base[b, re_rows, :] - applied[b, re_rows, :]
                res_im = base[b, im_rows, :] - applied[b, im_rows, :]
                res[b, re_rows, :] = res_re
                res[b, im_rows, :] = res_im
                p_re, p_im = pre_re[b, rows, :], pre_im[b, rows, :]
                re = resp[0, b, re_rows, :] + (res_re * p_re - res_im * p_im)
                im = resp[0, b, im_rows, :] + (res_im * p_re + res_re * p_im)
                resp[1, b, re_rows, :] = re
                resp[1, b, im_rows, :] = im
                high, low = halves(jnp.concatenate([re, im], 0))
                pieces[half, g * PIECE : (g + 1) * PIECE, cols] = high
                pieces[half, COLS + g * PIECE : COLS + (g + 1) * PIECE, cols] = low

    def expand(half):
        rows = pl.ds(pl.multiple_of(half * HALF_COLS, HALF_COLS), HALF_COLS)
        both = nn(pieces[half], coup_t_hi[rows, :])
        doubles = both[:COLS] + both[COLS:] + nn(pieces[half, :COLS, :], coup_t_lo[rows, :])
        both = nn(pieces[half], slab_t[rows, :])
        return doubles, both[:COLS] + both[COLS:]

    def finish_half(doubles, singles):
        for g in range(GROUPS):
            rows = pl.ds(g * SUB, SUB)
            for b in range(BLOCKS):
                cols = slice(b * LANES, (b + 1) * LANES)
                real = doubles[g * PIECE : g * PIECE + SUB, cols]
                imag = doubles[g * PIECE + SUB : (g + 1) * PIECE, cols]
                q_re, q_im = den_re[b, rows, :], den_im[b, rows, :]
                quotient = jnp.concatenate([real * q_re + imag * q_im, imag * q_re - real * q_im], 0)
                high, low = halves(quotient)
                w_pieces[g * PIECE : (g + 1) * PIECE, cols] = high
                w_pieces[COLS + g * PIECE : COLS + (g + 1) * PIECE, cols] = low
        high, low = halves(singles)
        t_pieces[:COLS, :] = high
        t_pieces[COLS:, :] = low

    def fold(sweep):
        swap = remote(part.at[sweep, 1 - core], from_core.at[sweep], core_sems.at[sweep], sibling)
        for side in (1 - core, core):
            if sweep == 0:
                cols = pl.ds(pl.multiple_of(side * HALF_COLS, HALF_COLS), HALF_COLS)
                from_amp, from_hi, from_lo = amp[:, cols], coup_hi[:, cols], coup_lo[:, cols]
            else:
                spread = [pl.ds(pl.multiple_of((2 * j + side) * LANES, LANES), LANES) for j in range(HALF)]
                from_amp = jnp.concatenate([amp[:, cols] for cols in spread], 1)
                from_hi = jnp.concatenate([coup_hi[:, cols] for cols in spread], 1)
                from_lo = jnp.concatenate([coup_lo[:, cols] for cols in spread], 1)
            both = nn(t_pieces[...], from_amp) + nn(w_pieces[...], from_hi)
            share = both[:COLS] + both[COLS:] + nn(w_pieces[:COLS, :], from_lo)
            if side is core:
                swap.wait_recv()
            for j in range(HALF):
                block = share[:, j * LANES : (j + 1) * LANES]
                if side is core:
                    own[sweep, j] = block + from_core[sweep, j]
                else:
                    part[sweep, side, j] = block
            if side is not core:
                swap.start()
        if stop == 2:
            swap.wait_send()
            return
        for i, device in enumerate(plane):
            to_x, to_y = plane_xy[i]
            remote(
                own.at[sweep, to_x, pl.ds(to_y * PIECE, PIECE)], from_plane.at[sweep, i],
                plane_sems.at[sweep], device,
            ).start()

    def wait_send(ref, sems):
        remote(ref, ref, sems, sibling).wait_send()

    def collect(sweep):
        slots = from_plane.at[sweep]
        remote(slots, slots, plane_sems.at[sweep], sibling).wait_recv()
        total = own[sweep, x, pl.ds(y * PIECE, PIECE), :]
        for i in range(len(plane)):
            total = total + from_plane[sweep, i]
        columns[sweep, z] = total
        if stop == 3:
            wait_send(slots, plane_sems.at[sweep])
            return None
        for device in column:
            remote(columns.at[sweep, z], columns.at[sweep, z], column_sems.at[sweep], device).start()
        seven = columns.at[sweep, pl.ds(0, NZ - 1)]
        remote(seven, seven, column_sems.at[sweep], sibling).wait_recv()
        total = columns[sweep, 0]
        for i in range(1, NZ):
            total = total + columns[sweep, i]
        return total

    def line_of(squares, group):
        summed = jnp.broadcast_to(jnp.sum(squares, axis=1, keepdims=True), (SUB, LANES))
        return jnp.sum(jnp.where(lane == sublane + group * SUB, summed, 0.0), axis=0, keepdims=True)

    def rms_of(line):
        return jnp.sqrt(line / (2 * BLOCKS * LANES) + 1e-06)[:, : GROUPS * SUB]

    start_half(0)
    start_half(1)
    doubles_0, singles_0 = expand(0)
    doubles_1, singles_1 = expand(1)
    finish_half(doubles_0 + doubles_1, singles_0 + singles_1)
    fold(0)
    if stop == 2:
        others.wait_send()
        return
    for g in range(GROUPS):
        rows, re_rows, im_rows = pl.ds(g * SUB, SUB), pl.ds(g * PIECE, SUB), pl.ds(g * PIECE + SUB, SUB)
        for b in range(BLOCKS):
            re, im, lev = resp[0, b, re_rows, :], resp[0, b, im_rows, :], level[b, rows, :]
            base[b, re_rows, :] = rhs[b, rows, :] - (lev * re + DAMP * im)
            base[b, im_rows, :] = -(lev * im - DAMP * re)
    total = collect(0)
    if stop == 3:
        others.wait_send()
        wait_send(from_core.at[0], core_sems.at[0])
        return
    block = applied.at[core * HALF + x, pl.ds(y * PIECE, PIECE)]
    applied[core * HALF + x, pl.ds(y * PIECE, PIECE), :] = total
    if stop == 4:
        others.wait_send()
        wait_send(from_core.at[0], core_sems.at[0])
        wait_send(from_plane.at[0], plane_sems.at[0])
        wait_send(columns.at[0, pl.ds(0, NZ - 1)], column_sems.at[0])
        return
    for device in plane:
        remote(block, block, gather_sems, device).start()
    slots = from_plane.at[0]
    remote(slots, slots, gather_sems, sibling).wait_recv()
    mine = applied.at[pl.ds(core * HALF, HALF)]
    share = remote(mine, mine, share_sem, sibling)
    share.start()
    if stop == 5:
        share.wait()
        others.wait_send()
        wait_send(from_core.at[0], core_sems.at[0])
        wait_send(from_plane.at[0], plane_sems.at[0])
        wait_send(from_plane.at[0], gather_sems)
        wait_send(columns.at[0, pl.ds(0, NZ - 1)], column_sems.at[0])
        return

    next_half(core)
    doubles_0, singles_0 = expand(core)
    share.wait_recv()
    next_half(1 - core)
    doubles_1, singles_1 = expand(1 - core)
    finish_half(doubles_0 + doubles_1, singles_0 + singles_1)
    fold(1)
    line = jnp.zeros((1, LANES), F32)
    for g in range(GROUPS):
        squares = jnp.zeros((SUB, LANES), F32)
        for b in range(BLOCKS):
            res_re, res_im = res[b, pl.ds(g * PIECE, SUB), :], res[b, pl.ds(g * PIECE + SUB, SUB), :]
            squares = squares + (res_re * res_re + res_im * res_im)
        line = line + line_of(squares, g)
    rms_ref[0:1, :] = rms_of(line)
    mine = x * 2 + core
    rows, re_rows = pl.ds(y * SUB, SUB), pl.ds(y * PIECE, SUB)
    im_rows = pl.ds(y * PIECE + SUB, SUB)
    re, im, lev = resp[1, mine, re_rows, :], resp[1, mine, im_rows, :], level[mine, rows, :]
    base_re = rhs[mine, rows, :] - (lev * re + DAMP * im)
    base_im = -(lev * im - DAMP * re)
    total = collect(1)
    if stop != 6:
        res_re, res_im = base_re - total[:SUB], base_im - total[SUB:]
        line = line_of(res_re * res_re + res_im * res_im, y)
        lines[mine * GROUPS + y] = line
        line_out[...] = line
        for device in plane + across + [sibling]:
            remote(line_out, lines.at[mine * GROUPS + y], line_sems, device).start()
        p_re, p_im = pre_re[mine, rows, :], pre_im[mine, rows, :]
        final[core, 0, rows, :] = re + (res_re * p_re - res_im * p_im)
        final[core, 1, rows, :] = im + (res_im * p_re + res_re * p_im)
        block = final.at[core, :, rows]
        near = [place(x, lax.rem(y + d, NY), z, c) for d in range(1, NY) for c in (core, 1 - core)]
        for device in near + [sibling]:
            remote(block, block, final_sems, device).start()
        seven = columns.at[1, pl.ds(0, NZ - 1)]
        remote(seven, seven, final_sems, sibling).wait_recv()
        out_ref[...] = final[z_hi]
        most = lines.at[pl.ds(0, BLOCKS * GROUPS - 1)]
        remote(most, most, line_sems, sibling).wait_recv()
        rms_ref[1:2, :] = rms_of(jnp.sum(lines[...], axis=0))
        wait_send(most, line_sems)
        wait_send(seven, final_sems)

    others.wait_send()
    share.wait_send()
    wait_send(from_plane.at[0], gather_sems)
    for sweep in range(2):
        wait_send(from_core.at[sweep], core_sems.at[sweep])
        wait_send(from_plane.at[sweep], plane_sems.at[sweep])
        wait_send(columns.at[sweep, pl.ds(0, NZ - 1)], column_sems.at[sweep])


def tail(response_in, rms_in, response_out, rms_out):
    response_out[...] = response_in[...]
    rms_out[...] = rms_in[...]


def per_device(
    amplitudes, integral_slab, coupling, pair_of_block, pair_shift, virt_energy,
    core_energy, core_index, frequency, dipole, stop=None, cid=0, name="response",
):
    rows, virt_total = amplitudes.shape
    k_total = GROUPS * SUB
    whole, wide_whole = (BLOCKS, k_total, LANES), (BLOCKS, COLS, LANES)
    vmem = pl.BlockSpec(memory_space=pltpu.VMEM)
    anywhere = pl.BlockSpec(memory_space=pl.ANY)
    dma = pltpu.SemaphoreType.DMA
    shapes = (
        jax.ShapeDtypeStruct((2, k_total, LANES), F32),
        jax.ShapeDtypeStruct((2, k_total), F32),
    )
    response, rms = pl.pallas_call(
        partial(kernel, stop),
        name=name,
        out_shape=shapes,
        in_specs=[anywhere] * 10,
        out_specs=(vmem, vmem),
        scratch_shapes=[
            pltpu.SMEM(pair_of_block.shape, jnp.int32),
            pltpu.SMEM(pair_shift.shape, F32),
            pltpu.SMEM(core_energy.shape, F32),
            pltpu.SMEM(core_index.shape, jnp.int32),
            pltpu.SMEM(frequency.shape, F32),
            pltpu.VMEM((BLOCKS, LANES), F32),
            pltpu.VMEM(dipole.shape, F32),
            pltpu.VMEM((rows, virt_total), BF16),
            pltpu.VMEM((rows, virt_total), BF16),
            pltpu.VMEM((virt_total, virt_total), F32),
            pltpu.VMEM((virt_total, rows), BF16),
            pltpu.VMEM((virt_total, virt_total), BF16),
            pltpu.VMEM((virt_total, virt_total), BF16),
            pltpu.VMEM((virt_total, virt_total), BF16),
            pltpu.VMEM((virt_total, virt_total), BF16),
            pltpu.VMEM((2, LANES), F32),
            pltpu.VMEM((BLOCKS, 2, LANES), F32),
            pltpu.VMEM(whole, F32),
            pltpu.VMEM(whole, F32),
            pltpu.VMEM(whole, F32),
            pltpu.VMEM(whole, F32),
            pltpu.VMEM(whole, F32),
            pltpu.VMEM(whole, F32),
            pltpu.VMEM((2,) + wide_whole, F32),
            pltpu.VMEM(wide_whole, F32),
            pltpu.VMEM(wide_whole, F32),
            pltpu.VMEM((2, 2 * COLS, HALF_COLS), BF16),
            pltpu.VMEM((2 * COLS, rows), BF16),
            pltpu.VMEM((2 * COLS, virt_total), BF16),
            pltpu.VMEM((2, 2, HALF, COLS, LANES), F32),
            pltpu.VMEM((2, HALF, COLS, LANES), F32),
            pltpu.VMEM((2, HALF, COLS, LANES), F32),
            pltpu.VMEM((2, len(PLANE), PIECE, LANES), F32),
            pltpu.VMEM((2, NZ, PIECE, LANES), F32),
            pltpu.VMEM(wide_whole, F32),
            pltpu.VMEM((2, 2, k_total, LANES), F32),
            pltpu.VMEM((BLOCKS * GROUPS, 1, LANES), F32),
            pltpu.VMEM((1, LANES), F32),
            dma((7,)),
            dma((3,)),
            dma((2,)),
            dma((2, 2)),
            dma((2, 2)),
            dma((2, 2)),
            dma((2,)),
            dma((2,)),
            dma((2,)),
            dma((2,)),
        ],
        compiler_params=pltpu.CompilerParams(
            collective_id=cid, has_side_effects=True, vmem_limit_bytes=56 * 2**20
        ),
    )(
        pair_of_block, pair_shift, core_energy, core_index, frequency,
        virt_energy.reshape(BLOCKS, LANES), dipole, amplitudes, integral_slab, coupling,
    )
    return pl.pallas_call(
        tail, name="tail", out_shape=shapes, in_specs=[vmem, vmem], out_specs=(vmem, vmem)
    )(response, rms)


def solution(mesh):
    rows = P(("wide", "narrow"), None)
    placed = (rows, rows, P(("wide", "narrow"), None, None)) + (P(),) * 6 + (P(None, "narrow"),)
    return jax.shard_map(
        per_device,
        mesh=mesh,
        in_specs=placed,
        out_specs=(P(None, None, "narrow"), P()),
        check_vma=False,
    )
```

```python
from functools import partial

import jax
import jax.numpy as jnp
from jax import lax
from jax.experimental import pallas as pl
from jax.experimental.pallas import tpu as pltpu
from jax.sharding import PartitionSpec as P

DAMP = 0.5
MESH = pl.DeviceIdType.MESH
F32 = jnp.float32
BF16 = jnp.bfloat16

NX, NY, NZ, NZLO = 4, 4, 8, 4


def ring(step, size):
    return min(step, size - step)


PLANE = tuple(
    sorted(
        tuple((dx, dy) for dx in range(NX) for dy in range(NY))[1:],
        key=lambda d: -ring(d[0], NX) - ring(d[1], NY),
    )
)
COLUMN = tuple(sorted(range(1, NZ), key=lambda d: -ring(d, NZ)))
ALONG = (2, 1, 3, 0)
GROUPS, SUB, LANES, BLOCKS = 4, 8, 128, 8
PIECE = 2 * SUB
COLS = GROUPS * PIECE
HALF = BLOCKS // 2
HALF_COLS = HALF * LANES
STRIP = 256


def place(x, y, z, core):
    return {
        "wide": (y * NZLO + lax.rem(z, NZLO)) * 2 + core,
        "narrow": x * 2 + z // NZLO,
    }


def nn(left, right):
    return lax.dot_general(left, right, (((1,), (0,)), ((), ())), preferred_element_type=F32)


def halves(value):
    high = value.astype(BF16)
    low = (value - high.astype(F32)).astype(BF16)
    return high, low


def remote(src, dst, sems, device):
    return pltpu.make_async_remote_copy(
        src_ref=src, dst_ref=dst, send_sem=sems.at[0], recv_sem=sems.at[1],
        device_id=device, device_id_type=MESH,
    )


def kernel(
    stop,
    pair_of_block_hbm, pair_shift_hbm, core_energy_hbm, core_index_hbm, frequency_hbm,
    virt_hbm, dipole_hbm, amp_hbm, slab_hbm, coup_hbm,
    out_ref, rms_ref,
    pair_of_block, pair_shift, core_energy, core_index, frequency, virt, dipole,
    amp, slab, coup, slab_t, coup_hi, coup_lo, coup_t_hi, coup_t_lo,
    picked, dip, rhs, pre_re, pre_im, level, den_re, den_im, resp, base, res,
    pieces, t_pieces, w_pieces,
    part, from_core, own, from_plane, columns, applied, final, lines, line_out,
    small_sem, hbm_sem, dip_sems, core_sems, plane_sems, column_sems, gather_sems, share_sem,
    final_sems, line_sems,
):
    wide, narrow = lax.axis_index("wide"), lax.axis_index("narrow")
    x, y, core = narrow // 2, wide // (2 * NZLO), lax.rem(wide, 2)
    z_hi, z_lo = lax.rem(narrow, 2), lax.rem(wide // 2, NZLO)
    z = z_hi * NZLO + z_lo
    mirror = (1 - z_hi) * NZLO + lax.rem(z_lo + 2, NZLO)

    sibling = place(x, y, z, 1 - core)
    plane_xy = [(lax.rem(x + dx, NX), lax.rem(y + dy, NY)) for dx, dy in PLANE]
    plane = [place(to_x, to_y, z, core) for to_x, to_y in plane_xy]
    across = [place(to_x, to_y, z, 1 - core) for to_x, to_y in plane_xy]
    everyone = [device for pair in zip(across, plane) for device in pair] + [sibling]
    column = [place(x, y, lax.rem(z + d, NZ), core) for d in COLUMN]
    mirrors = [place(lax.rem(x + d, NX), y, mirror, core) for d in ALONG]
    holders = mirrors + [place(lax.rem(x + d, NX), y, z, core) for d in ALONG[:-1]]

    barrier = pltpu.get_barrier_semaphore()
    greeted = mirrors[:-1] + column + everyone
    for device in greeted:
        pl.semaphore_signal(barrier, inc=1, device_id=device, device_id_type=MESH)

    small = [
        pltpu.make_async_copy(src, dst, small_sem.at[i])
        for i, (src, dst) in enumerate((
            (core_index_hbm, core_index), (dipole_hbm, dipole), (virt_hbm, virt),
            (core_energy_hbm, core_energy), (frequency_hbm, frequency),
            (pair_of_block_hbm, pair_of_block), (pair_shift_hbm, pair_shift),
        ))
    ]
    loads = [
        pltpu.make_async_copy(coup_hbm.at[0], coup, hbm_sem.at[0]),
        pltpu.make_async_copy(slab_hbm, slab, hbm_sem.at[1]),
        pltpu.make_async_copy(amp_hbm, amp, hbm_sem.at[2]),
    ]
    for load in small + loads:
        load.start()

    for load in small:
        load.wait()
    for c in range(2):
        picked[c : c + 1, :] = dipole[pl.ds(core_index[c], 1), :]
    pl.semaphore_wait(barrier, len(greeted))
    if stop == 0:
        for load in loads:
            load.wait()
        return
    for device in holders:
        remote(picked, dip.at[narrow], dip_sems, device).start()
    dip[narrow] = picked[...]

    sublane = lax.broadcasted_iota(jnp.int32, (SUB, LANES), 0)
    lane = lax.broadcasted_iota(jnp.int32, (SUB, LANES), 1)
    offset = pair_shift[pair_of_block[wide * 8 + narrow]]
    for g in range(GROUPS):
        energy = core_energy[core_index[g // 2]]
        shift = jnp.zeros((SUB, LANES), F32)
        for j in range(SUB):
            value = frequency[(g % 2) * SUB + j] + energy
            shift = jnp.where(sublane == j, value, shift)
        rows = pl.ds(g * SUB, SUB)
        for b in range(BLOCKS):
            energies = jnp.broadcast_to(virt[b : b + 1, :], (SUB, LANES))
            lev = energies - shift
            inverse = 1.0 / (lev * lev + DAMP * DAMP)
            level[b, rows, :] = lev
            pre_re[b, rows, :] = lev * inverse
            pre_im[b, rows, :] = DAMP * inverse
            den = (shift - offset) - energies
            inverse = 1.0 / (den * den + DAMP * DAMP)
            den_re[b, rows, :] = den * inverse
            den_im[b, rows, :] = DAMP * inverse
    if stop == "a":
        for load in loads:
            load.wait()
        dips = dip.at[pl.ds(0, BLOCKS - 1)]
        remote(dips, dips, dip_sems, sibling).wait()
        return

    loads[0].wait()

    def split_rows(i, _):
        rows = pl.ds(pl.multiple_of(i * STRIP, STRIP), STRIP)
        strip = coup[rows, :]
        high, low = halves(strip)
        coup_hi[rows, :] = high
        coup_lo[rows, :] = low
        coup_t_hi[:, rows] = high.T
        coup_t_lo[:, rows] = low.T
        return 0

    lax.fori_loop(0, coup.shape[0] // STRIP, split_rows, 0)
    loads[1].wait()

    def turn_rows(i, _):
        rows = pl.ds(pl.multiple_of(i * STRIP, STRIP), STRIP)
        slab_t[:, rows] = slab[rows, :].T
        return 0

    lax.fori_loop(0, slab.shape[0] // STRIP, turn_rows, 0)
    loads[2].wait()
    if stop == "b":
        dips = dip.at[pl.ds(0, BLOCKS - 1)]
        remote(dips, dips, dip_sems, sibling).wait()
        return

    dips = dip.at[pl.ds(0, BLOCKS - 1)]
    others = remote(dips, dips, dip_sems, sibling)
    others.wait_recv()
    if stop == 1:
        others.wait_send()
        return

    def start_half(half):
        for g in range(GROUPS):
            rows, re_rows, im_rows = pl.ds(g * SUB, SUB), pl.ds(g * PIECE, SUB), pl.ds(g * PIECE + SUB, SUB)
            for j in range(HALF):
                b, cols = half * HALF + j, slice(j * LANES, (j + 1) * LANES)
                source = jnp.broadcast_to(dip[b, g // 2 : g // 2 + 1, :], (SUB, LANES))
                rhs[b, rows, :] = source
                re, im = source * pre_re[b, rows, :], source * pre_im[b, rows, :]
                resp[0, b, re_rows, :] = re
                resp[0, b, im_rows, :] = im
                high, low = halves(jnp.concatenate([re, im], 0))
                pieces[half, g * PIECE : (g + 1) * PIECE, cols] = high
                pieces[half, COLS + g * PIECE : COLS + (g + 1) * PIECE, cols] = low

    def next_half(half):
        for g in range(GROUPS):
            rows, re_rows, im_rows = pl.ds(g * SUB, SUB), pl.ds(g * PIECE, SUB), pl.ds(g * PIECE + SUB, SUB)
            for j in range(HALF):
                b, cols = half * HALF + j, slice(j * LANES, (j + 1) * LANES)
                res_re = base[b, re_rows, :] - applied[b, re_rows, :]
                res_im = base[b, im_rows, :] - applied[b, im_rows, :]
                res[b, re_rows, :] = res_re
                res[b, im_rows, :] = res_im
                p_re, p_im = pre_re[b, rows, :], pre_im[b, rows, :]
                re = resp[0, b, re_rows, :] + (res_re * p_re - res_im * p_im)
                im = resp[0, b, im_rows, :] + (res_im * p_re + res_re * p_im)
                resp[1, b, re_rows, :] = re
                resp[1, b, im_rows, :] = im
                high, low = halves(jnp.concatenate([re, im], 0))
                pieces[half, g * PIECE : (g + 1) * PIECE, cols] = high
                pieces[half, COLS + g * PIECE : COLS + (g + 1) * PIECE, cols] = low

    def expand(half):
        rows = pl.ds(pl.multiple_of(half * HALF_COLS, HALF_COLS), HALF_COLS)
        both = nn(pieces[half], coup_t_hi[rows, :])
        doubles = both[:COLS] + both[COLS:] + nn(pieces[half, :COLS, :], coup_t_lo[rows, :])
        both = nn(pieces[half], slab_t[rows, :])
        return doubles, both[:COLS] + both[COLS:]

    def finish_half(doubles, singles):
        for g in range(GROUPS):
            rows = pl.ds(g * SUB, SUB)
            for b in range(BLOCKS):
                cols = slice(b * LANES, (b + 1) * LANES)
                real = doubles[g * PIECE : g * PIECE + SUB, cols]
                imag = doubles[g * PIECE + SUB : (g + 1) * PIECE, cols]
                q_re, q_im = den_re[b, rows, :], den_im[b, rows, :]
                quotient = jnp.concatenate([real * q_re + imag * q_im, imag * q_re - real * q_im], 0)
                high, low = halves(quotient)
                w_pieces[g * PIECE : (g + 1) * PIECE, cols] = high
                w_pieces[COLS + g * PIECE : COLS + (g + 1) * PIECE, cols] = low
        high, low = halves(singles)
        t_pieces[:COLS, :] = high
        t_pieces[COLS:, :] = low

    parity, far = lax.rem(x, 2), 1 - x // 2
    strips = (far, 1 - far)
    reach = ((2 * far + parity, 2 * far + 1 - parity), (3 - 2 * far - parity, 2 - 2 * far + parity))

    def fold(sweep):
        def share_of(side, strip):
            if sweep == 0:
                first = pl.multiple_of(side * HALF_COLS + strip * STRIP, STRIP)
                spans = [pl.ds(first, STRIP)]
            else:
                spans = [
                    pl.ds(pl.multiple_of((4 * strip + 2 * i + side) * LANES, LANES), LANES) for i in range(2)
                ]

            def pick(ref):
                return jnp.concatenate([ref[:, span] for span in spans], 1) if sweep else ref[:, spans[0]]

            both = nn(t_pieces[...], pick(amp)) + nn(w_pieces[...], pick(coup_hi))
            return both[:COLS] + both[COLS:] + nn(w_pieces[:COLS, :], pick(coup_lo))

        swaps = []
        for turn, strip in enumerate(strips):
            share = share_of(1 - core, strip)
            for i in range(2):
                part[sweep, turn, i] = share[:, i * LANES : (i + 1) * LANES]
            swap = remote(part.at[sweep, turn], from_core.at[sweep, turn], core_sems.at[sweep, turn], sibling)
            swap.start()
            swaps.append(swap)
        slot = 0
        for turn, strip in enumerate(strips):
            share = share_of(core, strip)
            swaps[turn].wait_recv()
            for i in range(2):
                own[sweep, 2 * strip + i] = share[:, i * LANES : (i + 1) * LANES] + from_core[sweep, turn, i]
            if stop == 2:
                continue
            for to_x in reach[turn]:
                for dy in ALONG[: NY if slot < 3 * NY else NY - 1]:
                    to_y = lax.rem(y + dy, NY)
                    remote(
                        own.at[sweep, to_x, pl.ds(to_y * PIECE, PIECE)], from_plane.at[sweep, slot],
                        plane_sems.at[sweep], place(to_x, to_y, z, core),
                    ).start()
                    slot += 1
        if stop == 2:
            for swap in swaps:
                swap.wait_send()

    def wait_send(ref, sems):
        remote(ref, ref, sems, sibling).wait_send()

    def wait_swaps(sweep):
        for turn in range(2):
            wait_send(from_core.at[sweep, turn], core_sems.at[sweep, turn])

    def collect(sweep):
        slots = from_plane.at[sweep]
        remote(slots, slots, plane_sems.at[sweep], sibling).wait_recv()
        total = own[sweep, x, pl.ds(y * PIECE, PIECE), :]
        for i in range(len(plane)):
            total = total + from_plane[sweep, i]
        columns[sweep, z] = total
        if stop == 3:
            wait_send(slots, plane_sems.at[sweep])
            return None
        for device in column:
            remote(columns.at[sweep, z], columns.at[sweep, z], column_sems.at[sweep], device).start()
        seven = columns.at[sweep, pl.ds(0, NZ - 1)]
        remote(seven, seven, column_sems.at[sweep], sibling).wait_recv()
        total = columns[sweep, 0]
        for i in range(1, NZ):
            total = total + columns[sweep, i]
        return total

    def line_of(squares, group):
        summed = jnp.broadcast_to(jnp.sum(squares, axis=1, keepdims=True), (SUB, LANES))
        return jnp.sum(jnp.where(lane == sublane + group * SUB, summed, 0.0), axis=0, keepdims=True)

    def rms_of(line):
        return jnp.sqrt(line / (2 * BLOCKS * LANES) + 1e-06)[:, : GROUPS * SUB]

    start_half(0)
    start_half(1)
    doubles_0, singles_0 = expand(0)
    doubles_1, singles_1 = expand(1)
    finish_half(doubles_0 + doubles_1, singles_0 + singles_1)
    fold(0)
    if stop == 2:
        others.wait_send()
        return
    for g in range(GROUPS):
        rows, re_rows, im_rows = pl.ds(g * SUB, SUB), pl.ds(g * PIECE, SUB), pl.ds(g * PIECE + SUB, SUB)
        for b in range(BLOCKS):
            re, im, lev = resp[0, b, re_rows, :], resp[0, b, im_rows, :], level[b, rows, :]
            base[b, re_rows, :] = rhs[b, rows, :] - (lev * re + DAMP * im)
            base[b, im_rows, :] = -(lev * im - DAMP * re)
    total = collect(0)
    if stop == 3:
        others.wait_send()
        wait_swaps(0)
        return
    block = applied.at[core * HALF + x, pl.ds(y * PIECE, PIECE)]
    applied[core * HALF + x, pl.ds(y * PIECE, PIECE), :] = total
    if stop == 4:
        others.wait_send()
        wait_swaps(0)
        wait_send(from_plane.at[0], plane_sems.at[0])
        wait_send(columns.at[0, pl.ds(0, NZ - 1)], column_sems.at[0])
        return
    for device in plane:
        remote(block, block, gather_sems, device).start()
    slots = from_plane.at[0]
    remote(slots, slots, gather_sems, sibling).wait_recv()
    mine = applied.at[pl.ds(core * HALF, HALF)]
    share = remote(mine, mine, share_sem, sibling)
    share.start()
    if stop == 5:
        share.wait()
        others.wait_send()
        wait_swaps(0)
        wait_send(from_plane.at[0], plane_sems.at[0])
        wait_send(from_plane.at[0], gather_sems)
        wait_send(columns.at[0, pl.ds(0, NZ - 1)], column_sems.at[0])
        return

    next_half(core)
    doubles_0, singles_0 = expand(core)
    share.wait_recv()
    next_half(1 - core)
    doubles_1, singles_1 = expand(1 - core)
    finish_half(doubles_0 + doubles_1, singles_0 + singles_1)
    fold(1)
    line = jnp.zeros((1, LANES), F32)
    for g in range(GROUPS):
        squares = jnp.zeros((SUB, LANES), F32)
        for b in range(BLOCKS):
            res_re, res_im = res[b, pl.ds(g * PIECE, SUB), :], res[b, pl.ds(g * PIECE + SUB, SUB), :]
            squares = squares + (res_re * res_re + res_im * res_im)
        line = line + line_of(squares, g)
    rms_ref[0:1, :] = rms_of(line)
    mine = x * 2 + core
    rows, re_rows = pl.ds(y * SUB, SUB), pl.ds(y * PIECE, SUB)
    im_rows = pl.ds(y * PIECE + SUB, SUB)
    re, im, lev = resp[1, mine, re_rows, :], resp[1, mine, im_rows, :], level[mine, rows, :]
    base_re = rhs[mine, rows, :] - (lev * re + DAMP * im)
    base_im = -(lev * im - DAMP * re)
    total = collect(1)
    if stop != 6:
        res_re, res_im = base_re - total[:SUB], base_im - total[SUB:]
        line = line_of(res_re * res_re + res_im * res_im, y)
        lines[mine * GROUPS + y] = line
        line_out[...] = line
        for device in everyone:
            remote(line_out, lines.at[mine * GROUPS + y], line_sems, device).start()
        p_re, p_im = pre_re[mine, rows, :], pre_im[mine, rows, :]
        final[core, 0, rows, :] = re + (res_re * p_re - res_im * p_im)
        final[core, 1, rows, :] = im + (res_im * p_re + res_re * p_im)
        block = final.at[core, :, rows]
        near = [place(x, lax.rem(y + d, NY), z, c) for d in ALONG[:-1] for c in (1 - core, core)]
        for device in near + [sibling]:
            remote(block, block, final_sems, device).start()
        seven = columns.at[1, pl.ds(0, NZ - 1)]
        remote(seven, seven, final_sems, sibling).wait_recv()
        out_ref[...] = final[z_hi]
        most = lines.at[pl.ds(0, BLOCKS * GROUPS - 1)]
        remote(most, most, line_sems, sibling).wait_recv()
        rms_ref[1:2, :] = rms_of(jnp.sum(lines[...], axis=0))
        wait_send(most, line_sems)
        wait_send(seven, final_sems)

    others.wait_send()
    share.wait_send()
    wait_send(from_plane.at[0], gather_sems)
    for sweep in range(2):
        wait_swaps(sweep)
        wait_send(from_plane.at[sweep], plane_sems.at[sweep])
        wait_send(columns.at[sweep, pl.ds(0, NZ - 1)], column_sems.at[sweep])


def tail(response_in, rms_in, response_out, rms_out):
    response_out[...] = response_in[...]
    rms_out[...] = rms_in[...]


def per_device(
    amplitudes, integral_slab, coupling, pair_of_block, pair_shift, virt_energy,
    core_energy, core_index, frequency, dipole, stop=None, cid=0, name="response",
):
    rows, virt_total = amplitudes.shape
    k_total = GROUPS * SUB
    whole, wide_whole = (BLOCKS, k_total, LANES), (BLOCKS, COLS, LANES)
    vmem = pl.BlockSpec(memory_space=pltpu.VMEM)
    anywhere = pl.BlockSpec(memory_space=pl.ANY)
    dma = pltpu.SemaphoreType.DMA
    shapes = (
        jax.ShapeDtypeStruct((2, k_total, LANES), F32),
        jax.ShapeDtypeStruct((2, k_total), F32),
    )
    response, rms = pl.pallas_call(
        partial(kernel, stop),
        name=name,
        out_shape=shapes,
        in_specs=[anywhere] * 10,
        out_specs=(vmem, vmem),
        scratch_shapes=[
            pltpu.SMEM(pair_of_block.shape, jnp.int32),
            pltpu.SMEM(pair_shift.shape, F32),
            pltpu.SMEM(core_energy.shape, F32),
            pltpu.SMEM(core_index.shape, jnp.int32),
            pltpu.SMEM(frequency.shape, F32),
            pltpu.VMEM((BLOCKS, LANES), F32),
            pltpu.VMEM(dipole.shape, F32),
            pltpu.VMEM((rows, virt_total), BF16),
            pltpu.VMEM((rows, virt_total), BF16),
            pltpu.VMEM((virt_total, virt_total), F32),
            pltpu.VMEM((virt_total, rows), BF16),
            pltpu.VMEM((virt_total, virt_total), BF16),
            pltpu.VMEM((virt_total, virt_total), BF16),
            pltpu.VMEM((virt_total, virt_total), BF16),
            pltpu.VMEM((virt_total, virt_total), BF16),
            pltpu.VMEM((2, LANES), F32),
            pltpu.VMEM((BLOCKS, 2, LANES), F32),
            pltpu.VMEM(whole, F32),
            pltpu.VMEM(whole, F32),
            pltpu.VMEM(whole, F32),
            pltpu.VMEM(whole, F32),
            pltpu.VMEM(whole, F32),
            pltpu.VMEM(whole, F32),
            pltpu.VMEM((2,) + wide_whole, F32),
            pltpu.VMEM(wide_whole, F32),
            pltpu.VMEM(wide_whole, F32),
            pltpu.VMEM((2, 2 * COLS, HALF_COLS), BF16),
            pltpu.VMEM((2 * COLS, rows), BF16),
            pltpu.VMEM((2 * COLS, virt_total), BF16),
            pltpu.VMEM((2, 2, 2, COLS, LANES), F32),
            pltpu.VMEM((2, 2, 2, COLS, LANES), F32),
            pltpu.VMEM((2, HALF, COLS, LANES), F32),
            pltpu.VMEM((2, len(PLANE), PIECE, LANES), F32),
            pltpu.VMEM((2, NZ, PIECE, LANES), F32),
            pltpu.VMEM(wide_whole, F32),
            pltpu.VMEM((2, 2, k_total, LANES), F32),
            pltpu.VMEM((BLOCKS * GROUPS, 1, LANES), F32),
            pltpu.VMEM((1, LANES), F32),
            dma((7,)),
            dma((3,)),
            dma((2,)),
            dma((2, 2, 2)),
            dma((2, 2)),
            dma((2, 2)),
            dma((2,)),
            dma((2,)),
            dma((2,)),
            dma((2,)),
        ],
        compiler_params=pltpu.CompilerParams(
            collective_id=cid, has_side_effects=True, vmem_limit_bytes=56 * 2**20
        ),
    )(
        pair_of_block, pair_shift, core_energy, core_index, frequency,
        virt_energy.reshape(BLOCKS, LANES), dipole, amplitudes, integral_slab, coupling,
    )
    return pl.pallas_call(
        tail, name="tail", out_shape=shapes, in_specs=[vmem, vmem], out_specs=(vmem, vmem)
    )(response, rms)


def solution(mesh):
    rows = P(("wide", "narrow"), None)
    placed = (rows, rows, P(("wide", "narrow"), None, None)) + (P(),) * 6 + (P(None, "narrow"),)
    return jax.shard_map(
        per_device,
        mesh=mesh,
        in_specs=placed,
        out_specs=(P(None, None, "narrow"), P()),
        check_vma=False,
    )
```

```python
from functools import partial

import jax
import jax.numpy as jnp
from jax import lax
from jax.experimental import pallas as pl
from jax.experimental.pallas import tpu as pltpu
from jax.sharding import PartitionSpec as P

DAMP = 0.5
MESH = pl.DeviceIdType.MESH
F32 = jnp.float32
BF16 = jnp.bfloat16

NX, NY, NZ, NZLO = 4, 4, 8, 4


def ring(step, size):
    return min(step, size - step)


PLANE = tuple(
    sorted(
        tuple((dx, dy) for dx in range(NX) for dy in range(NY))[1:],
        key=lambda d: -ring(d[0], NX) - ring(d[1], NY),
    )
)
COLUMN = tuple(sorted(range(1, NZ), key=lambda d: -ring(d, NZ)))
ALONG = (2, 1, 3, 0)
GROUPS, SUB, LANES, BLOCKS = 4, 8, 128, 8
PIECE = 2 * SUB
COLS = GROUPS * PIECE
HALF = BLOCKS // 2
HALF_COLS = HALF * LANES
STRIP = 256


def place(x, y, z, core):
    return {
        "wide": (y * NZLO + lax.rem(z, NZLO)) * 2 + core,
        "narrow": x * 2 + z // NZLO,
    }


def nn(left, right):
    return lax.dot_general(left, right, (((1,), (0,)), ((), ())), preferred_element_type=F32)


def halves(value):
    high = value.astype(BF16)
    low = (value - high.astype(F32)).astype(BF16)
    return high, low


def remote(src, dst, sems, device):
    return pltpu.make_async_remote_copy(
        src_ref=src, dst_ref=dst, send_sem=sems.at[0], recv_sem=sems.at[1],
        device_id=device, device_id_type=MESH,
    )


def kernel(
    stop,
    pair_of_block_hbm, pair_shift_hbm, core_energy_hbm, core_index_hbm, frequency_hbm,
    virt_hbm, dipole_hbm, amp_hbm, slab_hbm, coup_hbm,
    out_ref, rms_ref,
    pair_of_block, pair_shift, core_energy, core_index, frequency, virt, dipole,
    slab, coup, slab_t, right, coup_t,
    picked, dip, rhs, pre_re, pre_im, level, den_re, den_im, resp, base, res,
    pieces, left,
    part, from_core, own, from_plane, columns, applied, final, lines, line_out,
    small_sem, hbm_sem, dip_sems, core_sems, plane_sems, column_sems, gather_sems, share_sem,
    final_sems, line_sems,
):
    wide, narrow = lax.axis_index("wide"), lax.axis_index("narrow")
    x, y, core = narrow // 2, wide // (2 * NZLO), lax.rem(wide, 2)
    z_hi, z_lo = lax.rem(narrow, 2), lax.rem(wide // 2, NZLO)
    z = z_hi * NZLO + z_lo
    mirror = (1 - z_hi) * NZLO + lax.rem(z_lo + 2, NZLO)

    sibling = place(x, y, z, 1 - core)
    plane_xy = [(lax.rem(x + dx, NX), lax.rem(y + dy, NY)) for dx, dy in PLANE]
    plane = [place(to_x, to_y, z, core) for to_x, to_y in plane_xy]
    across = [place(to_x, to_y, z, 1 - core) for to_x, to_y in plane_xy]
    everyone = [device for pair in zip(across, plane) for device in pair] + [sibling]
    column = [place(x, y, lax.rem(z + d, NZ), core) for d in COLUMN]
    mirrors = [place(lax.rem(x + d, NX), y, mirror, core) for d in ALONG]
    holders = mirrors + [place(lax.rem(x + d, NX), y, z, core) for d in ALONG[:-1]]

    barrier = pltpu.get_barrier_semaphore()
    greeted = mirrors[:-1] + column + everyone
    for device in greeted:
        pl.semaphore_signal(barrier, inc=1, device_id=device, device_id_type=MESH)

    rows_total, virt_total = slab.shape
    small = [
        pltpu.make_async_copy(src, dst, small_sem.at[i])
        for i, (src, dst) in enumerate((
            (core_index_hbm, core_index), (dipole_hbm, dipole), (virt_hbm, virt),
            (core_energy_hbm, core_energy), (frequency_hbm, frequency),
            (pair_of_block_hbm, pair_of_block), (pair_shift_hbm, pair_shift),
        ))
    ]
    loads = [
        pltpu.make_async_copy(coup_hbm.at[0], coup, hbm_sem.at[0]),
        pltpu.make_async_copy(slab_hbm, slab, hbm_sem.at[1]),
        pltpu.make_async_copy(amp_hbm, right.at[pl.ds(0, rows_total)], hbm_sem.at[2]),
    ]
    for load in small + loads:
        load.start()

    for load in small:
        load.wait()
    for c in range(2):
        picked[c : c + 1, :] = dipole[pl.ds(core_index[c], 1), :]
    pl.semaphore_wait(barrier, len(greeted))
    if stop == 0:
        for load in loads:
            load.wait()
        return
    for device in holders:
        remote(picked, dip.at[narrow], dip_sems, device).start()
    dip[narrow] = picked[...]

    sublane = lax.broadcasted_iota(jnp.int32, (SUB, LANES), 0)
    lane = lax.broadcasted_iota(jnp.int32, (SUB, LANES), 1)
    offset = pair_shift[pair_of_block[wide * 8 + narrow]]
    for g in range(GROUPS):
        energy = core_energy[core_index[g // 2]]
        shift = jnp.zeros((SUB, LANES), F32)
        for j in range(SUB):
            value = frequency[(g % 2) * SUB + j] + energy
            shift = jnp.where(sublane == j, value, shift)
        rows = pl.ds(g * SUB, SUB)
        for b in range(BLOCKS):
            energies = jnp.broadcast_to(virt[b : b + 1, :], (SUB, LANES))
            lev = energies - shift
            inverse = 1.0 / (lev * lev + DAMP * DAMP)
            level[b, rows, :] = lev
            pre_re[b, rows, :] = lev * inverse
            pre_im[b, rows, :] = DAMP * inverse
            den = (shift - offset) - energies
            inverse = 1.0 / (den * den + DAMP * DAMP)
            den_re[b, rows, :] = den * inverse
            den_im[b, rows, :] = DAMP * inverse
    if stop == "a":
        for load in loads:
            load.wait()
        dips = dip.at[pl.ds(0, BLOCKS - 1)]
        remote(dips, dips, dip_sems, sibling).wait()
        return

    loads[0].wait()

    def split_rows(i, _):
        rows = pl.ds(pl.multiple_of(i * STRIP, STRIP), STRIP)
        strip = coup[rows, :]
        high, low = halves(strip)
        start = rows_total + i * STRIP
        right[pl.ds(pl.multiple_of(start, STRIP), STRIP), :] = high
        right[pl.ds(pl.multiple_of(start + virt_total, STRIP), STRIP), :] = low
        high, low = high.T, low.T
        for half in range(2):
            own_rows = slice(half * HALF_COLS, (half + 1) * HALF_COLS)
            coup_t[2 * half * HALF_COLS : (2 * half + 1) * HALF_COLS, rows] = high[own_rows]
            coup_t[(2 * half + 1) * HALF_COLS : (2 * half + 2) * HALF_COLS, rows] = low[own_rows]
        return 0

    lax.fori_loop(0, coup.shape[0] // STRIP, split_rows, 0)
    loads[1].wait()

    def turn_rows(i, _):
        rows = pl.ds(pl.multiple_of(i * STRIP, STRIP), STRIP)
        slab_t[:, rows] = slab[rows, :].T
        return 0

    lax.fori_loop(0, slab.shape[0] // STRIP, turn_rows, 0)
    loads[2].wait()
    if stop == "b":
        dips = dip.at[pl.ds(0, BLOCKS - 1)]
        remote(dips, dips, dip_sems, sibling).wait()
        return

    dips = dip.at[pl.ds(0, BLOCKS - 1)]
    others = remote(dips, dips, dip_sems, sibling)
    others.wait_recv()
    if stop == 1:
        others.wait_send()
        return

    def start_half(half):
        for g in range(GROUPS):
            rows, re_rows, im_rows = pl.ds(g * SUB, SUB), pl.ds(g * PIECE, SUB), pl.ds(g * PIECE + SUB, SUB)
            for j in range(HALF):
                b, cols = half * HALF + j, slice(j * LANES, (j + 1) * LANES)
                source = jnp.broadcast_to(dip[b, g // 2 : g // 2 + 1, :], (SUB, LANES))
                rhs[b, rows, :] = source
                re, im = source * pre_re[b, rows, :], source * pre_im[b, rows, :]
                resp[0, b, re_rows, :] = re
                resp[0, b, im_rows, :] = im
                high, low = halves(jnp.concatenate([re, im], 0))
                pieces[half, g * PIECE : (g + 1) * PIECE, cols] = high
                pieces[half, COLS + g * PIECE : COLS + (g + 1) * PIECE, cols] = low

    def next_half(half):
        for g in range(GROUPS):
            rows, re_rows, im_rows = pl.ds(g * SUB, SUB), pl.ds(g * PIECE, SUB), pl.ds(g * PIECE + SUB, SUB)
            for j in range(HALF):
                b, cols = half * HALF + j, slice(j * LANES, (j + 1) * LANES)
                res_re = base[b, re_rows, :] - applied[b, re_rows, :]
                res_im = base[b, im_rows, :] - applied[b, im_rows, :]
                res[b, re_rows, :] = res_re
                res[b, im_rows, :] = res_im
                p_re, p_im = pre_re[b, rows, :], pre_im[b, rows, :]
                re = resp[0, b, re_rows, :] + (res_re * p_re - res_im * p_im)
                im = resp[0, b, im_rows, :] + (res_im * p_re + res_re * p_im)
                resp[1, b, re_rows, :] = re
                resp[1, b, im_rows, :] = im
                high, low = halves(jnp.concatenate([re, im], 0))
                pieces[half, g * PIECE : (g + 1) * PIECE, cols] = high
                pieces[half, COLS + g * PIECE : COLS + (g + 1) * PIECE, cols] = low

    def joined(both):
        return both[:COLS] + both[COLS:]

    def expand(half):
        piece = pieces[half]
        rows = pl.ds(pl.multiple_of(half * 2 * HALF_COLS, HALF_COLS), 2 * HALF_COLS)
        doubles = nn(jnp.concatenate([piece, piece], 1), coup_t[rows, :])
        rows = pl.ds(pl.multiple_of(half * HALF_COLS, HALF_COLS), HALF_COLS)
        return joined(doubles), joined(nn(piece, slab_t[rows, :]))

    def finish(doubles, singles):
        for g in range(GROUPS):
            rows = pl.ds(g * SUB, SUB)
            for b in range(BLOCKS):
                cols = slice(b * LANES, (b + 1) * LANES)
                real = doubles[g * PIECE : g * PIECE + SUB, cols]
                imag = doubles[g * PIECE + SUB : (g + 1) * PIECE, cols]
                q_re, q_im = den_re[b, rows, :], den_im[b, rows, :]
                quotient = jnp.concatenate([real * q_re + imag * q_im, imag * q_re - real * q_im], 0)
                high, low = halves(quotient)
                cols = slice(rows_total + b * LANES, rows_total + (b + 1) * LANES)
                left[g * PIECE : (g + 1) * PIECE, cols] = high
                left[COLS + g * PIECE : COLS + (g + 1) * PIECE, cols] = low
        high, low = halves(singles)
        left[:COLS, :rows_total] = high
        left[COLS:, :rows_total] = low

    parity, far = lax.rem(x, 2), 1 - x // 2
    strips = (far, 1 - far)
    reach = ((2 * far + parity, 2 * far + 1 - parity), (3 - 2 * far - parity, 2 - 2 * far + parity))

    def fold(sweep):
        def share_of(side, strip):
            if sweep == 0:
                first = pl.multiple_of(side * HALF_COLS + strip * STRIP, STRIP)
                spans = [pl.ds(first, STRIP)]
            else:
                spans = [
                    pl.ds(pl.multiple_of((4 * strip + 2 * i + side) * LANES, LANES), LANES) for i in range(2)
                ]

            strip_of = [right[:, span] for span in spans]
            strip_of = jnp.concatenate(strip_of, 1) if sweep else strip_of[0]
            return joined(nn(jnp.concatenate([left[...], left[:, rows_total:]], 1), strip_of))

        swaps = []
        for turn, strip in enumerate(strips):
            share = share_of(1 - core, strip)
            for i in range(2):
                part[sweep, turn, i] = share[:, i * LANES : (i + 1) * LANES]
            swap = remote(part.at[sweep, turn], from_core.at[sweep, turn], core_sems.at[sweep, turn], sibling)
            swap.start()
            swaps.append(swap)
        slot = 0
        for turn, strip in enumerate(strips):
            share = share_of(core, strip)
            swaps[turn].wait_recv()
            for i in range(2):
                own[sweep, 2 * strip + i] = share[:, i * LANES : (i + 1) * LANES] + from_core[sweep, turn, i]
            if stop == 2:
                continue
            for to_x in reach[turn]:
                for dy in ALONG[: NY if slot < 3 * NY else NY - 1]:
                    to_y = lax.rem(y + dy, NY)
                    remote(
                        own.at[sweep, to_x, pl.ds(to_y * PIECE, PIECE)], from_plane.at[sweep, slot],
                        plane_sems.at[sweep], place(to_x, to_y, z, core),
                    ).start()
                    slot += 1
        if stop == 2:
            for swap in swaps:
                swap.wait_send()

    def wait_send(ref, sems):
        remote(ref, ref, sems, sibling).wait_send()

    def wait_swaps(sweep):
        for turn in range(2):
            wait_send(from_core.at[sweep, turn], core_sems.at[sweep, turn])

    def collect(sweep):
        slots = from_plane.at[sweep]
        remote(slots, slots, plane_sems.at[sweep], sibling).wait_recv()
        total = own[sweep, x, pl.ds(y * PIECE, PIECE), :]
        for i in range(len(plane)):
            total = total + from_plane[sweep, i]
        columns[sweep, z] = total
        if stop == 3:
            wait_send(slots, plane_sems.at[sweep])
            return None
        for device in column:
            remote(columns.at[sweep, z], columns.at[sweep, z], column_sems.at[sweep], device).start()
        seven = columns.at[sweep, pl.ds(0, NZ - 1)]
        remote(seven, seven, column_sems.at[sweep], sibling).wait_recv()
        total = columns[sweep, 0]
        for i in range(1, NZ):
            total = total + columns[sweep, i]
        return total

    def line_of(squares, group):
        summed = jnp.broadcast_to(jnp.sum(squares, axis=1, keepdims=True), (SUB, LANES))
        return jnp.sum(jnp.where(lane == sublane + group * SUB, summed, 0.0), axis=0, keepdims=True)

    def rms_of(line):
        return jnp.sqrt(line / (2 * BLOCKS * LANES) + 1e-06)[:, : GROUPS * SUB]

    start_half(0)
    start_half(1)
    both = [pieces[0], pieces[1]]
    doubles = joined(nn(jnp.concatenate([both[0], both[0], both[1], both[1]], 1), coup_t[...]))
    finish(doubles, joined(nn(jnp.concatenate(both, 1), slab_t[...])))
    fold(0)
    if stop == 2:
        others.wait_send()
        return
    for g in range(GROUPS):
        rows, re_rows, im_rows = pl.ds(g * SUB, SUB), pl.ds(g * PIECE, SUB), pl.ds(g * PIECE + SUB, SUB)
        for b in range(BLOCKS):
            re, im, lev = resp[0, b, re_rows, :], resp[0, b, im_rows, :], level[b, rows, :]
            base[b, re_rows, :] = rhs[b, rows, :] - (lev * re + DAMP * im)
            base[b, im_rows, :] = -(lev * im - DAMP * re)
    total = collect(0)
    if stop == 3:
        others.wait_send()
        wait_swaps(0)
        return
    block = applied.at[core * HALF + x, pl.ds(y * PIECE, PIECE)]
    applied[core * HALF + x, pl.ds(y * PIECE, PIECE), :] = total
    if stop == 4:
        others.wait_send()
        wait_swaps(0)
        wait_send(from_plane.at[0], plane_sems.at[0])
        wait_send(columns.at[0, pl.ds(0, NZ - 1)], column_sems.at[0])
        return
    for device in plane:
        remote(block, block, gather_sems, device).start()
    slots = from_plane.at[0]
    remote(slots, slots, gather_sems, sibling).wait_recv()
    mine = applied.at[pl.ds(core * HALF, HALF)]
    share = remote(mine, mine, share_sem, sibling)
    share.start()
    if stop == 5:
        share.wait()
        others.wait_send()
        wait_swaps(0)
        wait_send(from_plane.at[0], plane_sems.at[0])
        wait_send(from_plane.at[0], gather_sems)
        wait_send(columns.at[0, pl.ds(0, NZ - 1)], column_sems.at[0])
        return

    next_half(core)
    doubles_0, singles_0 = expand(core)
    share.wait_recv()
    next_half(1 - core)
    doubles_1, singles_1 = expand(1 - core)
    finish(doubles_0 + doubles_1, singles_0 + singles_1)
    fold(1)
    line = jnp.zeros((1, LANES), F32)
    for g in range(GROUPS):
        squares = jnp.zeros((SUB, LANES), F32)
        for b in range(BLOCKS):
            res_re, res_im = res[b, pl.ds(g * PIECE, SUB), :], res[b, pl.ds(g * PIECE + SUB, SUB), :]
            squares = squares + (res_re * res_re + res_im * res_im)
        line = line + line_of(squares, g)
    rms_ref[0:1, :] = rms_of(line)
    mine = x * 2 + core
    rows, re_rows = pl.ds(y * SUB, SUB), pl.ds(y * PIECE, SUB)
    im_rows = pl.ds(y * PIECE + SUB, SUB)
    re, im, lev = resp[1, mine, re_rows, :], resp[1, mine, im_rows, :], level[mine, rows, :]
    base_re = rhs[mine, rows, :] - (lev * re + DAMP * im)
    base_im = -(lev * im - DAMP * re)
    total = collect(1)
    if stop != 6:
        res_re, res_im = base_re - total[:SUB], base_im - total[SUB:]
        line = line_of(res_re * res_re + res_im * res_im, y)
        lines[mine * GROUPS + y] = line
        line_out[...] = line
        for device in everyone:
            remote(line_out, lines.at[mine * GROUPS + y], line_sems, device).start()
        p_re, p_im = pre_re[mine, rows, :], pre_im[mine, rows, :]
        final[core, 0, rows, :] = re + (res_re * p_re - res_im * p_im)
        final[core, 1, rows, :] = im + (res_im * p_re + res_re * p_im)
        block = final.at[core, :, rows]
        near = [place(x, lax.rem(y + d, NY), z, c) for d in ALONG[:-1] for c in (1 - core, core)]
        for device in near + [sibling]:
            remote(block, block, final_sems, device).start()
        seven = columns.at[1, pl.ds(0, NZ - 1)]
        remote(seven, seven, final_sems, sibling).wait_recv()
        out_ref[...] = final[z_hi]
        most = lines.at[pl.ds(0, BLOCKS * GROUPS - 1)]
        remote(most, most, line_sems, sibling).wait_recv()
        rms_ref[1:2, :] = rms_of(jnp.sum(lines[...], axis=0))
        wait_send(most, line_sems)
        wait_send(seven, final_sems)

    others.wait_send()
    share.wait_send()
    wait_send(from_plane.at[0], gather_sems)
    for sweep in range(2):
        wait_swaps(sweep)
        wait_send(from_plane.at[sweep], plane_sems.at[sweep])
        wait_send(columns.at[sweep, pl.ds(0, NZ - 1)], column_sems.at[sweep])


def tail(response_in, rms_in, response_out, rms_out):
    response_out[...] = response_in[...]
    rms_out[...] = rms_in[...]


def per_device(
    amplitudes, integral_slab, coupling, pair_of_block, pair_shift, virt_energy,
    core_energy, core_index, frequency, dipole, stop=None, cid=0, name="response",
):
    rows, virt_total = amplitudes.shape
    k_total = GROUPS * SUB
    whole, wide_whole = (BLOCKS, k_total, LANES), (BLOCKS, COLS, LANES)
    vmem = pl.BlockSpec(memory_space=pltpu.VMEM)
    anywhere = pl.BlockSpec(memory_space=pl.ANY)
    dma = pltpu.SemaphoreType.DMA
    shapes = (
        jax.ShapeDtypeStruct((2, k_total, LANES), F32),
        jax.ShapeDtypeStruct((2, k_total), F32),
    )
    response, rms = pl.pallas_call(
        partial(kernel, stop),
        name=name,
        out_shape=tuple(pltpu.VMEM(shape.shape, shape.dtype) for shape in shapes),
        in_specs=[anywhere] * 10,
        out_specs=(vmem, vmem),
        scratch_shapes=[
            pltpu.SMEM(pair_of_block.shape, jnp.int32),
            pltpu.SMEM(pair_shift.shape, F32),
            pltpu.SMEM(core_energy.shape, F32),
            pltpu.SMEM(core_index.shape, jnp.int32),
            pltpu.SMEM(frequency.shape, F32),
            pltpu.VMEM((BLOCKS, LANES), F32),
            pltpu.VMEM(dipole.shape, F32),
            pltpu.VMEM((rows, virt_total), BF16),
            pltpu.VMEM((virt_total, virt_total), F32),
            pltpu.VMEM((virt_total, rows), BF16),
            pltpu.VMEM((rows + 2 * virt_total, virt_total), BF16),
            pltpu.VMEM((2 * virt_total, virt_total), BF16),
            pltpu.VMEM((2, LANES), F32),
            pltpu.VMEM((BLOCKS, 2, LANES), F32),
            pltpu.VMEM(whole, F32),
            pltpu.VMEM(whole, F32),
            pltpu.VMEM(whole, F32),
            pltpu.VMEM(whole, F32),
            pltpu.VMEM(whole, F32),
            pltpu.VMEM(whole, F32),
            pltpu.VMEM((2,) + wide_whole, F32),
            pltpu.VMEM(wide_whole, F32),
            pltpu.VMEM(wide_whole, F32),
            pltpu.VMEM((2, 2 * COLS, HALF_COLS), BF16),
            pltpu.VMEM((2 * COLS, rows + virt_total), BF16),
            pltpu.VMEM((2, 2, 2, COLS, LANES), F32),
            pltpu.VMEM((2, 2, 2, COLS, LANES), F32),
            pltpu.VMEM((2, HALF, COLS, LANES), F32),
            pltpu.VMEM((2, len(PLANE), PIECE, LANES), F32),
            pltpu.VMEM((2, NZ, PIECE, LANES), F32),
            pltpu.VMEM(wide_whole, F32),
            pltpu.VMEM((2, 2, k_total, LANES), F32),
            pltpu.VMEM((BLOCKS * GROUPS, 1, LANES), F32),
            pltpu.VMEM((1, LANES), F32),
            dma((7,)),
            dma((3,)),
            dma((2,)),
            dma((2, 2, 2)),
            dma((2, 2)),
            dma((2, 2)),
            dma((2,)),
            dma((2,)),
            dma((2,)),
            dma((2,)),
        ],
        compiler_params=pltpu.CompilerParams(
            collective_id=cid, has_side_effects=True, vmem_limit_bytes=56 * 2**20
        ),
    )(
        pair_of_block, pair_shift, core_energy, core_index, frequency,
        virt_energy.reshape(BLOCKS, LANES), dipole, amplitudes, integral_slab, coupling,
    )
    return pl.pallas_call(
        tail, name="tail", out_shape=shapes, in_specs=[vmem, vmem], out_specs=(vmem, vmem)
    )(*(pltpu.with_memory_space_constraint(value, pltpu.VMEM) for value in (response, rms)))


def solution(mesh):
    rows = P(("wide", "narrow"), None)
    placed = (rows, rows, P(("wide", "narrow"), None, None)) + (P(),) * 6 + (P(None, "narrow"),)
    return jax.shard_map(
        per_device,
        mesh=mesh,
        in_specs=placed,
        out_specs=(P(None, None, "narrow"), P()),
        check_vma=False,
    )
```

```python
import jax
import jax.numpy as jnp
from jax import lax
from jax.experimental import pallas as pl
from jax.experimental.pallas import tpu as pltpu
from jax.sharding import PartitionSpec as P

DAMP = 0.5
MESH = pl.DeviceIdType.MESH
F32 = jnp.float32
BF16 = jnp.bfloat16

NX, NY, NZ, NZLO = 4, 4, 8, 4


def ring(step, size):
    return min(step, size - step)


PLANE = tuple(
    sorted(
        tuple((dx, dy) for dx in range(NX) for dy in range(NY))[1:],
        key=lambda d: -ring(d[0], NX) - ring(d[1], NY),
    )
)
COLUMN = tuple(sorted(range(1, NZ), key=lambda d: -ring(d, NZ)))
ALONG = (2, 1, 3, 0)
GROUPS, SUB, LANES, BLOCKS = 4, 8, 128, 8
PIECE = 2 * SUB
COLS = GROUPS * PIECE
HALF = BLOCKS // 2
HALF_COLS = HALF * LANES
STRIP = 256


def place(x, y, z, core):
    return {
        "wide": (y * NZLO + lax.rem(z, NZLO)) * 2 + core,
        "narrow": x * 2 + z // NZLO,
    }


def spot(block):
    return (block % 2) * HALF + block // 2


def nn(left, right):
    return lax.dot_general(left, right, (((1,), (0,)), ((), ())), preferred_element_type=F32)


def halves(value):
    high = value.astype(BF16)
    low = (value - high.astype(F32)).astype(BF16)
    return high, low


def remote(src, dst, sems, device):
    return pltpu.make_async_remote_copy(
        src_ref=src, dst_ref=dst, send_sem=sems.at[0], recv_sem=sems.at[1],
        device_id=device, device_id_type=MESH,
    )


def kernel(
    pair_of_block_hbm, pair_shift_hbm, core_energy_hbm, core_index_hbm, frequency_hbm,
    virt_hbm, dipole_hbm, amp_hbm, slab_hbm, coup_hbm,
    out_ref, rms_ref,
    pair_of_block, pair_shift, core_energy, core_index, frequency, virt, dipole,
    slab, coup, slab_t, right, coup_t,
    picked, dip, rhs, pre_re, pre_im, level, den_re, den_im, resp, base, res,
    pieces, left,
    part, from_core, own, from_plane, columns, applied, final, lines, line_out,
    small_sem, hbm_sem, dip_sems, core_sems, plane_sems, column_sems, gather_sems, share_sem,
    final_sems, line_sems,
):
    wide, narrow = lax.axis_index("wide"), lax.axis_index("narrow")
    x, y, core = narrow // 2, wide // (2 * NZLO), lax.rem(wide, 2)
    z_hi, z_lo = lax.rem(narrow, 2), lax.rem(wide // 2, NZLO)
    z = z_hi * NZLO + z_lo
    mirror = (1 - z_hi) * NZLO + lax.rem(z_lo + 2, NZLO)

    sibling = place(x, y, z, 1 - core)
    plane_xy = [(lax.rem(x + dx, NX), lax.rem(y + dy, NY)) for dx, dy in PLANE]
    plane = [place(to_x, to_y, z, core) for to_x, to_y in plane_xy]
    across = [place(to_x, to_y, z, 1 - core) for to_x, to_y in plane_xy]
    everyone = [device for pair in zip(across, plane) for device in pair] + [sibling]
    column = [place(x, y, lax.rem(z + d, NZ), core) for d in COLUMN]
    mirrors = [place(lax.rem(x + d, NX), y, mirror, core) for d in ALONG]
    beside = [place(lax.rem(x + d, NX), y, z, core) for d in ALONG[:-1]]

    barrier = pltpu.get_barrier_semaphore()
    far_plane = sum(ring(dx, NX) + ring(dy, NY) > 2 for dx, dy in PLANE)
    greeted = mirrors[:1] + column[:1] + everyone[: 2 * far_plane] + mirrors[1:-1] + column[1:]
    greeted = greeted + everyone[2 * far_plane :]
    for device in greeted:
        pl.semaphore_signal(barrier, inc=1, device_id=device, device_id_type=MESH)

    rows_total, virt_total = slab.shape
    small = [
        pltpu.make_async_copy(src, dst, small_sem.at[i])
        for i, (src, dst) in enumerate((
            (core_index_hbm, core_index), (dipole_hbm, dipole), (virt_hbm, virt),
            (core_energy_hbm, core_energy), (frequency_hbm, frequency),
            (pair_of_block_hbm, pair_of_block), (pair_shift_hbm, pair_shift),
        ))
    ]
    loads = [
        pltpu.make_async_copy(coup_hbm.at[0], coup, hbm_sem.at[0]),
        pltpu.make_async_copy(slab_hbm, slab, hbm_sem.at[1]),
    ] + [
        pltpu.make_async_copy(
            amp_hbm.at[:, pl.ds(b * LANES, LANES)],
            right.at[pl.ds(0, rows_total), pl.ds(spot(b) * LANES, LANES)],
            hbm_sem.at[2 + b],
        )
        for b in range(BLOCKS)
    ]
    for load in small + loads:
        load.start()

    for load in small:
        load.wait()
    for c in range(2):
        picked[c : c + 1, :] = dipole[pl.ds(core_index[c], 1), :]
    pl.semaphore_wait(barrier, len(greeted))
    for device in mirrors:
        remote(picked, dip.at[narrow], dip_sems.at[1], device).start()
    for device in beside:
        remote(picked, dip.at[narrow], dip_sems.at[0], device).start()
    dip[narrow] = picked[...]

    sublane = lax.broadcasted_iota(jnp.int32, (SUB, LANES), 0)
    lane = lax.broadcasted_iota(jnp.int32, (SUB, LANES), 1)
    offset = pair_shift[pair_of_block[wide * 8 + narrow]]
    for g in range(GROUPS):
        energy = core_energy[core_index[g // 2]]
        shift = jnp.zeros((SUB, LANES), F32)
        for j in range(SUB):
            value = frequency[(g % 2) * SUB + j] + energy
            shift = jnp.where(sublane == j, value, shift)
        rows = pl.ds(g * SUB, SUB)
        for b in range(BLOCKS):
            energies = jnp.broadcast_to(virt[b : b + 1, :], (SUB, LANES))
            lev = energies - shift
            inverse = 1.0 / (lev * lev + DAMP * DAMP)
            level[spot(b), rows, :] = lev
            pre_re[spot(b), rows, :] = lev * inverse
            pre_im[spot(b), rows, :] = DAMP * inverse
            den = (shift - offset) - energies
            inverse = 1.0 / (den * den + DAMP * DAMP)
            den_re[b, rows, :] = den * inverse
            den_im[b, rows, :] = DAMP * inverse
    loads[0].wait()

    def split_rows(i, _):
        rows = pl.ds(pl.multiple_of(i * STRIP, STRIP), STRIP)
        strip = coup[rows, :]
        high, low = halves(strip)
        start = rows_total + i * STRIP
        for b in range(BLOCKS):
            cols, there = slice(b * LANES, (b + 1) * LANES), slice(spot(b) * LANES, (spot(b) + 1) * LANES)
            right[pl.ds(pl.multiple_of(start, STRIP), STRIP), there] = high[:, cols]
            right[pl.ds(pl.multiple_of(start + virt_total, STRIP), STRIP), there] = low[:, cols]
        high, low = high.T, low.T
        for b in range(BLOCKS):
            cols, there = slice(b * LANES, (b + 1) * LANES), (b % 2) * 2 * HALF_COLS + (b // 2) * LANES
            coup_t[there : there + LANES, rows] = high[cols]
            coup_t[there + HALF_COLS : there + HALF_COLS + LANES, rows] = low[cols]
        return 0

    lax.fori_loop(0, coup.shape[0] // STRIP, split_rows, 0)
    loads[1].wait()

    def turn_rows(i, _):
        rows = pl.ds(pl.multiple_of(i * STRIP, STRIP), STRIP)
        turned = slab[rows, :].T
        for b in range(BLOCKS):
            slab_t[spot(b) * LANES : (spot(b) + 1) * LANES, rows] = turned[b * LANES : (b + 1) * LANES]
        return 0

    lax.fori_loop(0, slab.shape[0] // STRIP, turn_rows, 0)
    for load in loads[2:]:
        load.wait()
    same = remote(dip.at[pl.ds(0, NX - 1)], dip.at[pl.ds(0, NX - 1)], dip_sems.at[0], sibling)
    mirrored = remote(dip.at[pl.ds(0, NX)], dip.at[pl.ds(0, NX)], dip_sems.at[1], sibling)

    def start_half(half):
        for g in range(GROUPS):
            rows, re_rows, im_rows = pl.ds(g * SUB, SUB), pl.ds(g * PIECE, SUB), pl.ds(g * PIECE + SUB, SUB)
            for j in range(HALF):
                b, cols = half * HALF + j, slice(j * LANES, (j + 1) * LANES)
                source = jnp.broadcast_to(dip[2 * j + half, g // 2 : g // 2 + 1, :], (SUB, LANES))
                rhs[b, rows, :] = source
                re, im = source * pre_re[b, rows, :], source * pre_im[b, rows, :]
                resp[0, b, re_rows, :] = re
                resp[0, b, im_rows, :] = im
                high, low = halves(jnp.concatenate([re, im], 0))
                pieces[half, g * PIECE : (g + 1) * PIECE, cols] = high
                pieces[half, COLS + g * PIECE : COLS + (g + 1) * PIECE, cols] = low

    def next_half(half):
        for g in range(GROUPS):
            rows, re_rows, im_rows = pl.ds(g * SUB, SUB), pl.ds(g * PIECE, SUB), pl.ds(g * PIECE + SUB, SUB)
            for j in range(HALF):
                b, cols = half * HALF + j, slice(j * LANES, (j + 1) * LANES)
                res_re = base[b, re_rows, :] - applied[b, re_rows, :]
                res_im = base[b, im_rows, :] - applied[b, im_rows, :]
                res[b, re_rows, :] = res_re
                res[b, im_rows, :] = res_im
                p_re, p_im = pre_re[b, rows, :], pre_im[b, rows, :]
                re = resp[0, b, re_rows, :] + (res_re * p_re - res_im * p_im)
                im = resp[0, b, im_rows, :] + (res_im * p_re + res_re * p_im)
                resp[1, b, re_rows, :] = re
                resp[1, b, im_rows, :] = im
                high, low = halves(jnp.concatenate([re, im], 0))
                pieces[half, g * PIECE : (g + 1) * PIECE, cols] = high
                pieces[half, COLS + g * PIECE : COLS + (g + 1) * PIECE, cols] = low

    def joined(both):
        return both[:COLS] + both[COLS:]

    def expand(half):
        piece = pieces[half]
        rows = pl.ds(pl.multiple_of(half * 2 * HALF_COLS, HALF_COLS), 2 * HALF_COLS)
        doubles = nn(jnp.concatenate([piece, piece], 1), coup_t[rows, :])
        rows = pl.ds(pl.multiple_of(half * HALF_COLS, HALF_COLS), HALF_COLS)
        return joined(doubles), joined(nn(piece, slab_t[rows, :]))

    def finish(doubles, singles):
        for g in range(GROUPS):
            rows = pl.ds(g * SUB, SUB)
            for b in range(BLOCKS):
                cols = slice(b * LANES, (b + 1) * LANES)
                real = doubles[g * PIECE : g * PIECE + SUB, cols]
                imag = doubles[g * PIECE + SUB : (g + 1) * PIECE, cols]
                q_re, q_im = den_re[b, rows, :], den_im[b, rows, :]
                quotient = jnp.concatenate([real * q_re + imag * q_im, imag * q_re - real * q_im], 0)
                high, low = halves(quotient)
                cols = slice(rows_total + b * LANES, rows_total + (b + 1) * LANES)
                left[g * PIECE : (g + 1) * PIECE, cols] = high
                left[COLS + g * PIECE : COLS + (g + 1) * PIECE, cols] = low
        high, low = halves(singles)
        left[:COLS, :rows_total] = high
        left[COLS:, :rows_total] = low

    parity, far = lax.rem(x, 2), 1 - x // 2
    strips = (far, 1 - far)
    reach = ((2 * far + parity, 2 * far + 1 - parity), (3 - 2 * far - parity, 2 - 2 * far + parity))

    def fold(sweep):
        def share_of(side, strip):
            cols = pl.ds(pl.multiple_of(side * HALF_COLS + strip * STRIP, STRIP), STRIP)
            return joined(nn(jnp.concatenate([left[...], left[:, rows_total:]], 1), right[:, cols]))

        swaps = []
        for turn, strip in enumerate(strips):
            share = share_of(1 - core, strip)
            for i in range(2):
                part[sweep, turn, i] = share[:, i * LANES : (i + 1) * LANES]
            swap = remote(part.at[sweep, turn], from_core.at[sweep, turn], core_sems.at[sweep, turn], sibling)
            swap.start()
            swaps.append(swap)
        slot = 0
        for turn, strip in enumerate(strips):
            share = share_of(core, strip)
            swaps[turn].wait_recv()
            for i in range(2):
                own[sweep, 2 * strip + i] = share[:, i * LANES : (i + 1) * LANES] + from_core[sweep, turn, i]
            for to_x in reach[turn]:
                for dy in ALONG[: NY if slot < 3 * NY else NY - 1]:
                    to_y = lax.rem(y + dy, NY)
                    remote(
                        own.at[sweep, to_x, pl.ds(to_y * PIECE, PIECE)], from_plane.at[sweep, slot],
                        plane_sems.at[sweep], place(to_x, to_y, z, core),
                    ).start()
                    slot += 1
    def wait_send(ref, sems):
        remote(ref, ref, sems, sibling).wait_send()

    def wait_dipoles():
        same.wait_send()
        mirrored.wait_send()

    def wait_swaps(sweep):
        for turn in range(2):
            wait_send(from_core.at[sweep, turn], core_sems.at[sweep, turn])

    def collect(sweep):
        slots = from_plane.at[sweep]
        remote(slots, slots, plane_sems.at[sweep], sibling).wait_recv()
        total = own[sweep, x, pl.ds(y * PIECE, PIECE), :]
        for i in range(len(plane)):
            total = total + from_plane[sweep, i]
        columns[sweep, z] = total
        for device in column:
            remote(columns.at[sweep, z], columns.at[sweep, z], column_sems.at[sweep], device).start()
        seven = columns.at[sweep, pl.ds(0, NZ - 1)]
        remote(seven, seven, column_sems.at[sweep], sibling).wait_recv()
        total = columns[sweep, 0]
        for i in range(1, NZ):
            total = total + columns[sweep, i]
        return total

    def line_of(squares, group):
        summed = jnp.broadcast_to(jnp.sum(squares, axis=1, keepdims=True), (SUB, LANES))
        return jnp.sum(jnp.where(lane == sublane + group * SUB, summed, 0.0), axis=0, keepdims=True)

    def rms_of(line):
        return jnp.sqrt(line / (2 * BLOCKS * LANES) + 1e-06)[:, : GROUPS * SUB]

    same.wait_recv()
    start_half(z_hi)
    doubles_0, singles_0 = expand(z_hi)
    mirrored.wait_recv()
    start_half(1 - z_hi)
    doubles_1, singles_1 = expand(1 - z_hi)
    finish(doubles_0 + doubles_1, singles_0 + singles_1)
    fold(0)
    for g in range(GROUPS):
        rows, re_rows, im_rows = pl.ds(g * SUB, SUB), pl.ds(g * PIECE, SUB), pl.ds(g * PIECE + SUB, SUB)
        for b in range(BLOCKS):
            re, im, lev = resp[0, b, re_rows, :], resp[0, b, im_rows, :], level[b, rows, :]
            base[b, re_rows, :] = rhs[b, rows, :] - (lev * re + DAMP * im)
            base[b, im_rows, :] = -(lev * im - DAMP * re)
    total = collect(0)
    block = applied.at[core * HALF + x, pl.ds(y * PIECE, PIECE)]
    applied[core * HALF + x, pl.ds(y * PIECE, PIECE), :] = total
    for device in plane:
        remote(block, block, gather_sems, device).start()
    slots = from_plane.at[0]
    remote(slots, slots, gather_sems, sibling).wait_recv()
    mine = applied.at[pl.ds(core * HALF, HALF)]
    share = remote(mine, mine, share_sem, sibling)
    share.start()
    next_half(core)
    doubles_0, singles_0 = expand(core)
    share.wait_recv()
    next_half(1 - core)
    doubles_1, singles_1 = expand(1 - core)
    finish(doubles_0 + doubles_1, singles_0 + singles_1)
    fold(1)
    line = jnp.zeros((1, LANES), F32)
    for g in range(GROUPS):
        squares = jnp.zeros((SUB, LANES), F32)
        for b in range(BLOCKS):
            res_re, res_im = res[b, pl.ds(g * PIECE, SUB), :], res[b, pl.ds(g * PIECE + SUB, SUB), :]
            squares = squares + (res_re * res_re + res_im * res_im)
        line = line + line_of(squares, g)
    rms_ref[0:1, :] = rms_of(line)
    mine = core * HALF + x
    rows, re_rows = pl.ds(y * SUB, SUB), pl.ds(y * PIECE, SUB)
    im_rows = pl.ds(y * PIECE + SUB, SUB)
    re, im, lev = resp[1, mine, re_rows, :], resp[1, mine, im_rows, :], level[mine, rows, :]
    base_re = rhs[mine, rows, :] - (lev * re + DAMP * im)
    base_im = -(lev * im - DAMP * re)
    total = collect(1)
    res_re, res_im = base_re - total[:SUB], base_im - total[SUB:]
    line = line_of(res_re * res_re + res_im * res_im, y)
    lines[mine * GROUPS + y] = line
    line_out[...] = line
    for device in everyone:
        remote(line_out, lines.at[mine * GROUPS + y], line_sems, device).start()
    p_re, p_im = pre_re[mine, rows, :], pre_im[mine, rows, :]
    final[core, 0, rows, :] = re + (res_re * p_re - res_im * p_im)
    final[core, 1, rows, :] = im + (res_im * p_re + res_re * p_im)
    block = final.at[core, :, rows]
    near = [place(x, lax.rem(y + d, NY), z, c) for d in ALONG[:-1] for c in (1 - core, core)]
    for device in near + [sibling]:
        remote(block, block, final_sems, device).start()
    seven = columns.at[1, pl.ds(0, NZ - 1)]
    remote(seven, seven, final_sems, sibling).wait_recv()
    out_ref[...] = final[z_hi]
    most = lines.at[pl.ds(0, BLOCKS * GROUPS - 1)]
    remote(most, most, line_sems, sibling).wait_recv()
    rms_ref[1:2, :] = rms_of(jnp.sum(lines[...], axis=0))
    wait_send(most, line_sems)
    wait_send(seven, final_sems)

    wait_dipoles()
    share.wait_send()
    wait_send(from_plane.at[0], gather_sems)
    for sweep in range(2):
        wait_swaps(sweep)
        wait_send(from_plane.at[sweep], plane_sems.at[sweep])
        wait_send(columns.at[sweep, pl.ds(0, NZ - 1)], column_sems.at[sweep])


def tail(response_in, rms_in, response_out, rms_out):
    response_out[...] = response_in[...]
    rms_out[...] = rms_in[...]


def per_device(
    amplitudes, integral_slab, coupling, pair_of_block, pair_shift, virt_energy,
    core_energy, core_index, frequency, dipole,
):
    rows, virt_total = amplitudes.shape
    k_total = GROUPS * SUB
    whole, wide_whole = (BLOCKS, k_total, LANES), (BLOCKS, COLS, LANES)
    vmem = pl.BlockSpec(memory_space=pltpu.VMEM)
    anywhere = pl.BlockSpec(memory_space=pl.ANY)
    dma = pltpu.SemaphoreType.DMA
    shapes = (
        jax.ShapeDtypeStruct((2, k_total, LANES), F32),
        jax.ShapeDtypeStruct((2, k_total), F32),
    )
    response, rms = pl.pallas_call(
        kernel,
        name="response",
        out_shape=tuple(pltpu.VMEM(shape.shape, shape.dtype) for shape in shapes),
        in_specs=[anywhere] * 10,
        out_specs=(vmem, vmem),
        scratch_shapes=[
            pltpu.SMEM(pair_of_block.shape, jnp.int32),
            pltpu.SMEM(pair_shift.shape, F32),
            pltpu.SMEM(core_energy.shape, F32),
            pltpu.SMEM(core_index.shape, jnp.int32),
            pltpu.SMEM(frequency.shape, F32),
            pltpu.VMEM((BLOCKS, LANES), F32),
            pltpu.VMEM(dipole.shape, F32),
            pltpu.VMEM((rows, virt_total), BF16),
            pltpu.VMEM((virt_total, virt_total), F32),
            pltpu.VMEM((virt_total, rows), BF16),
            pltpu.VMEM((rows + 2 * virt_total, virt_total), BF16),
            pltpu.VMEM((2 * virt_total, virt_total), BF16),
            pltpu.VMEM((2, LANES), F32),
            pltpu.VMEM((BLOCKS, 2, LANES), F32),
            pltpu.VMEM(whole, F32),
            pltpu.VMEM(whole, F32),
            pltpu.VMEM(whole, F32),
            pltpu.VMEM(whole, F32),
            pltpu.VMEM(whole, F32),
            pltpu.VMEM(whole, F32),
            pltpu.VMEM((2,) + wide_whole, F32),
            pltpu.VMEM(wide_whole, F32),
            pltpu.VMEM(wide_whole, F32),
            pltpu.VMEM((2, 2 * COLS, HALF_COLS), BF16),
            pltpu.VMEM((2 * COLS, rows + virt_total), BF16),
            pltpu.VMEM((2, 2, 2, COLS, LANES), F32),
            pltpu.VMEM((2, 2, 2, COLS, LANES), F32),
            pltpu.VMEM((2, HALF, COLS, LANES), F32),
            pltpu.VMEM((2, len(PLANE), PIECE, LANES), F32),
            pltpu.VMEM((2, NZ, PIECE, LANES), F32),
            pltpu.VMEM(wide_whole, F32),
            pltpu.VMEM((2, 2, k_total, LANES), F32),
            pltpu.VMEM((BLOCKS * GROUPS, 1, LANES), F32),
            pltpu.VMEM((1, LANES), F32),
            dma((7,)),
            dma((2 + BLOCKS,)),
            dma((2, 2)),
            dma((2, 2, 2)),
            dma((2, 2)),
            dma((2, 2)),
            dma((2,)),
            dma((2,)),
            dma((2,)),
            dma((2,)),
        ],
        compiler_params=pltpu.CompilerParams(
            collective_id=0, has_side_effects=True, vmem_limit_bytes=56 * 2**20
        ),
    )(
        pair_of_block, pair_shift, core_energy, core_index, frequency,
        virt_energy.reshape(BLOCKS, LANES), dipole, amplitudes, integral_slab, coupling,
    )
    return pl.pallas_call(
        tail, name="tail", out_shape=shapes, in_specs=[vmem, vmem], out_specs=(vmem, vmem)
    )(*(pltpu.with_memory_space_constraint(value, pltpu.VMEM) for value in (response, rms)))


def solution(mesh):
    rows = P(("wide", "narrow"), None)
    placed = (rows, rows, P(("wide", "narrow"), None, None)) + (P(),) * 6 + (P(None, "narrow"),)
    return jax.shard_map(
        per_device,
        mesh=mesh,
        in_specs=placed,
        out_specs=(P(None, None, "narrow"), P()),
        check_vma=False,
    )
```

```python
import jax
import jax.numpy as jnp
from jax import lax
from jax.experimental import pallas as pl
from jax.experimental.pallas import tpu as pltpu
from jax.sharding import PartitionSpec as P

DAMP = 0.5
MESH = pl.DeviceIdType.MESH
F32 = jnp.float32
BF16 = jnp.bfloat16

NX, NY, NZ, NZLO = 4, 4, 8, 4


def ring(step, size):
    return min(step, size - step)


PLANE = tuple(
    sorted(
        tuple((dx, dy) for dx in range(NX) for dy in range(NY))[1:],
        key=lambda d: -ring(d[0], NX) - ring(d[1], NY),
    )
)
COLUMN = tuple(sorted(range(1, NZ), key=lambda d: -ring(d, NZ)))
ALONG = (2, 1, 3, 0)
GROUPS, SUB, LANES, BLOCKS = 4, 8, 128, 8
PIECE = 2 * SUB
COLS = GROUPS * PIECE
HALF = BLOCKS // 2
HALF_COLS = HALF * LANES
STRIP = 256


def place(x, y, z, core):
    return {
        "wide": (y * NZLO + lax.rem(z, NZLO)) * 2 + core,
        "narrow": x * 2 + z // NZLO,
    }


def spot(block):
    return (block % 2) * HALF + block // 2


def nn(left, right):
    return lax.dot_general(left, right, (((1,), (0,)), ((), ())), preferred_element_type=F32)


def halves(value):
    high = value.astype(BF16)
    low = (value - high.astype(F32)).astype(BF16)
    return high, low


def remote(src, dst, sems, device):
    return pltpu.make_async_remote_copy(
        src_ref=src, dst_ref=dst, send_sem=sems.at[0], recv_sem=sems.at[1],
        device_id=device, device_id_type=MESH,
    )


def kernel(
    pair_of_block_hbm, pair_shift_hbm, core_energy_hbm, core_index_hbm, frequency_hbm,
    virt_hbm, dipole_hbm, amp_hbm, slab_hbm, coup_hbm,
    out_ref, rms_ref,
    pair_of_block, pair_shift, core_energy, core_index, frequency, virt, dipole,
    slab, coup, slab_t, right, coup_t,
    picked, dip, rhs, pre_re, pre_im, level, den_re, den_im, resp, base, res,
    pieces, left,
    part, from_core, own, from_plane, columns, applied, final, lines, line_out,
    small_sem, hbm_sem, dip_sems, core_sems, plane_sems, column_sems, gather_sems, share_sem,
    final_sems, line_sems,
):
    wide, narrow = lax.axis_index("wide"), lax.axis_index("narrow")
    x, y, core = narrow // 2, wide // (2 * NZLO), lax.rem(wide, 2)
    z_hi, z_lo = lax.rem(narrow, 2), lax.rem(wide // 2, NZLO)
    z = z_hi * NZLO + z_lo
    rows_total, virt_total = slab.shape
    mirror = (1 - z_hi) * NZLO + lax.rem(z_lo + 2, NZLO)

    loads = [
        pltpu.make_async_copy(coup_hbm.at[0], coup, hbm_sem.at[0]),
        pltpu.make_async_copy(slab_hbm, slab, hbm_sem.at[1]),
        pltpu.make_async_copy(amp_hbm, right.at[pl.ds(0, rows_total)], hbm_sem.at[2]),
    ]
    sibling = place(x, y, z, 1 - core)
    plane_xy = [(lax.rem(x + dx, NX), lax.rem(y + dy, NY)) for dx, dy in PLANE]
    plane = [place(to_x, to_y, z, core) for to_x, to_y in plane_xy]
    across = [place(to_x, to_y, z, 1 - core) for to_x, to_y in plane_xy]
    everyone = [device for pair in zip(across, plane) for device in pair] + [sibling]
    column = [place(x, y, lax.rem(z + d, NZ), core) for d in COLUMN]
    mirrors = [place(lax.rem(x + d, NX), y, mirror, core) for d in ALONG]
    beside = [place(lax.rem(x + d, NX), y, z, core) for d in ALONG[:-1]]

    barrier = pltpu.get_barrier_semaphore()
    greeted = mirrors[:-1] + column
    for device in greeted:
        pl.semaphore_signal(barrier, inc=1, device_id=device, device_id_type=MESH)

    small = [
        pltpu.make_async_copy(src, dst, small_sem.at[i])
        for i, (src, dst) in enumerate((
            (core_index_hbm, core_index), (dipole_hbm, dipole), (virt_hbm, virt),
            (core_energy_hbm, core_energy), (frequency_hbm, frequency),
            (pair_of_block_hbm, pair_of_block), (pair_shift_hbm, pair_shift),
        ))
    ]
    for load in small + loads[:2]:
        load.start()
    for device in everyone:
        pl.semaphore_signal(barrier, inc=1, device_id=device, device_id_type=MESH)

    for load in small:
        load.wait()
    for c in range(2):
        picked[c : c + 1, :] = dipole[pl.ds(core_index[c], 1), :]

    sublane = lax.broadcasted_iota(jnp.int32, (SUB, LANES), 0)
    lane = lax.broadcasted_iota(jnp.int32, (SUB, LANES), 1)
    offset = pair_shift[pair_of_block[wide * 8 + narrow]]
    for g in range(GROUPS):
        energy = core_energy[core_index[g // 2]]
        shift = jnp.zeros((SUB, LANES), F32)
        for j in range(SUB):
            value = frequency[(g % 2) * SUB + j] + energy
            shift = jnp.where(sublane == j, value, shift)
        rows = pl.ds(g * SUB, SUB)
        for b in range(BLOCKS):
            energies = jnp.broadcast_to(virt[b : b + 1, :], (SUB, LANES))
            lev = energies - shift
            inverse = 1.0 / (lev * lev + DAMP * DAMP)
            level[spot(b), rows, :] = lev
            pre_re[spot(b), rows, :] = lev * inverse
            pre_im[spot(b), rows, :] = DAMP * inverse
            den = (shift - offset) - energies
            inverse = 1.0 / (den * den + DAMP * DAMP)
            den_re[b, rows, :] = den * inverse
            den_im[b, rows, :] = DAMP * inverse

    pl.semaphore_wait(barrier, len(greeted) + len(everyone))
    for device in mirrors:
        remote(picked, dip.at[narrow], dip_sems.at[1], device).start()
    for device in beside:
        remote(picked, dip.at[narrow], dip_sems.at[0], device).start()
    loads[2].start()
    dip[narrow] = picked[...]

    loads[0].wait()

    def split_rows(i, _):
        rows = pl.ds(pl.multiple_of(i * STRIP, STRIP), STRIP)
        strip = coup[rows, :]
        high, low = halves(strip)
        start = rows_total + i * STRIP
        right[pl.ds(pl.multiple_of(start, STRIP), STRIP), :] = high
        right[pl.ds(pl.multiple_of(start + virt_total, STRIP), STRIP), :] = low
        high, low = high.T, low.T
        for b in range(BLOCKS):
            cols, there = slice(b * LANES, (b + 1) * LANES), (b % 2) * 2 * HALF_COLS + (b // 2) * LANES
            coup_t[there : there + LANES, rows] = high[cols]
            coup_t[there + HALF_COLS : there + HALF_COLS + LANES, rows] = low[cols]
        return 0

    lax.fori_loop(0, coup.shape[0] // STRIP, split_rows, 0)
    loads[1].wait()

    def turn_rows(i, _):
        rows = pl.ds(pl.multiple_of(i * STRIP, STRIP), STRIP)
        turned = slab[rows, :].T
        for b in range(BLOCKS):
            slab_t[spot(b) * LANES : (spot(b) + 1) * LANES, rows] = turned[b * LANES : (b + 1) * LANES]
        return 0

    lax.fori_loop(0, slab.shape[0] // STRIP, turn_rows, 0)
    same = remote(dip.at[pl.ds(0, NX - 1)], dip.at[pl.ds(0, NX - 1)], dip_sems.at[0], sibling)
    mirrored = remote(dip.at[pl.ds(0, NX)], dip.at[pl.ds(0, NX)], dip_sems.at[1], sibling)

    def start_half(half):
        for g in range(GROUPS):
            rows, re_rows, im_rows = pl.ds(g * SUB, SUB), pl.ds(g * PIECE, SUB), pl.ds(g * PIECE + SUB, SUB)
            for j in range(HALF):
                b, cols = half * HALF + j, slice(j * LANES, (j + 1) * LANES)
                source = jnp.broadcast_to(dip[2 * j + half, g // 2 : g // 2 + 1, :], (SUB, LANES))
                rhs[b, rows, :] = source
                re, im = source * pre_re[b, rows, :], source * pre_im[b, rows, :]
                resp[0, b, re_rows, :] = re
                resp[0, b, im_rows, :] = im
                high, low = halves(jnp.concatenate([re, im], 0))
                pieces[half, g * PIECE : (g + 1) * PIECE, cols] = high
                pieces[half, COLS + g * PIECE : COLS + (g + 1) * PIECE, cols] = low

    def next_half(half):
        for g in range(GROUPS):
            rows, re_rows, im_rows = pl.ds(g * SUB, SUB), pl.ds(g * PIECE, SUB), pl.ds(g * PIECE + SUB, SUB)
            for j in range(HALF):
                b, cols = half * HALF + j, slice(j * LANES, (j + 1) * LANES)
                res_re = base[b, re_rows, :] - applied[b, re_rows, :]
                res_im = base[b, im_rows, :] - applied[b, im_rows, :]
                res[b, re_rows, :] = res_re
                res[b, im_rows, :] = res_im
                p_re, p_im = pre_re[b, rows, :], pre_im[b, rows, :]
                re = resp[0, b, re_rows, :] + (res_re * p_re - res_im * p_im)
                im = resp[0, b, im_rows, :] + (res_im * p_re + res_re * p_im)
                resp[1, b, re_rows, :] = re
                resp[1, b, im_rows, :] = im
                high, low = halves(jnp.concatenate([re, im], 0))
                pieces[half, g * PIECE : (g + 1) * PIECE, cols] = high
                pieces[half, COLS + g * PIECE : COLS + (g + 1) * PIECE, cols] = low

    def joined(both):
        return both[:COLS] + both[COLS:]

    def expand(half):
        piece = pieces[half]
        rows = pl.ds(pl.multiple_of(half * 2 * HALF_COLS, HALF_COLS), 2 * HALF_COLS)
        doubles = nn(jnp.concatenate([piece, piece], 1), coup_t[rows, :])
        rows = pl.ds(pl.multiple_of(half * HALF_COLS, HALF_COLS), HALF_COLS)
        return joined(doubles), joined(nn(piece, slab_t[rows, :]))

    def finish(doubles, singles):
        for g in range(GROUPS):
            rows = pl.ds(g * SUB, SUB)
            for b in range(BLOCKS):
                cols = slice(b * LANES, (b + 1) * LANES)
                real = doubles[g * PIECE : g * PIECE + SUB, cols]
                imag = doubles[g * PIECE + SUB : (g + 1) * PIECE, cols]
                q_re, q_im = den_re[b, rows, :], den_im[b, rows, :]
                quotient = jnp.concatenate([real * q_re + imag * q_im, imag * q_re - real * q_im], 0)
                high, low = halves(quotient)
                cols = slice(rows_total + b * LANES, rows_total + (b + 1) * LANES)
                left[g * PIECE : (g + 1) * PIECE, cols] = high
                left[COLS + g * PIECE : COLS + (g + 1) * PIECE, cols] = low
        high, low = halves(singles)
        left[:COLS, :rows_total] = high
        left[COLS:, :rows_total] = low

    parity, far = lax.rem(x, 2), 1 - x // 2
    strips = (far, 1 - far)
    reach = ((2 * far + parity, 2 * far + 1 - parity), (3 - 2 * far - parity, 2 - 2 * far + parity))

    def fold(sweep):
        def share_of(side, strip):
            columns_of = [
                right[:, pl.ds(pl.multiple_of((4 * strip + 2 * i + side) * LANES, LANES), LANES)] for i in range(2)
            ]
            rows_of = jnp.concatenate([left[...], left[:, rows_total:]], 1)
            return joined(nn(rows_of, jnp.concatenate(columns_of, 1)))

        swaps = []
        for turn, strip in enumerate(strips):
            share = share_of(1 - core, strip)
            for i in range(2):
                part[sweep, turn, i] = share[:, i * LANES : (i + 1) * LANES]
            swap = remote(part.at[sweep, turn], from_core.at[sweep, turn], core_sems.at[sweep, turn], sibling)
            swap.start()
            swaps.append(swap)
        slot = 0
        for turn, strip in enumerate(strips):
            share = share_of(core, strip)
            swaps[turn].wait_recv()
            for i in range(2):
                own[sweep, 2 * strip + i] = share[:, i * LANES : (i + 1) * LANES] + from_core[sweep, turn, i]
            for to_x in reach[turn]:
                for dy in ALONG[: NY if slot < 3 * NY else NY - 1]:
                    to_y = lax.rem(y + dy, NY)
                    remote(
                        own.at[sweep, to_x, pl.ds(to_y * PIECE, PIECE)], from_plane.at[sweep, slot],
                        plane_sems.at[sweep], place(to_x, to_y, z, core),
                    ).start()
                    slot += 1
    def wait_send(ref, sems):
        remote(ref, ref, sems, sibling).wait_send()

    def wait_dipoles():
        same.wait_send()
        mirrored.wait_send()

    def wait_swaps(sweep):
        for turn in range(2):
            wait_send(from_core.at[sweep, turn], core_sems.at[sweep, turn])

    def collect(sweep):
        slots = from_plane.at[sweep]
        remote(slots, slots, plane_sems.at[sweep], sibling).wait_recv()
        total = own[sweep, x, pl.ds(y * PIECE, PIECE), :]
        for i in range(len(plane)):
            total = total + from_plane[sweep, i]
        columns[sweep, z] = total
        for device in column:
            remote(columns.at[sweep, z], columns.at[sweep, z], column_sems.at[sweep], device).start()
        seven = columns.at[sweep, pl.ds(0, NZ - 1)]
        remote(seven, seven, column_sems.at[sweep], sibling).wait_recv()
        total = columns[sweep, 0]
        for i in range(1, NZ):
            total = total + columns[sweep, i]
        return total

    def line_of(squares, group):
        summed = jnp.broadcast_to(jnp.sum(squares, axis=1, keepdims=True), (SUB, LANES))
        return jnp.sum(jnp.where(lane == sublane + group * SUB, summed, 0.0), axis=0, keepdims=True)

    def rms_of(line):
        return jnp.sqrt(line / (2 * BLOCKS * LANES) + 1e-06)[:, : GROUPS * SUB]

    same.wait_recv()
    start_half(z_hi)
    doubles_0, singles_0 = expand(z_hi)
    mirrored.wait_recv()
    start_half(1 - z_hi)
    doubles_1, singles_1 = expand(1 - z_hi)
    finish(doubles_0 + doubles_1, singles_0 + singles_1)
    loads[2].wait()
    fold(0)
    for g in range(GROUPS):
        rows, re_rows, im_rows = pl.ds(g * SUB, SUB), pl.ds(g * PIECE, SUB), pl.ds(g * PIECE + SUB, SUB)
        for b in range(BLOCKS):
            re, im, lev = resp[0, b, re_rows, :], resp[0, b, im_rows, :], level[b, rows, :]
            base[b, re_rows, :] = rhs[b, rows, :] - (lev * re + DAMP * im)
            base[b, im_rows, :] = -(lev * im - DAMP * re)
    total = collect(0)
    block = applied.at[core * HALF + x, pl.ds(y * PIECE, PIECE)]
    applied[core * HALF + x, pl.ds(y * PIECE, PIECE), :] = total
    for device in plane:
        remote(block, block, gather_sems, device).start()
    slots = from_plane.at[0]
    remote(slots, slots, gather_sems, sibling).wait_recv()
    mine = applied.at[pl.ds(core * HALF, HALF)]
    share = remote(mine, mine, share_sem, sibling)
    share.start()
    next_half(core)
    doubles_0, singles_0 = expand(core)
    share.wait_recv()
    next_half(1 - core)
    doubles_1, singles_1 = expand(1 - core)
    finish(doubles_0 + doubles_1, singles_0 + singles_1)
    fold(1)
    line = jnp.zeros((1, LANES), F32)
    for g in range(GROUPS):
        squares = jnp.zeros((SUB, LANES), F32)
        for b in range(BLOCKS):
            res_re, res_im = res[b, pl.ds(g * PIECE, SUB), :], res[b, pl.ds(g * PIECE + SUB, SUB), :]
            squares = squares + (res_re * res_re + res_im * res_im)
        line = line + line_of(squares, g)
    rms_ref[0:1, :] = rms_of(line)
    mine = core * HALF + x
    rows, re_rows = pl.ds(y * SUB, SUB), pl.ds(y * PIECE, SUB)
    im_rows = pl.ds(y * PIECE + SUB, SUB)
    re, im, lev = resp[1, mine, re_rows, :], resp[1, mine, im_rows, :], level[mine, rows, :]
    base_re = rhs[mine, rows, :] - (lev * re + DAMP * im)
    base_im = -(lev * im - DAMP * re)
    total = collect(1)
    res_re, res_im = base_re - total[:SUB], base_im - total[SUB:]
    line = line_of(res_re * res_re + res_im * res_im, y)
    lines[mine * GROUPS + y] = line
    line_out[...] = line
    for device in everyone:
        remote(line_out, lines.at[mine * GROUPS + y], line_sems, device).start()
    p_re, p_im = pre_re[mine, rows, :], pre_im[mine, rows, :]
    final[core, 0, rows, :] = re + (res_re * p_re - res_im * p_im)
    final[core, 1, rows, :] = im + (res_im * p_re + res_re * p_im)
    block = final.at[core, :, rows]
    near = [place(x, lax.rem(y + d, NY), z, c) for d in ALONG[:-1] for c in (1 - core, core)]
    for device in near + [sibling]:
        remote(block, block, final_sems, device).start()
    seven = columns.at[1, pl.ds(0, NZ - 1)]
    remote(seven, seven, final_sems, sibling).wait_recv()
    out_ref[...] = final[z_hi]
    most = lines.at[pl.ds(0, BLOCKS * GROUPS - 1)]
    remote(most, most, line_sems, sibling).wait_recv()
    rms_ref[1:2, :] = rms_of(jnp.sum(lines[...], axis=0))
    wait_send(most, line_sems)
    wait_send(seven, final_sems)

    wait_dipoles()
    share.wait_send()
    wait_send(from_plane.at[0], gather_sems)
    for sweep in range(2):
        wait_swaps(sweep)
        wait_send(from_plane.at[sweep], plane_sems.at[sweep])
        wait_send(columns.at[sweep, pl.ds(0, NZ - 1)], column_sems.at[sweep])


def tail(response_in, rms_in, response_out, rms_out):
    response_out[...] = response_in[...]
    rms_out[...] = rms_in[...]


def per_device(
    amplitudes, integral_slab, coupling, pair_of_block, pair_shift, virt_energy,
    core_energy, core_index, frequency, dipole,
):
    rows, virt_total = amplitudes.shape
    k_total = GROUPS * SUB
    whole, wide_whole = (BLOCKS, k_total, LANES), (BLOCKS, COLS, LANES)
    vmem = pl.BlockSpec(memory_space=pltpu.VMEM)
    anywhere = pl.BlockSpec(memory_space=pl.ANY)
    dma = pltpu.SemaphoreType.DMA
    shapes = (
        jax.ShapeDtypeStruct((2, k_total, LANES), F32),
        jax.ShapeDtypeStruct((2, k_total), F32),
    )
    response, rms = pl.pallas_call(
        kernel,
        name="response",
        out_shape=tuple(pltpu.VMEM(shape.shape, shape.dtype) for shape in shapes),
        in_specs=[anywhere] * 10,
        out_specs=(vmem, vmem),
        scratch_shapes=[
            pltpu.SMEM(pair_of_block.shape, jnp.int32),
            pltpu.SMEM(pair_shift.shape, F32),
            pltpu.SMEM(core_energy.shape, F32),
            pltpu.SMEM(core_index.shape, jnp.int32),
            pltpu.SMEM(frequency.shape, F32),
            pltpu.VMEM((BLOCKS, LANES), F32),
            pltpu.VMEM(dipole.shape, F32),
            pltpu.VMEM((rows, virt_total), BF16),
            pltpu.VMEM((virt_total, virt_total), F32),
            pltpu.VMEM((virt_total, rows), BF16),
            pltpu.VMEM((rows + 2 * virt_total, virt_total), BF16),
            pltpu.VMEM((2 * virt_total, virt_total), BF16),
            pltpu.VMEM((2, LANES), F32),
            pltpu.VMEM((BLOCKS, 2, LANES), F32),
            pltpu.VMEM(whole, F32),
            pltpu.VMEM(whole, F32),
            pltpu.VMEM(whole, F32),
            pltpu.VMEM(whole, F32),
            pltpu.VMEM(whole, F32),
            pltpu.VMEM(whole, F32),
            pltpu.VMEM((2,) + wide_whole, F32),
            pltpu.VMEM(wide_whole, F32),
            pltpu.VMEM(wide_whole, F32),
            pltpu.VMEM((2, 2 * COLS, HALF_COLS), BF16),
            pltpu.VMEM((2 * COLS, rows + virt_total), BF16),
            pltpu.VMEM((2, 2, 2, COLS, LANES), F32),
            pltpu.VMEM((2, 2, 2, COLS, LANES), F32),
            pltpu.VMEM((2, HALF, COLS, LANES), F32),
            pltpu.VMEM((2, len(PLANE), PIECE, LANES), F32),
            pltpu.VMEM((2, NZ, PIECE, LANES), F32),
            pltpu.VMEM(wide_whole, F32),
            pltpu.VMEM((2, 2, k_total, LANES), F32),
            pltpu.VMEM((BLOCKS * GROUPS, 1, LANES), F32),
            pltpu.VMEM((1, LANES), F32),
            dma((7,)),
            dma((3,)),
            dma((2, 2)),
            dma((2, 2, 2)),
            dma((2, 2)),
            dma((2, 2)),
            dma((2,)),
            dma((2,)),
            dma((2,)),
            dma((2,)),
        ],
        compiler_params=pltpu.CompilerParams(
            collective_id=0, has_side_effects=True, vmem_limit_bytes=56 * 2**20
        ),
    )(
        pair_of_block, pair_shift, core_energy, core_index, frequency,
        virt_energy.reshape(BLOCKS, LANES), dipole, amplitudes, integral_slab, coupling,
    )
    return pl.pallas_call(
        tail, name="tail", out_shape=shapes, in_specs=[vmem, vmem], out_specs=(vmem, vmem)
    )(*(pltpu.with_memory_space_constraint(value, pltpu.VMEM) for value in (response, rms)))


def solution(mesh):
    rows = P(("wide", "narrow"), None)
    placed = (rows, rows, P(("wide", "narrow"), None, None)) + (P(),) * 6 + (P(None, "narrow"),)
    return jax.shard_map(
        per_device,
        mesh=mesh,
        in_specs=placed,
        out_specs=(P(None, None, "narrow"), P()),
        check_vma=False,
    )
```

```python
import jax
import jax.numpy as jnp
from jax import lax
from jax.experimental import pallas as pl
from jax.experimental.pallas import tpu as pltpu
from jax.sharding import PartitionSpec as P

DAMP = 0.5
MESH = pl.DeviceIdType.MESH
F32 = jnp.float32
BF16 = jnp.bfloat16

NX, NY, NZ, NZLO = 4, 4, 8, 4


def ring(step, size):
    return min(step, size - step)


PLANE = tuple(
    sorted(
        tuple((dx, dy) for dx in range(NX) for dy in range(NY))[1:],
        key=lambda d: -ring(d[0], NX) - ring(d[1], NY),
    )
)
COLUMN = tuple(sorted(range(1, NZ), key=lambda d: -ring(d, NZ)))
ALONG = (2, 1, 3, 0)
GROUPS, SUB, LANES, BLOCKS = 4, 8, 128, 8
PIECE = 2 * SUB
COLS = GROUPS * PIECE
HALF = BLOCKS // 2
HALF_COLS = HALF * LANES
STRIP = 256


def place(x, y, z, core):
    return {
        "wide": (y * NZLO + lax.rem(z, NZLO)) * 2 + core,
        "narrow": x * 2 + z // NZLO,
    }


def spot(block):
    return (block % 2) * HALF + block // 2


def nn(left, right):
    return lax.dot_general(left, right, (((1,), (0,)), ((), ())), preferred_element_type=F32)


def halves(value):
    high = value.astype(BF16)
    low = (value - high.astype(F32)).astype(BF16)
    return high, low


def remote(src, dst, sems, device):
    return pltpu.make_async_remote_copy(
        src_ref=src, dst_ref=dst, send_sem=sems.at[0], recv_sem=sems.at[1],
        device_id=device, device_id_type=MESH,
    )


def kernel(
    pair_of_block_hbm, pair_shift_hbm, core_energy_hbm, core_index_hbm, frequency_hbm,
    virt_hbm, dipole_hbm, amp_hbm, slab_hbm, coup_hbm,
    out_ref, rms_ref,
    pair_of_block, pair_shift, core_energy, core_index, frequency, virt, dipole,
    slab, coup, slab_t, right, coup_t,
    picked, dip, rhs, pre_re, pre_im, level, den_re, den_im, resp, base, res,
    pieces, left,
    part, from_core, own, from_plane, columns, applied, final, lines, line_out,
    small_sem, hbm_sem, dip_sems, core_sems, plane_sems, column_sems, gather_sems, share_sem,
    final_sems, line_sems,
):
    wide, narrow = lax.axis_index("wide"), lax.axis_index("narrow")
    x, y, core = narrow // 2, wide // (2 * NZLO), lax.rem(wide, 2)
    z_hi, z_lo = lax.rem(narrow, 2), lax.rem(wide // 2, NZLO)
    z = z_hi * NZLO + z_lo
    rows_total, virt_total = slab.shape
    mirror = (1 - z_hi) * NZLO + lax.rem(z_lo + 2, NZLO)

    loads = [
        pltpu.make_async_copy(coup_hbm.at[0], coup, hbm_sem.at[0]),
        pltpu.make_async_copy(slab_hbm, slab, hbm_sem.at[1]),
        pltpu.make_async_copy(amp_hbm, right.at[pl.ds(0, rows_total)], hbm_sem.at[2]),
    ]
    sibling = place(x, y, z, 1 - core)
    plane_xy = [(lax.rem(x + dx, NX), lax.rem(y + dy, NY)) for dx, dy in PLANE]
    plane = [place(to_x, to_y, z, core) for to_x, to_y in plane_xy]
    across = [place(to_x, to_y, z, 1 - core) for to_x, to_y in plane_xy]
    everyone = [device for pair in zip(across, plane) for device in pair] + [sibling]
    column = [place(x, y, lax.rem(z + d, NZ), core) for d in COLUMN]
    mirrors = [place(lax.rem(x + d, NX), y, mirror, core) for d in ALONG]
    beside = [place(lax.rem(x + d, NX), y, z, core) for d in ALONG[:-1]]

    barrier = pltpu.get_barrier_semaphore()
    greeted = mirrors[:-1] + column
    for device in greeted:
        pl.semaphore_signal(barrier, inc=1, device_id=device, device_id_type=MESH)

    small = [
        pltpu.make_async_copy(src, dst, small_sem.at[i])
        for i, (src, dst) in enumerate((
            (core_index_hbm, core_index), (dipole_hbm, dipole), (virt_hbm, virt),
            (core_energy_hbm, core_energy), (frequency_hbm, frequency),
            (pair_of_block_hbm, pair_of_block), (pair_shift_hbm, pair_shift),
        ))
    ]
    for load in small + loads[:2]:
        load.start()
    for device in everyone:
        pl.semaphore_signal(barrier, inc=1, device_id=device, device_id_type=MESH)

    for load in small:
        load.wait()
    for c in range(2):
        picked[c : c + 1, :] = dipole[pl.ds(core_index[c], 1), :]

    sublane = lax.broadcasted_iota(jnp.int32, (SUB, LANES), 0)
    lane = lax.broadcasted_iota(jnp.int32, (SUB, LANES), 1)
    offset = pair_shift[pair_of_block[wide * 8 + narrow]]
    for g in range(GROUPS):
        energy = core_energy[core_index[g // 2]]
        shift = jnp.zeros((SUB, LANES), F32)
        for j in range(SUB):
            value = frequency[(g % 2) * SUB + j] + energy
            shift = jnp.where(sublane == j, value, shift)
        rows = pl.ds(g * SUB, SUB)
        for b in range(BLOCKS):
            energies = jnp.broadcast_to(virt[b : b + 1, :], (SUB, LANES))
            lev = energies - shift
            inverse = 1.0 / (lev * lev + DAMP * DAMP)
            level[spot(b), rows, :] = lev
            pre_re[spot(b), rows, :] = lev * inverse
            pre_im[spot(b), rows, :] = DAMP * inverse
            den = (shift - offset) - energies
            inverse = 1.0 / (den * den + DAMP * DAMP)
            den_re[b, rows, :] = den * inverse
            den_im[b, rows, :] = DAMP * inverse

    pl.semaphore_wait(barrier, len(greeted) + len(everyone))
    for device in mirrors:
        remote(picked, dip.at[narrow], dip_sems.at[1], device).start()
    for device in beside:
        remote(picked, dip.at[narrow], dip_sems.at[0], device).start()
    loads[2].start()
    dip[narrow] = picked[...]

    loads[0].wait()

    def split_rows(i, _):
        rows = pl.ds(pl.multiple_of(i * STRIP, STRIP), STRIP)
        strip = coup[rows, :]
        high, low = halves(strip)
        start = rows_total + i * STRIP
        right[pl.ds(pl.multiple_of(start, STRIP), STRIP), :] = high
        right[pl.ds(pl.multiple_of(start + virt_total, STRIP), STRIP), :] = low
        high, low = high.T, low.T
        for b in range(BLOCKS):
            cols, there = slice(b * LANES, (b + 1) * LANES), (b % 2) * 2 * HALF_COLS + (b // 2) * LANES
            coup_t[there : there + LANES, rows] = high[cols]
            coup_t[there + HALF_COLS : there + HALF_COLS + LANES, rows] = low[cols]
        return 0

    lax.fori_loop(0, coup.shape[0] // STRIP, split_rows, 0)
    loads[1].wait()

    def turn_rows(i, _):
        rows = pl.ds(pl.multiple_of(i * STRIP, STRIP), STRIP)
        turned = slab[rows, :].T
        for b in range(BLOCKS):
            slab_t[spot(b) * LANES : (spot(b) + 1) * LANES, rows] = turned[b * LANES : (b + 1) * LANES]
        return 0

    lax.fori_loop(0, slab.shape[0] // STRIP, turn_rows, 0)
    same = remote(dip.at[pl.ds(0, NX - 1)], dip.at[pl.ds(0, NX - 1)], dip_sems.at[0], sibling)
    mirrored = remote(dip.at[pl.ds(0, NX)], dip.at[pl.ds(0, NX)], dip_sems.at[1], sibling)

    def start_half(half):
        for g in range(GROUPS):
            rows, re_rows, im_rows = pl.ds(g * SUB, SUB), pl.ds(g * PIECE, SUB), pl.ds(g * PIECE + SUB, SUB)
            for j in range(HALF):
                b, cols = half * HALF + j, slice(j * LANES, (j + 1) * LANES)
                source = jnp.broadcast_to(dip[2 * j + half, g // 2 : g // 2 + 1, :], (SUB, LANES))
                rhs[b, rows, :] = source
                re, im = source * pre_re[b, rows, :], source * pre_im[b, rows, :]
                resp[0, b, re_rows, :] = re
                resp[0, b, im_rows, :] = im
                high, low = halves(jnp.concatenate([re, im], 0))
                pieces[half, g * PIECE : (g + 1) * PIECE, cols] = high
                pieces[half, COLS + g * PIECE : COLS + (g + 1) * PIECE, cols] = low

    def next_half(half):
        for g in range(GROUPS):
            rows, re_rows, im_rows = pl.ds(g * SUB, SUB), pl.ds(g * PIECE, SUB), pl.ds(g * PIECE + SUB, SUB)
            for j in range(HALF):
                b, cols = half * HALF + j, slice(j * LANES, (j + 1) * LANES)
                res_re = base[b, re_rows, :] - applied[b, re_rows, :]
                res_im = base[b, im_rows, :] - applied[b, im_rows, :]
                res[b, re_rows, :] = res_re
                res[b, im_rows, :] = res_im
                p_re, p_im = pre_re[b, rows, :], pre_im[b, rows, :]
                re = resp[0, b, re_rows, :] + (res_re * p_re - res_im * p_im)
                im = resp[0, b, im_rows, :] + (res_im * p_re + res_re * p_im)
                resp[1, b, re_rows, :] = re
                resp[1, b, im_rows, :] = im
                high, low = halves(jnp.concatenate([re, im], 0))
                pieces[half, g * PIECE : (g + 1) * PIECE, cols] = high
                pieces[half, COLS + g * PIECE : COLS + (g + 1) * PIECE, cols] = low

    def joined(both):
        return both[:COLS] + both[COLS:]

    def expand(half):
        piece = pieces[half]
        rows = pl.ds(pl.multiple_of(half * 2 * HALF_COLS, HALF_COLS), 2 * HALF_COLS)
        doubles = nn(jnp.concatenate([piece, piece], 1), coup_t[rows, :])
        rows = pl.ds(pl.multiple_of(half * HALF_COLS, HALF_COLS), HALF_COLS)
        return joined(doubles), joined(nn(piece, slab_t[rows, :]))

    def finish(doubles, singles):
        for g in range(GROUPS):
            rows = pl.ds(g * SUB, SUB)
            for b in range(BLOCKS):
                cols = slice(b * LANES, (b + 1) * LANES)
                real = doubles[g * PIECE : g * PIECE + SUB, cols]
                imag = doubles[g * PIECE + SUB : (g + 1) * PIECE, cols]
                q_re, q_im = den_re[b, rows, :], den_im[b, rows, :]
                quotient = jnp.concatenate([real * q_re + imag * q_im, imag * q_re - real * q_im], 0)
                high, low = halves(quotient)
                cols = slice(rows_total + b * LANES, rows_total + (b + 1) * LANES)
                left[g * PIECE : (g + 1) * PIECE, cols] = high
                left[COLS + g * PIECE : COLS + (g + 1) * PIECE, cols] = low
        high, low = halves(singles)
        left[:COLS, :rows_total] = high
        left[COLS:, :rows_total] = low

    parity, far = lax.rem(x, 2), 1 - x // 2

    def fold(sweep):
        def share_of(side, strip):
            columns_of = [
                right[:, pl.ds(pl.multiple_of((4 * strip + 2 * i + side) * LANES, LANES), LANES)] for i in range(2)
            ]
            rows_of = jnp.concatenate([left[...], left[:, rows_total:]], 1)
            return joined(nn(rows_of, jnp.concatenate(columns_of, 1)))

        def swap_of(turn):
            return remote(part.at[sweep, turn], from_core.at[sweep, turn], core_sems.at[sweep, turn], sibling)

        def give(turn, _):
            share = share_of(1 - core, lax.rem(far + turn, 2))
            for i in range(2):
                part[sweep, turn, i] = share[:, i * LANES : (i + 1) * LANES]
            swap_of(turn).start()
            return 0

        def keep(turn, _):
            strip = lax.rem(far + turn, 2)
            share = share_of(core, strip)
            swap_of(turn).wait_recv()
            for i in range(2):
                own[sweep, 2 * strip + i] = share[:, i * LANES : (i + 1) * LANES] + from_core[sweep, turn, i]
            for i in range(2):
                to_x = 2 * strip + lax.rem(parity + i + turn, 2)

                def send(at):
                    to_y = lax.rem(y + ALONG[at], NY)
                    remote(
                        own.at[sweep, to_x, pl.ds(to_y * PIECE, PIECE)],
                        from_plane.at[sweep, (2 * turn + i) * NY + at],
                        plane_sems.at[sweep], place(to_x, to_y, z, core),
                    ).start()

                for at in range(NY - 1):
                    send(at)
                pl.when(turn + i < 2)(lambda: send(NY - 1))
            return 0

        lax.fori_loop(0, 2, give, 0)
        lax.fori_loop(0, 2, keep, 0)

    def wait_send(ref, sems):
        remote(ref, ref, sems, sibling).wait_send()

    def wait_dipoles():
        same.wait_send()
        mirrored.wait_send()

    def wait_swaps(sweep):
        for turn in range(2):
            wait_send(from_core.at[sweep, turn], core_sems.at[sweep, turn])

    def collect(sweep):
        slots = from_plane.at[sweep]
        remote(slots, slots, plane_sems.at[sweep], sibling).wait_recv()
        total = own[sweep, x, pl.ds(y * PIECE, PIECE), :]
        for i in range(len(plane)):
            total = total + from_plane[sweep, i]
        columns[sweep, z] = total
        for device in column:
            remote(columns.at[sweep, z], columns.at[sweep, z], column_sems.at[sweep], device).start()
        seven = columns.at[sweep, pl.ds(0, NZ - 1)]
        remote(seven, seven, column_sems.at[sweep], sibling).wait_recv()
        total = columns[sweep, 0]
        for i in range(1, NZ):
            total = total + columns[sweep, i]
        return total

    def line_of(squares, group):
        summed = jnp.broadcast_to(jnp.sum(squares, axis=1, keepdims=True), (SUB, LANES))
        return jnp.sum(jnp.where(lane == sublane + group * SUB, summed, 0.0), axis=0, keepdims=True)

    def rms_of(line):
        return jnp.sqrt(line / (2 * BLOCKS * LANES) + 1e-06)[:, : GROUPS * SUB]

    same.wait_recv()
    start_half(z_hi)
    doubles_0, singles_0 = expand(z_hi)
    mirrored.wait_recv()
    start_half(1 - z_hi)
    doubles_1, singles_1 = expand(1 - z_hi)
    finish(doubles_0 + doubles_1, singles_0 + singles_1)
    loads[2].wait()
    fold(0)
    for g in range(GROUPS):
        rows, re_rows, im_rows = pl.ds(g * SUB, SUB), pl.ds(g * PIECE, SUB), pl.ds(g * PIECE + SUB, SUB)
        for b in range(BLOCKS):
            re, im, lev = resp[0, b, re_rows, :], resp[0, b, im_rows, :], level[b, rows, :]
            base[b, re_rows, :] = rhs[b, rows, :] - (lev * re + DAMP * im)
            base[b, im_rows, :] = -(lev * im - DAMP * re)
    total = collect(0)
    block = applied.at[core * HALF + x, pl.ds(y * PIECE, PIECE)]
    applied[core * HALF + x, pl.ds(y * PIECE, PIECE), :] = total
    for device in plane:
        remote(block, block, gather_sems, device).start()
    slots = from_plane.at[0]
    remote(slots, slots, gather_sems, sibling).wait_recv()
    mine = applied.at[pl.ds(core * HALF, HALF)]
    share = remote(mine, mine, share_sem, sibling)
    share.start()
    next_half(core)
    doubles_0, singles_0 = expand(core)
    share.wait_recv()
    next_half(1 - core)
    doubles_1, singles_1 = expand(1 - core)
    finish(doubles_0 + doubles_1, singles_0 + singles_1)
    fold(1)
    line = jnp.zeros((1, LANES), F32)
    for g in range(GROUPS):
        squares = jnp.zeros((SUB, LANES), F32)
        for b in range(BLOCKS):
            res_re, res_im = res[b, pl.ds(g * PIECE, SUB), :], res[b, pl.ds(g * PIECE + SUB, SUB), :]
            squares = squares + (res_re * res_re + res_im * res_im)
        line = line + line_of(squares, g)
    rms_ref[0:1, :] = rms_of(line)
    mine = core * HALF + x
    rows, re_rows = pl.ds(y * SUB, SUB), pl.ds(y * PIECE, SUB)
    im_rows = pl.ds(y * PIECE + SUB, SUB)
    re, im, lev = resp[1, mine, re_rows, :], resp[1, mine, im_rows, :], level[mine, rows, :]
    base_re = rhs[mine, rows, :] - (lev * re + DAMP * im)
    base_im = -(lev * im - DAMP * re)
    total = collect(1)
    res_re, res_im = base_re - total[:SUB], base_im - total[SUB:]
    line = line_of(res_re * res_re + res_im * res_im, y)
    lines[mine * GROUPS + y] = line
    line_out[...] = line
    for device in everyone:
        remote(line_out, lines.at[mine * GROUPS + y], line_sems, device).start()
    p_re, p_im = pre_re[mine, rows, :], pre_im[mine, rows, :]
    final[core, 0, rows, :] = re + (res_re * p_re - res_im * p_im)
    final[core, 1, rows, :] = im + (res_im * p_re + res_re * p_im)
    block = final.at[core, :, rows]
    near = [place(x, lax.rem(y + d, NY), z, c) for d in ALONG[:-1] for c in (1 - core, core)]
    for device in near + [sibling]:
        remote(block, block, final_sems, device).start()
    seven = columns.at[1, pl.ds(0, NZ - 1)]
    remote(seven, seven, final_sems, sibling).wait_recv()
    out_ref[...] = final[z_hi]
    most = lines.at[pl.ds(0, BLOCKS * GROUPS - 1)]
    remote(most, most, line_sems, sibling).wait_recv()
    rms_ref[1:2, :] = rms_of(jnp.sum(lines[...], axis=0))
    wait_send(most, line_sems)
    wait_send(seven, final_sems)

    wait_dipoles()
    share.wait_send()
    wait_send(from_plane.at[0], gather_sems)
    for sweep in range(2):
        wait_swaps(sweep)
        wait_send(from_plane.at[sweep], plane_sems.at[sweep])
        wait_send(columns.at[sweep, pl.ds(0, NZ - 1)], column_sems.at[sweep])


def tail(response_in, rms_in, response_out, rms_out):
    response_out[...] = response_in[...]
    rms_out[...] = rms_in[...]


def per_device(
    amplitudes, integral_slab, coupling, pair_of_block, pair_shift, virt_energy,
    core_energy, core_index, frequency, dipole,
):
    rows, virt_total = amplitudes.shape
    k_total = GROUPS * SUB
    whole, wide_whole = (BLOCKS, k_total, LANES), (BLOCKS, COLS, LANES)
    vmem = pl.BlockSpec(memory_space=pltpu.VMEM)
    anywhere = pl.BlockSpec(memory_space=pl.ANY)
    dma = pltpu.SemaphoreType.DMA
    shapes = (
        jax.ShapeDtypeStruct((2, k_total, LANES), F32),
        jax.ShapeDtypeStruct((2, k_total), F32),
    )
    response, rms = pl.pallas_call(
        kernel,
        name="response",
        out_shape=tuple(pltpu.VMEM(shape.shape, shape.dtype) for shape in shapes),
        in_specs=[anywhere] * 10,
        out_specs=(vmem, vmem),
        scratch_shapes=[
            pltpu.SMEM(pair_of_block.shape, jnp.int32),
            pltpu.SMEM(pair_shift.shape, F32),
            pltpu.SMEM(core_energy.shape, F32),
            pltpu.SMEM(core_index.shape, jnp.int32),
            pltpu.SMEM(frequency.shape, F32),
            pltpu.VMEM((BLOCKS, LANES), F32),
            pltpu.VMEM(dipole.shape, F32),
            pltpu.VMEM((rows, virt_total), BF16),
            pltpu.VMEM((virt_total, virt_total), F32),
            pltpu.VMEM((virt_total, rows), BF16),
            pltpu.VMEM((rows + 2 * virt_total, virt_total), BF16),
            pltpu.VMEM((2 * virt_total, virt_total), BF16),
            pltpu.VMEM((2, LANES), F32),
            pltpu.VMEM((BLOCKS, 2, LANES), F32),
            pltpu.VMEM(whole, F32),
            pltpu.VMEM(whole, F32),
            pltpu.VMEM(whole, F32),
            pltpu.VMEM(whole, F32),
            pltpu.VMEM(whole, F32),
            pltpu.VMEM(whole, F32),
            pltpu.VMEM((2,) + wide_whole, F32),
            pltpu.VMEM(wide_whole, F32),
            pltpu.VMEM(wide_whole, F32),
            pltpu.VMEM((2, 2 * COLS, HALF_COLS), BF16),
            pltpu.VMEM((2 * COLS, rows + virt_total), BF16),
            pltpu.VMEM((2, 2, 2, COLS, LANES), F32),
            pltpu.VMEM((2, 2, 2, COLS, LANES), F32),
            pltpu.VMEM((2, HALF, COLS, LANES), F32),
            pltpu.VMEM((2, len(PLANE), PIECE, LANES), F32),
            pltpu.VMEM((2, NZ, PIECE, LANES), F32),
            pltpu.VMEM(wide_whole, F32),
            pltpu.VMEM((2, 2, k_total, LANES), F32),
            pltpu.VMEM((BLOCKS * GROUPS, 1, LANES), F32),
            pltpu.VMEM((1, LANES), F32),
            dma((7,)),
            dma((3,)),
            dma((2, 2)),
            dma((2, 2, 2)),
            dma((2, 2)),
            dma((2, 2)),
            dma((2,)),
            dma((2,)),
            dma((2,)),
            dma((2,)),
        ],
        compiler_params=pltpu.CompilerParams(
            collective_id=0, has_side_effects=True, vmem_limit_bytes=56 * 2**20
        ),
    )(
        pair_of_block, pair_shift, core_energy, core_index, frequency,
        virt_energy.reshape(BLOCKS, LANES), dipole, amplitudes, integral_slab, coupling,
    )
    return pl.pallas_call(
        tail, name="tail", out_shape=shapes, in_specs=[vmem, vmem], out_specs=(vmem, vmem)
    )(*(pltpu.with_memory_space_constraint(value, pltpu.VMEM) for value in (response, rms)))


def solution(mesh):
    rows = P(("wide", "narrow"), None)
    placed = (rows, rows, P(("wide", "narrow"), None, None)) + (P(),) * 6 + (P(None, "narrow"),)
    return jax.shard_map(
        per_device,
        mesh=mesh,
        in_specs=placed,
        out_specs=(P(None, None, "narrow"), P()),
        check_vma=False,
    )
```

```python
import jax
import jax.numpy as jnp
from jax import lax
from jax.experimental import pallas as pl
from jax.experimental.pallas import tpu as pltpu
from jax.sharding import PartitionSpec as P

DAMP = 0.5
MESH = pl.DeviceIdType.MESH
F32 = jnp.float32
BF16 = jnp.bfloat16

NX, NY, NZ, NZLO = 4, 4, 8, 4


def ring(step, size):
    return min(step, size - step)


PLANE = tuple(
    sorted(
        tuple((dx, dy) for dx in range(NX) for dy in range(NY))[1:],
        key=lambda d: -ring(d[0], NX) - ring(d[1], NY),
    )
)
COLUMN = tuple(sorted(range(1, NZ), key=lambda d: -ring(d, NZ)))
ALONG = (2, 1, 3, 0)
GROUPS, SUB, LANES, BLOCKS = 4, 8, 128, 8
PIECE = 2 * SUB
COLS = GROUPS * PIECE
HALF = BLOCKS // 2
HALF_COLS = HALF * LANES
STRIP = 256


def place(x, y, z, core):
    return {
        "wide": (y * NZLO + lax.rem(z, NZLO)) * 2 + core,
        "narrow": x * 2 + z // NZLO,
    }


def spot(block):
    return (block % 2) * HALF + block // 2


def nn(left, right):
    return lax.dot_general(left, right, (((1,), (0,)), ((), ())), preferred_element_type=F32)


def halves(value):
    high = value.astype(BF16)
    low = (value - high.astype(F32)).astype(BF16)
    return high, low


def remote(src, dst, sems, device):
    return pltpu.make_async_remote_copy(
        src_ref=src, dst_ref=dst, send_sem=sems.at[0], recv_sem=sems.at[1],
        device_id=device, device_id_type=MESH,
    )


def kernel(
    pair_of_block_hbm, pair_shift_hbm, core_energy_hbm, core_index_hbm, frequency_hbm,
    virt_hbm, dipole_hbm, amp_hbm, slab_hbm, coup_hbm,
    out_ref, rms_ref,
    pair_of_block, pair_shift, core_energy, core_index, frequency, virt, dipole,
    slab, coup, slab_t, right, coup_t,
    picked, dip, rhs, pre_re, pre_im, level, den_re, den_im, resp, base, res,
    pieces, left,
    part, from_core, own, from_plane, columns, applied, final, lines, line_out,
    small_sem, hbm_sem, dip_sems, core_sems, plane_sems, column_sems, gather_sems, share_sems,
    final_sems, line_sems,
):
    wide, narrow = lax.axis_index("wide"), lax.axis_index("narrow")
    x, y, core = narrow // 2, wide // (2 * NZLO), lax.rem(wide, 2)
    z_hi, z_lo = lax.rem(narrow, 2), lax.rem(wide // 2, NZLO)
    z = z_hi * NZLO + z_lo
    rows_total, virt_total = slab.shape
    mirror = (1 - z_hi) * NZLO + lax.rem(z_lo + 2, NZLO)

    loads = [
        pltpu.make_async_copy(coup_hbm.at[0], coup, hbm_sem.at[0]),
        pltpu.make_async_copy(slab_hbm, slab, hbm_sem.at[1]),
        pltpu.make_async_copy(amp_hbm, right.at[pl.ds(0, rows_total)], hbm_sem.at[2]),
    ]
    sibling = place(x, y, z, 1 - core)
    plane_xy = [(lax.rem(x + dx, NX), lax.rem(y + dy, NY)) for dx, dy in PLANE]
    plane = [place(to_x, to_y, z, core) for to_x, to_y in plane_xy]
    across = [place(to_x, to_y, z, 1 - core) for to_x, to_y in plane_xy]
    everyone = [device for pair in zip(across, plane) for device in pair] + [sibling]
    column = [place(x, y, lax.rem(z + d, NZ), core) for d in COLUMN]
    mirrors = [place(lax.rem(x + d, NX), y, mirror, core) for d in ALONG]
    beside = [place(lax.rem(x + d, NX), y, z, core) for d in ALONG[:-1]]

    barrier = pltpu.get_barrier_semaphore()
    greeted = mirrors[:-1] + column
    for device in greeted:
        pl.semaphore_signal(barrier, inc=1, device_id=device, device_id_type=MESH)

    small = [
        pltpu.make_async_copy(src, dst, small_sem.at[i])
        for i, (src, dst) in enumerate((
            (core_index_hbm, core_index), (dipole_hbm, dipole), (virt_hbm, virt),
            (core_energy_hbm, core_energy), (frequency_hbm, frequency),
            (pair_of_block_hbm, pair_of_block), (pair_shift_hbm, pair_shift),
        ))
    ]
    for load in small + loads[:2]:
        load.start()
    for device in everyone:
        pl.semaphore_signal(barrier, inc=1, device_id=device, device_id_type=MESH)

    for load in small:
        load.wait()
    for c in range(2):
        picked[c : c + 1, :] = dipole[pl.ds(core_index[c], 1), :]

    sublane = lax.broadcasted_iota(jnp.int32, (SUB, LANES), 0)
    lane = lax.broadcasted_iota(jnp.int32, (SUB, LANES), 1)
    offset = pair_shift[pair_of_block[wide * 8 + narrow]]
    for g in range(GROUPS):
        energy = core_energy[core_index[g // 2]]
        shift = jnp.zeros((SUB, LANES), F32)
        for j in range(SUB):
            value = frequency[(g % 2) * SUB + j] + energy
            shift = jnp.where(sublane == j, value, shift)
        rows = pl.ds(g * SUB, SUB)
        for b in range(BLOCKS):
            energies = jnp.broadcast_to(virt[b : b + 1, :], (SUB, LANES))
            lev = energies - shift
            inverse = 1.0 / (lev * lev + DAMP * DAMP)
            level[spot(b), rows, :] = lev
            pre_re[spot(b), rows, :] = lev * inverse
            pre_im[spot(b), rows, :] = DAMP * inverse
            den = (shift - offset) - energies
            inverse = 1.0 / (den * den + DAMP * DAMP)
            den_re[b, rows, :] = den * inverse
            den_im[b, rows, :] = DAMP * inverse

    pl.semaphore_wait(barrier, len(greeted) + len(everyone))
    for device in mirrors:
        remote(picked, dip.at[narrow], dip_sems.at[1], device).start()
    for device in beside:
        remote(picked, dip.at[narrow], dip_sems.at[0], device).start()
    loads[2].start()
    dip[narrow] = picked[...]

    loads[0].wait()

    def split_rows(i, _):
        rows = pl.ds(pl.multiple_of(i * STRIP, STRIP), STRIP)
        strip = coup[rows, :]
        high, low = halves(strip)
        start = rows_total + i * STRIP
        right[pl.ds(pl.multiple_of(start, STRIP), STRIP), :] = high
        right[pl.ds(pl.multiple_of(start + virt_total, STRIP), STRIP), :] = low
        high, low = high.T, low.T
        for b in range(BLOCKS):
            cols, there = slice(b * LANES, (b + 1) * LANES), (b % 2) * 2 * HALF_COLS + (b // 2) * LANES
            coup_t[there : there + LANES, rows] = high[cols]
            coup_t[there + HALF_COLS : there + HALF_COLS + LANES, rows] = low[cols]
        return 0

    lax.fori_loop(0, coup.shape[0] // STRIP, split_rows, 0)
    loads[1].wait()

    def turn_rows(i, _):
        rows = pl.ds(pl.multiple_of(i * STRIP, STRIP), STRIP)
        turned = slab[rows, :].T
        for b in range(BLOCKS):
            slab_t[spot(b) * LANES : (spot(b) + 1) * LANES, rows] = turned[b * LANES : (b + 1) * LANES]
        return 0

    lax.fori_loop(0, slab.shape[0] // STRIP, turn_rows, 0)
    same = remote(dip.at[pl.ds(0, NX - 1)], dip.at[pl.ds(0, NX - 1)], dip_sems.at[0], sibling)
    mirrored = remote(dip.at[pl.ds(0, NX)], dip.at[pl.ds(0, NX)], dip_sems.at[1], sibling)

    def start_half(half):
        for g in range(GROUPS):
            rows, re_rows, im_rows = pl.ds(g * SUB, SUB), pl.ds(g * PIECE, SUB), pl.ds(g * PIECE + SUB, SUB)
            for j in range(HALF):
                b, cols = half * HALF + j, slice(j * LANES, (j + 1) * LANES)
                source = jnp.broadcast_to(dip[2 * j + half, g // 2 : g // 2 + 1, :], (SUB, LANES))
                rhs[b, rows, :] = source
                re, im = source * pre_re[b, rows, :], source * pre_im[b, rows, :]
                resp[0, b, re_rows, :] = re
                resp[0, b, im_rows, :] = im
                high, low = halves(jnp.concatenate([re, im], 0))
                pieces[half, g * PIECE : (g + 1) * PIECE, cols] = high
                pieces[half, COLS + g * PIECE : COLS + (g + 1) * PIECE, cols] = low

    def next_block(half, j):
        b, cols = half * HALF + j, pl.ds(pl.multiple_of(j * LANES, LANES), LANES)
        for g in range(GROUPS):
            rows, re_rows, im_rows = pl.ds(g * SUB, SUB), pl.ds(g * PIECE, SUB), pl.ds(g * PIECE + SUB, SUB)
            res_re = base[b, re_rows, :] - applied[b, re_rows, :]
            res_im = base[b, im_rows, :] - applied[b, im_rows, :]
            res[b, re_rows, :] = res_re
            res[b, im_rows, :] = res_im
            p_re, p_im = pre_re[b, rows, :], pre_im[b, rows, :]
            re = resp[0, b, re_rows, :] + (res_re * p_re - res_im * p_im)
            im = resp[0, b, im_rows, :] + (res_im * p_re + res_re * p_im)
            resp[1, b, re_rows, :] = re
            resp[1, b, im_rows, :] = im
            high, low = halves(jnp.concatenate([re, im], 0))
            pieces[half, g * PIECE : (g + 1) * PIECE, cols] = high
            pieces[half, COLS + g * PIECE : COLS + (g + 1) * PIECE, cols] = low

    def joined(both):
        return both[:COLS] + both[COLS:]

    def expand(half):
        piece = pieces[half]
        rows = pl.ds(pl.multiple_of(half * 2 * HALF_COLS, HALF_COLS), 2 * HALF_COLS)
        doubles = nn(jnp.concatenate([piece, piece], 1), coup_t[rows, :])
        rows = pl.ds(pl.multiple_of(half * HALF_COLS, HALF_COLS), HALF_COLS)
        return joined(doubles), joined(nn(piece, slab_t[rows, :]))

    def finish(doubles, singles):
        for g in range(GROUPS):
            rows = pl.ds(g * SUB, SUB)
            for b in range(BLOCKS):
                cols = slice(b * LANES, (b + 1) * LANES)
                real = doubles[g * PIECE : g * PIECE + SUB, cols]
                imag = doubles[g * PIECE + SUB : (g + 1) * PIECE, cols]
                q_re, q_im = den_re[b, rows, :], den_im[b, rows, :]
                quotient = jnp.concatenate([real * q_re + imag * q_im, imag * q_re - real * q_im], 0)
                high, low = halves(quotient)
                cols = slice(rows_total + b * LANES, rows_total + (b + 1) * LANES)
                left[g * PIECE : (g + 1) * PIECE, cols] = high
                left[COLS + g * PIECE : COLS + (g + 1) * PIECE, cols] = low
        high, low = halves(singles)
        left[:COLS, :rows_total] = high
        left[COLS:, :rows_total] = low

    parity, far = lax.rem(x, 2), 1 - x // 2
    strips = (far, 1 - far)
    reach = ((2 * far + parity, 2 * far + 1 - parity), (3 - 2 * far - parity, 2 - 2 * far + parity))

    def fold(sweep):
        def share_of(side, strip):
            columns_of = [
                right[:, pl.ds(pl.multiple_of((4 * strip + 2 * i + side) * LANES, LANES), LANES)] for i in range(2)
            ]
            rows_of = jnp.concatenate([left[...], left[:, rows_total:]], 1)
            return joined(nn(rows_of, jnp.concatenate(columns_of, 1)))

        swaps = []
        for turn, strip in enumerate(strips):
            share = share_of(1 - core, strip)
            for i in range(2):
                part[sweep, turn, i] = share[:, i * LANES : (i + 1) * LANES]
            swap = remote(part.at[sweep, turn], from_core.at[sweep, turn], core_sems.at[sweep, turn], sibling)
            swap.start()
            swaps.append(swap)
        slot = 0
        for turn, strip in enumerate(strips):
            share = share_of(core, strip)
            swaps[turn].wait_recv()
            for i in range(2):
                own[sweep, 2 * strip + i] = share[:, i * LANES : (i + 1) * LANES] + from_core[sweep, turn, i]
            for to_x in reach[turn]:
                for dy in ALONG[: NY if slot < 3 * NY else NY - 1]:
                    to_y = lax.rem(y + dy, NY)
                    remote(
                        own.at[sweep, to_x, pl.ds(to_y * PIECE, PIECE)], from_plane.at[sweep, slot],
                        plane_sems.at[sweep], place(to_x, to_y, z, core),
                    ).start()
                    slot += 1
    def wait_send(ref, sems):
        remote(ref, ref, sems, sibling).wait_send()

    def wait_dipoles():
        same.wait_send()
        mirrored.wait_send()

    def wait_swaps(sweep):
        for turn in range(2):
            wait_send(from_core.at[sweep, turn], core_sems.at[sweep, turn])

    def collect(sweep):
        slots = from_plane.at[sweep]
        remote(slots, slots, plane_sems.at[sweep], sibling).wait_recv()
        total = own[sweep, x, pl.ds(y * PIECE, PIECE), :]
        for i in range(len(plane)):
            total = total + from_plane[sweep, i]
        columns[sweep, z] = total
        for device in column:
            remote(columns.at[sweep, z], columns.at[sweep, z], column_sems.at[sweep], device).start()
        seven = columns.at[sweep, pl.ds(0, NZ - 1)]
        remote(seven, seven, column_sems.at[sweep], sibling).wait_recv()
        total = columns[sweep, 0]
        for i in range(1, NZ):
            total = total + columns[sweep, i]
        return total

    def line_of(squares, group):
        summed = jnp.broadcast_to(jnp.sum(squares, axis=1, keepdims=True), (SUB, LANES))
        return jnp.sum(jnp.where(lane == sublane + group * SUB, summed, 0.0), axis=0, keepdims=True)

    def rms_of(line):
        return jnp.sqrt(line / (2 * BLOCKS * LANES) + 1e-06)[:, : GROUPS * SUB]

    same.wait_recv()
    start_half(z_hi)
    doubles_0, singles_0 = expand(z_hi)
    mirrored.wait_recv()
    start_half(1 - z_hi)
    doubles_1, singles_1 = expand(1 - z_hi)
    finish(doubles_0 + doubles_1, singles_0 + singles_1)
    loads[2].wait()
    fold(0)
    for g in range(GROUPS):
        rows, re_rows, im_rows = pl.ds(g * SUB, SUB), pl.ds(g * PIECE, SUB), pl.ds(g * PIECE + SUB, SUB)
        for b in range(BLOCKS):
            re, im, lev = resp[0, b, re_rows, :], resp[0, b, im_rows, :], level[b, rows, :]
            base[b, re_rows, :] = rhs[b, rows, :] - (lev * re + DAMP * im)
            base[b, im_rows, :] = -(lev * im - DAMP * re)
    total = collect(0)
    block = applied.at[core * HALF + x, pl.ds(y * PIECE, PIECE)]
    applied[core * HALF + x, pl.ds(y * PIECE, PIECE), :] = total
    for (dx, _), device in zip(PLANE, plane):
        remote(block, block, gather_sems.at[int(dx == 2)], device).start()
    across_x = [lax.rem(x + d, NX) for d in (0, 1, 3, 2)]

    def pass_on(j, sems):
        mine = applied.at[core * HALF + j]
        remote(mine, mine, sems, sibling).start()

    near_slots = from_plane.at[0, pl.ds(0, len(plane) - NY)]
    far_slots = from_plane.at[0, pl.ds(0, NY)]
    remote(near_slots, near_slots, gather_sems.at[0], sibling).wait_recv()
    for j in across_x[:3]:
        pass_on(j, share_sems.at[0])
    for j in across_x[:3]:
        next_block(core, j)
    remote(far_slots, far_slots, gather_sems.at[1], sibling).wait_recv()
    pass_on(across_x[3], share_sems.at[1])
    next_block(core, across_x[3])
    doubles_0, singles_0 = expand(core)
    three, one = applied.at[pl.ds(0, 3)], applied.at[pl.ds(0, 1)]
    remote(three, three, share_sems.at[0], sibling).wait_recv()
    for j in across_x[:3]:
        next_block(1 - core, j)
    remote(one, one, share_sems.at[1], sibling).wait_recv()
    next_block(1 - core, across_x[3])
    doubles_1, singles_1 = expand(1 - core)
    finish(doubles_0 + doubles_1, singles_0 + singles_1)
    fold(1)
    line = jnp.zeros((1, LANES), F32)
    for g in range(GROUPS):
        squares = jnp.zeros((SUB, LANES), F32)
        for b in range(BLOCKS):
            res_re, res_im = res[b, pl.ds(g * PIECE, SUB), :], res[b, pl.ds(g * PIECE + SUB, SUB), :]
            squares = squares + (res_re * res_re + res_im * res_im)
        line = line + line_of(squares, g)
    rms_ref[0:1, :] = rms_of(line)
    mine = core * HALF + x
    rows, re_rows = pl.ds(y * SUB, SUB), pl.ds(y * PIECE, SUB)
    im_rows = pl.ds(y * PIECE + SUB, SUB)
    re, im, lev = resp[1, mine, re_rows, :], resp[1, mine, im_rows, :], level[mine, rows, :]
    base_re = rhs[mine, rows, :] - (lev * re + DAMP * im)
    base_im = -(lev * im - DAMP * re)
    total = collect(1)
    res_re, res_im = base_re - total[:SUB], base_im - total[SUB:]
    line = line_of(res_re * res_re + res_im * res_im, y)
    lines[mine * GROUPS + y] = line
    line_out[...] = line
    for device in everyone:
        remote(line_out, lines.at[mine * GROUPS + y], line_sems, device).start()
    p_re, p_im = pre_re[mine, rows, :], pre_im[mine, rows, :]
    final[core, 0, rows, :] = re + (res_re * p_re - res_im * p_im)
    final[core, 1, rows, :] = im + (res_im * p_re + res_re * p_im)
    block = final.at[core, :, rows]
    near = [place(x, lax.rem(y + d, NY), z, c) for d in ALONG[:-1] for c in (1 - core, core)]
    for device in near + [sibling]:
        remote(block, block, final_sems, device).start()
    seven = columns.at[1, pl.ds(0, NZ - 1)]
    remote(seven, seven, final_sems, sibling).wait_recv()
    out_ref[...] = final[z_hi]
    most = lines.at[pl.ds(0, BLOCKS * GROUPS - 1)]
    remote(most, most, line_sems, sibling).wait_recv()
    rms_ref[1:2, :] = rms_of(jnp.sum(lines[...], axis=0))
    wait_send(most, line_sems)
    wait_send(seven, final_sems)

    wait_dipoles()
    wait_send(near_slots, gather_sems.at[0])
    wait_send(far_slots, gather_sems.at[1])
    wait_send(three, share_sems.at[0])
    wait_send(one, share_sems.at[1])
    for sweep in range(2):
        wait_swaps(sweep)
        wait_send(from_plane.at[sweep], plane_sems.at[sweep])
        wait_send(columns.at[sweep, pl.ds(0, NZ - 1)], column_sems.at[sweep])


def tail(response_in, rms_in, response_out, rms_out):
    response_out[...] = response_in[...]
    rms_out[...] = rms_in[...]


def per_device(
    amplitudes, integral_slab, coupling, pair_of_block, pair_shift, virt_energy,
    core_energy, core_index, frequency, dipole,
):
    rows, virt_total = amplitudes.shape
    k_total = GROUPS * SUB
    whole, wide_whole = (BLOCKS, k_total, LANES), (BLOCKS, COLS, LANES)
    vmem = pl.BlockSpec(memory_space=pltpu.VMEM)
    anywhere = pl.BlockSpec(memory_space=pl.ANY)
    dma = pltpu.SemaphoreType.DMA
    shapes = (
        jax.ShapeDtypeStruct((2, k_total, LANES), F32),
        jax.ShapeDtypeStruct((2, k_total), F32),
    )
    response, rms = pl.pallas_call(
        kernel,
        name="response",
        out_shape=tuple(pltpu.VMEM(shape.shape, shape.dtype) for shape in shapes),
        in_specs=[anywhere] * 10,
        out_specs=(vmem, vmem),
        scratch_shapes=[
            pltpu.SMEM(pair_of_block.shape, jnp.int32),
            pltpu.SMEM(pair_shift.shape, F32),
            pltpu.SMEM(core_energy.shape, F32),
            pltpu.SMEM(core_index.shape, jnp.int32),
            pltpu.SMEM(frequency.shape, F32),
            pltpu.VMEM((BLOCKS, LANES), F32),
            pltpu.VMEM(dipole.shape, F32),
            pltpu.VMEM((rows, virt_total), BF16),
            pltpu.VMEM((virt_total, virt_total), F32),
            pltpu.VMEM((virt_total, rows), BF16),
            pltpu.VMEM((rows + 2 * virt_total, virt_total), BF16),
            pltpu.VMEM((2 * virt_total, virt_total), BF16),
            pltpu.VMEM((2, LANES), F32),
            pltpu.VMEM((BLOCKS, 2, LANES), F32),
            pltpu.VMEM(whole, F32),
            pltpu.VMEM(whole, F32),
            pltpu.VMEM(whole, F32),
            pltpu.VMEM(whole, F32),
            pltpu.VMEM(whole, F32),
            pltpu.VMEM(whole, F32),
            pltpu.VMEM((2,) + wide_whole, F32),
            pltpu.VMEM(wide_whole, F32),
            pltpu.VMEM(wide_whole, F32),
            pltpu.VMEM((2, 2 * COLS, HALF_COLS), BF16),
            pltpu.VMEM((2 * COLS, rows + virt_total), BF16),
            pltpu.VMEM((2, 2, 2, COLS, LANES), F32),
            pltpu.VMEM((2, 2, 2, COLS, LANES), F32),
            pltpu.VMEM((2, HALF, COLS, LANES), F32),
            pltpu.VMEM((2, len(PLANE), PIECE, LANES), F32),
            pltpu.VMEM((2, NZ, PIECE, LANES), F32),
            pltpu.VMEM(wide_whole, F32),
            pltpu.VMEM((2, 2, k_total, LANES), F32),
            pltpu.VMEM((BLOCKS * GROUPS, 1, LANES), F32),
            pltpu.VMEM((1, LANES), F32),
            dma((7,)),
            dma((3,)),
            dma((2, 2)),
            dma((2, 2, 2)),
            dma((2, 2)),
            dma((2, 2)),
            dma((2, 2)),
            dma((2, 2)),
            dma((2,)),
            dma((2,)),
        ],
        compiler_params=pltpu.CompilerParams(
            collective_id=0, has_side_effects=True, vmem_limit_bytes=56 * 2**20
        ),
    )(
        pair_of_block, pair_shift, core_energy, core_index, frequency,
        virt_energy.reshape(BLOCKS, LANES), dipole, amplitudes, integral_slab, coupling,
    )
    return pl.pallas_call(
        tail, name="tail", out_shape=shapes, in_specs=[vmem, vmem], out_specs=(vmem, vmem)
    )(*(pltpu.with_memory_space_constraint(value, pltpu.VMEM) for value in (response, rms)))


def solution(mesh):
    rows = P(("wide", "narrow"), None)
    placed = (rows, rows, P(("wide", "narrow"), None, None)) + (P(),) * 6 + (P(None, "narrow"),)
    return jax.shard_map(
        per_device,
        mesh=mesh,
        in_specs=placed,
        out_specs=(P(None, None, "narrow"), P()),
        check_vma=False,
    )
```

```python
import jax
import jax.numpy as jnp
from jax import lax
from jax.experimental import pallas as pl
from jax.experimental.pallas import tpu as pltpu
from jax.sharding import PartitionSpec as P

DAMP = 0.5
MESH = pl.DeviceIdType.MESH
F32 = jnp.float32
BF16 = jnp.bfloat16

NX, NY, NZ, NZLO = 4, 4, 8, 4


def ring(step, size):
    return min(step, size - step)


PLANE = tuple(
    sorted(
        tuple((dx, dy) for dx in range(NX) for dy in range(NY))[1:],
        key=lambda d: -ring(d[0], NX) - ring(d[1], NY),
    )
)
COLUMN = tuple(sorted(range(1, NZ), key=lambda d: -ring(d, NZ)))
ALONG = (2, 1, 3, 0)
GROUPS, SUB, LANES, BLOCKS = 4, 8, 128, 8
PIECE = 2 * SUB
COLS = GROUPS * PIECE
HALF = BLOCKS // 2
HALF_COLS = HALF * LANES
STRIP = 256


def place(x, y, z, core):
    return {
        "wide": (y * NZLO + lax.rem(z, NZLO)) * 2 + core,
        "narrow": x * 2 + z // NZLO,
    }


def spot(block):
    return (block % 2) * HALF + block // 2


def nn(left, right):
    return lax.dot_general(left, right, (((1,), (0,)), ((), ())), preferred_element_type=F32)


def halves(value):
    high = value.astype(BF16)
    low = (value - high.astype(F32)).astype(BF16)
    return high, low


def remote(src, dst, sems, device):
    return pltpu.make_async_remote_copy(
        src_ref=src, dst_ref=dst, send_sem=sems.at[0], recv_sem=sems.at[1],
        device_id=device, device_id_type=MESH,
    )


def kernel(
    pair_of_block_hbm, pair_shift_hbm, core_energy_hbm, core_index_hbm, frequency_hbm,
    virt_hbm, dipole_hbm, amp_hbm, slab_hbm, coup_hbm,
    out_ref, rms_ref,
    pair_of_block, pair_shift, core_energy, core_index, frequency, virt, dipole,
    slab, coup, slab_t, right, coup_t,
    picked, dip, rhs, pre_re, pre_im, level, den_re, den_im, resp, base, res,
    pieces, left,
    part, from_core, own, from_plane, columns, applied, final, lines, line_out,
    small_sem, hbm_sem, dip_sems, core_sems, plane_sems, column_sems, gather_sems, share_sem,
    final_sems, line_sems,
):
    wide, narrow = lax.axis_index("wide"), lax.axis_index("narrow")
    x, y, core = narrow // 2, wide // (2 * NZLO), lax.rem(wide, 2)
    z_hi, z_lo = lax.rem(narrow, 2), lax.rem(wide // 2, NZLO)
    z = z_hi * NZLO + z_lo
    rows_total, virt_total = slab.shape
    mirror = (1 - z_hi) * NZLO + lax.rem(z_lo + 2, NZLO)

    loads = [
        pltpu.make_async_copy(coup_hbm.at[0], coup, hbm_sem.at[0]),
        pltpu.make_async_copy(slab_hbm, slab, hbm_sem.at[1]),
        pltpu.make_async_copy(amp_hbm, right.at[pl.ds(0, rows_total)], hbm_sem.at[2]),
    ]
    sibling = place(x, y, z, 1 - core)
    plane_xy = [(lax.rem(x + dx, NX), lax.rem(y + dy, NY)) for dx, dy in PLANE]
    plane = [place(to_x, to_y, z, core) for to_x, to_y in plane_xy]
    across = [place(to_x, to_y, z, 1 - core) for to_x, to_y in plane_xy]
    everyone = [device for pair in zip(across, plane) for device in pair] + [sibling]
    column = [place(x, y, lax.rem(z + d, NZ), core) for d in COLUMN]
    mirrors = [place(lax.rem(x + d, NX), y, mirror, core) for d in ALONG]
    beside = [place(lax.rem(x + d, NX), y, z, core) for d in ALONG[:-1]]

    barrier = pltpu.get_barrier_semaphore()
    greeted = mirrors[:-1] + column
    for device in greeted:
        pl.semaphore_signal(barrier, inc=1, device_id=device, device_id_type=MESH)

    small = [
        pltpu.make_async_copy(src, dst, small_sem.at[i])
        for i, (src, dst) in enumerate((
            (core_index_hbm, core_index), (dipole_hbm, dipole), (virt_hbm, virt),
            (core_energy_hbm, core_energy), (frequency_hbm, frequency),
            (pair_of_block_hbm, pair_of_block), (pair_shift_hbm, pair_shift),
        ))
    ]
    for load in small + loads[:2]:
        load.start()
    for device in everyone:
        pl.semaphore_signal(barrier, inc=1, device_id=device, device_id_type=MESH)

    for load in small:
        load.wait()
    for c in range(2):
        picked[c : c + 1, :] = dipole[pl.ds(core_index[c], 1), :]

    sublane = lax.broadcasted_iota(jnp.int32, (SUB, LANES), 0)
    lane = lax.broadcasted_iota(jnp.int32, (SUB, LANES), 1)
    offset = pair_shift[pair_of_block[wide * 8 + narrow]]
    for g in range(GROUPS):
        energy = core_energy[core_index[g // 2]]
        shift = jnp.zeros((SUB, LANES), F32)
        for j in range(SUB):
            value = frequency[(g % 2) * SUB + j] + energy
            shift = jnp.where(sublane == j, value, shift)
        rows = pl.ds(g * SUB, SUB)
        for b in range(BLOCKS):
            energies = jnp.broadcast_to(virt[b : b + 1, :], (SUB, LANES))
            lev = energies - shift
            inverse = 1.0 / (lev * lev + DAMP * DAMP)
            level[spot(b), rows, :] = lev
            pre_re[spot(b), rows, :] = lev * inverse
            pre_im[spot(b), rows, :] = DAMP * inverse
            den = (shift - offset) - energies
            inverse = 1.0 / (den * den + DAMP * DAMP)
            den_re[b, rows, :] = den * inverse
            den_im[b, rows, :] = DAMP * inverse

    pl.semaphore_wait(barrier, len(greeted) + len(everyone))
    for device in mirrors:
        remote(picked, dip.at[narrow], dip_sems.at[1], device).start()
    for device in beside:
        remote(picked, dip.at[narrow], dip_sems.at[0], device).start()
    loads[2].start()
    dip[narrow] = picked[...]

    loads[0].wait()

    def split_rows(i, _):
        rows = pl.ds(pl.multiple_of(i * STRIP, STRIP), STRIP)
        strip = coup[rows, :]
        high, low = halves(strip)
        start = rows_total + i * STRIP
        right[pl.ds(pl.multiple_of(start, STRIP), STRIP), :] = high
        right[pl.ds(pl.multiple_of(start + virt_total, STRIP), STRIP), :] = low
        high, low = high.T, low.T
        for b in range(BLOCKS):
            cols, there = slice(b * LANES, (b + 1) * LANES), (b % 2) * 2 * HALF_COLS + (b // 2) * LANES
            coup_t[there : there + LANES, rows] = high[cols]
            coup_t[there + HALF_COLS : there + HALF_COLS + LANES, rows] = low[cols]
        return 0

    lax.fori_loop(0, coup.shape[0] // STRIP, split_rows, 0)
    loads[1].wait()

    def turn_rows(i, _):
        rows = pl.ds(pl.multiple_of(i * STRIP, STRIP), STRIP)
        turned = slab[rows, :].T
        for b in range(BLOCKS):
            slab_t[spot(b) * LANES : (spot(b) + 1) * LANES, rows] = turned[b * LANES : (b + 1) * LANES]
        return 0

    lax.fori_loop(0, slab.shape[0] // STRIP, turn_rows, 0)
    same = remote(dip.at[pl.ds(0, NX - 1)], dip.at[pl.ds(0, NX - 1)], dip_sems.at[0], sibling)
    mirrored = remote(dip.at[pl.ds(0, NX)], dip.at[pl.ds(0, NX)], dip_sems.at[1], sibling)

    def start_half(half):
        for g in range(GROUPS):
            rows, re_rows, im_rows = pl.ds(g * SUB, SUB), pl.ds(g * PIECE, SUB), pl.ds(g * PIECE + SUB, SUB)
            for j in range(HALF):
                b, cols = half * HALF + j, slice(j * LANES, (j + 1) * LANES)
                source = jnp.broadcast_to(dip[2 * j + half, g // 2 : g // 2 + 1, :], (SUB, LANES))
                rhs[b, rows, :] = source
                re, im = source * pre_re[b, rows, :], source * pre_im[b, rows, :]
                resp[0, b, re_rows, :] = re
                resp[0, b, im_rows, :] = im
                high, low = halves(jnp.concatenate([re, im], 0))
                pieces[half, g * PIECE : (g + 1) * PIECE, cols] = high
                pieces[half, COLS + g * PIECE : COLS + (g + 1) * PIECE, cols] = low

    def next_half(half):
        for g in range(GROUPS):
            rows, re_rows, im_rows = pl.ds(g * SUB, SUB), pl.ds(g * PIECE, SUB), pl.ds(g * PIECE + SUB, SUB)
            for j in range(HALF):
                b, cols = half * HALF + j, slice(j * LANES, (j + 1) * LANES)
                res_re = base[b, re_rows, :] - applied[b, re_rows, :]
                res_im = base[b, im_rows, :] - applied[b, im_rows, :]
                res[b, re_rows, :] = res_re
                res[b, im_rows, :] = res_im
                p_re, p_im = pre_re[b, rows, :], pre_im[b, rows, :]
                re = resp[0, b, re_rows, :] + (res_re * p_re - res_im * p_im)
                im = resp[0, b, im_rows, :] + (res_im * p_re + res_re * p_im)
                resp[1, b, re_rows, :] = re
                resp[1, b, im_rows, :] = im
                high, low = halves(jnp.concatenate([re, im], 0))
                pieces[half, g * PIECE : (g + 1) * PIECE, cols] = high
                pieces[half, COLS + g * PIECE : COLS + (g + 1) * PIECE, cols] = low

    def joined(both):
        return both[:COLS] + both[COLS:]

    def expand(half):
        piece = pieces[half]
        rows = pl.ds(pl.multiple_of(half * 2 * HALF_COLS, HALF_COLS), 2 * HALF_COLS)
        doubles = nn(jnp.concatenate([piece, piece], 1), coup_t[rows, :])
        rows = pl.ds(pl.multiple_of(half * HALF_COLS, HALF_COLS), HALF_COLS)
        return joined(doubles), joined(nn(piece, slab_t[rows, :]))

    def finish(doubles, singles):
        for g in range(GROUPS):
            rows = pl.ds(g * SUB, SUB)
            for b in range(BLOCKS):
                cols = slice(b * LANES, (b + 1) * LANES)
                real = doubles[g * PIECE : g * PIECE + SUB, cols]
                imag = doubles[g * PIECE + SUB : (g + 1) * PIECE, cols]
                q_re, q_im = den_re[b, rows, :], den_im[b, rows, :]
                quotient = jnp.concatenate([real * q_re + imag * q_im, imag * q_re - real * q_im], 0)
                high, low = halves(quotient)
                cols = slice(rows_total + b * LANES, rows_total + (b + 1) * LANES)
                left[g * PIECE : (g + 1) * PIECE, cols] = high
                left[COLS + g * PIECE : COLS + (g + 1) * PIECE, cols] = low
        high, low = halves(singles)
        left[:COLS, :rows_total] = high
        left[COLS:, :rows_total] = low

    parity, far = lax.rem(x, 2), 1 - x // 2
    strips = (far, 1 - far)
    reach = ((2 * far + parity, 2 * far + 1 - parity), (3 - 2 * far - parity, 2 - 2 * far + parity))

    def fold(sweep):
        def share_of(side, strip):
            columns_of = [
                right[:, pl.ds(pl.multiple_of((4 * strip + 2 * i + side) * LANES, LANES), LANES)] for i in range(2)
            ]
            rows_of = jnp.concatenate([left[...], left[:, rows_total:]], 1)
            return joined(nn(rows_of, jnp.concatenate(columns_of, 1)))

        swaps = []
        for turn, strip in enumerate(strips):
            share = share_of(1 - core, strip)
            for i in range(2):
                part[sweep, turn, i] = share[:, i * LANES : (i + 1) * LANES]
            swap = remote(part.at[sweep, turn], from_core.at[sweep, turn], core_sems.at[sweep, turn], sibling)
            swap.start()
            swaps.append(swap)
        slot = 0
        for turn, strip in enumerate(strips):
            share = share_of(core, strip)
            swaps[turn].wait_recv()
            for i in range(2):
                own[sweep, 2 * strip + i] = share[:, i * LANES : (i + 1) * LANES] + from_core[sweep, turn, i]
            for to_x in reach[turn]:
                for dy in ALONG[: NY if slot < 3 * NY else NY - 1]:
                    to_y = lax.rem(y + dy, NY)
                    remote(
                        own.at[sweep, to_x, pl.ds(to_y * PIECE, PIECE)], from_plane.at[sweep, slot],
                        plane_sems.at[sweep], place(to_x, to_y, z, core),
                    ).start()
                    slot += 1
    def wait_send(ref, sems):
        remote(ref, ref, sems, sibling).wait_send()

    def wait_dipoles():
        same.wait_send()
        mirrored.wait_send()

    def wait_swaps(sweep):
        for turn in range(2):
            wait_send(from_core.at[sweep, turn], core_sems.at[sweep, turn])

    def collect(sweep):
        slots = from_plane.at[sweep]
        remote(slots, slots, plane_sems.at[sweep], sibling).wait_recv()
        total = own[sweep, x, pl.ds(y * PIECE, PIECE), :]
        for i in range(len(plane)):
            total = total + from_plane[sweep, i]
        columns[sweep, z] = total
        for device in column:
            remote(columns.at[sweep, z], columns.at[sweep, z], column_sems.at[sweep], device).start()
        seven = columns.at[sweep, pl.ds(0, NZ - 1)]
        remote(seven, seven, column_sems.at[sweep], sibling).wait_recv()
        total = columns[sweep, 0]
        for i in range(1, NZ):
            total = total + columns[sweep, i]
        return total

    def line_of(squares, group):
        summed = jnp.broadcast_to(jnp.sum(squares, axis=1, keepdims=True), (SUB, LANES))
        return jnp.sum(jnp.where(lane == sublane + group * SUB, summed, 0.0), axis=0, keepdims=True)

    def rms_of(line):
        return jnp.sqrt(line / (2 * BLOCKS * LANES) + 1e-06)[:, : GROUPS * SUB]

    same.wait_recv()
    start_half(z_hi)
    doubles_0, singles_0 = expand(z_hi)
    mirrored.wait_recv()
    start_half(1 - z_hi)
    doubles_1, singles_1 = expand(1 - z_hi)
    finish(doubles_0 + doubles_1, singles_0 + singles_1)
    loads[2].wait()
    fold(0)
    for g in range(GROUPS):
        rows, re_rows, im_rows = pl.ds(g * SUB, SUB), pl.ds(g * PIECE, SUB), pl.ds(g * PIECE + SUB, SUB)
        for b in range(BLOCKS):
            re, im, lev = resp[0, b, re_rows, :], resp[0, b, im_rows, :], level[b, rows, :]
            base[b, re_rows, :] = rhs[b, rows, :] - (lev * re + DAMP * im)
            base[b, im_rows, :] = -(lev * im - DAMP * re)
    total = collect(0)
    block = applied.at[core * HALF + x, pl.ds(y * PIECE, PIECE)]
    applied[core * HALF + x, pl.ds(y * PIECE, PIECE), :] = total
    for device in plane:
        remote(block, block, gather_sems, device).start()
    slots = from_plane.at[0]
    remote(slots, slots, gather_sems, sibling).wait_recv()
    mine = applied.at[pl.ds(core * HALF, HALF)]
    share = remote(mine, mine, share_sem, sibling)
    share.start()
    next_half(core)
    doubles_0, singles_0 = expand(core)
    share.wait_recv()
    next_half(1 - core)
    doubles_1, singles_1 = expand(1 - core)
    finish(doubles_0 + doubles_1, singles_0 + singles_1)
    fold(1)
    line = jnp.zeros((1, LANES), F32)
    for g in range(GROUPS):
        squares = jnp.zeros((SUB, LANES), F32)
        for b in range(BLOCKS):
            res_re, res_im = res[b, pl.ds(g * PIECE, SUB), :], res[b, pl.ds(g * PIECE + SUB, SUB), :]
            squares = squares + (res_re * res_re + res_im * res_im)
        line = line + line_of(squares, g)
    rms_ref[0:1, :] = rms_of(line)
    mine = core * HALF + x
    rows, re_rows = pl.ds(y * SUB, SUB), pl.ds(y * PIECE, SUB)
    im_rows = pl.ds(y * PIECE + SUB, SUB)
    re, im, lev = resp[1, mine, re_rows, :], resp[1, mine, im_rows, :], level[mine, rows, :]
    base_re = rhs[mine, rows, :] - (lev * re + DAMP * im)
    base_im = -(lev * im - DAMP * re)
    total = collect(1)
    res_re, res_im = base_re - total[:SUB], base_im - total[SUB:]
    line = line_of(res_re * res_re + res_im * res_im, y)
    lines[mine * GROUPS + y] = line
    line_out[...] = line
    for device in everyone:
        remote(line_out, lines.at[mine * GROUPS + y], line_sems, device).start()
    p_re, p_im = pre_re[mine, rows, :], pre_im[mine, rows, :]
    final[core, 0, rows, :] = re + (res_re * p_re - res_im * p_im)
    final[core, 1, rows, :] = im + (res_im * p_re + res_re * p_im)
    block = final.at[core, :, rows]
    near = [place(x, lax.rem(y + d, NY), z, c) for d in ALONG[:-1] for c in (1 - core, core)]

    def show():
        for device in near + [sibling]:
            remote(block, block, final_sems, device).start()

    def await_pieces(count):
        pieces_in = columns.at[1, pl.ds(0, count)]
        remote(pieces_in, pieces_in, final_sems, sibling).wait_recv()

    pl.when(core == z_hi)(show)
    pl.when(core == z_hi)(lambda: await_pieces(NY - 1))
    pl.when(core != z_hi)(lambda: await_pieces(NY))
    out_ref[...] = final[z_hi]
    most = lines.at[pl.ds(0, BLOCKS * GROUPS - 1)]
    remote(most, most, line_sems, sibling).wait_recv()
    rms_ref[1:2, :] = rms_of(jnp.sum(lines[...], axis=0))
    wait_send(most, line_sems)
    pl.when(core == z_hi)(lambda: wait_send(columns.at[1, pl.ds(0, NZ - 1)], final_sems))

    wait_dipoles()
    share.wait_send()
    wait_send(from_plane.at[0], gather_sems)
    for sweep in range(2):
        wait_swaps(sweep)
        wait_send(from_plane.at[sweep], plane_sems.at[sweep])
        wait_send(columns.at[sweep, pl.ds(0, NZ - 1)], column_sems.at[sweep])


def tail(response_in, rms_in, response_out, rms_out):
    response_out[...] = response_in[...]
    rms_out[...] = rms_in[...]


def per_device(
    amplitudes, integral_slab, coupling, pair_of_block, pair_shift, virt_energy,
    core_energy, core_index, frequency, dipole,
):
    rows, virt_total = amplitudes.shape
    k_total = GROUPS * SUB
    whole, wide_whole = (BLOCKS, k_total, LANES), (BLOCKS, COLS, LANES)
    vmem = pl.BlockSpec(memory_space=pltpu.VMEM)
    anywhere = pl.BlockSpec(memory_space=pl.ANY)
    dma = pltpu.SemaphoreType.DMA
    shapes = (
        jax.ShapeDtypeStruct((2, k_total, LANES), F32),
        jax.ShapeDtypeStruct((2, k_total), F32),
    )
    response, rms = pl.pallas_call(
        kernel,
        name="response",
        out_shape=tuple(pltpu.VMEM(shape.shape, shape.dtype) for shape in shapes),
        in_specs=[anywhere] * 10,
        out_specs=(vmem, vmem),
        scratch_shapes=[
            pltpu.SMEM(pair_of_block.shape, jnp.int32),
            pltpu.SMEM(pair_shift.shape, F32),
            pltpu.SMEM(core_energy.shape, F32),
            pltpu.SMEM(core_index.shape, jnp.int32),
            pltpu.SMEM(frequency.shape, F32),
            pltpu.VMEM((BLOCKS, LANES), F32),
            pltpu.VMEM(dipole.shape, F32),
            pltpu.VMEM((rows, virt_total), BF16),
            pltpu.VMEM((virt_total, virt_total), F32),
            pltpu.VMEM((virt_total, rows), BF16),
            pltpu.VMEM((rows + 2 * virt_total, virt_total), BF16),
            pltpu.VMEM((2 * virt_total, virt_total), BF16),
            pltpu.VMEM((2, LANES), F32),
            pltpu.VMEM((BLOCKS, 2, LANES), F32),
            pltpu.VMEM(whole, F32),
            pltpu.VMEM(whole, F32),
            pltpu.VMEM(whole, F32),
            pltpu.VMEM(whole, F32),
            pltpu.VMEM(whole, F32),
            pltpu.VMEM(whole, F32),
            pltpu.VMEM((2,) + wide_whole, F32),
            pltpu.VMEM(wide_whole, F32),
            pltpu.VMEM(wide_whole, F32),
            pltpu.VMEM((2, 2 * COLS, HALF_COLS), BF16),
            pltpu.VMEM((2 * COLS, rows + virt_total), BF16),
            pltpu.VMEM((2, 2, 2, COLS, LANES), F32),
            pltpu.VMEM((2, 2, 2, COLS, LANES), F32),
            pltpu.VMEM((2, HALF, COLS, LANES), F32),
            pltpu.VMEM((2, len(PLANE), PIECE, LANES), F32),
            pltpu.VMEM((2, NZ, PIECE, LANES), F32),
            pltpu.VMEM(wide_whole, F32),
            pltpu.VMEM((2, 2, k_total, LANES), F32),
            pltpu.VMEM((BLOCKS * GROUPS, 1, LANES), F32),
            pltpu.VMEM((1, LANES), F32),
            dma((7,)),
            dma((3,)),
            dma((2, 2)),
            dma((2, 2, 2)),
            dma((2, 2)),
            dma((2, 2)),
            dma((2,)),
            dma((2,)),
            dma((2,)),
            dma((2,)),
        ],
        compiler_params=pltpu.CompilerParams(
            collective_id=0, has_side_effects=True, vmem_limit_bytes=56 * 2**20
        ),
    )(
        pair_of_block, pair_shift, core_energy, core_index, frequency,
        virt_energy.reshape(BLOCKS, LANES), dipole, amplitudes, integral_slab, coupling,
    )
    return pl.pallas_call(
        tail, name="tail", out_shape=shapes, in_specs=[vmem, vmem], out_specs=(vmem, vmem)
    )(*(pltpu.with_memory_space_constraint(value, pltpu.VMEM) for value in (response, rms)))


def solution(mesh):
    rows = P(("wide", "narrow"), None)
    placed = (rows, rows, P(("wide", "narrow"), None, None)) + (P(),) * 6 + (P(None, "narrow"),)
    return jax.shard_map(
        per_device,
        mesh=mesh,
        in_specs=placed,
        out_specs=(P(None, None, "narrow"), P()),
        check_vma=False,
    )
```
